32 devices in a mesh: slab: 8 (over z, y), load: 4 (over x, core).
Axes of the slice: x: 2, y: 2, z: 4, core: 2. Of those that a mesh axis runs over, the one named last changes fastest.
Arguments:
- start_disp: float32 [8, 3, 8, 64, 128], P('load', None, 'slab'), may hold values from -10 to 10
- density: float32 [8, 64, 128], P('slab'), may hold values from 0.05 to 1
- design: int32 [8, 64, 128], P('slab'), may hold values from 0 to 1, as said below
- support: int32 [8, 64, 128], P('slab'), may hold values 0 or 1
- load_nodes: int32 [8, 2048], P('load'), may hold values from 0 to 65535
- load_forces: float32 [8, 3, 2048], P('load'), may hold values from -6 to 6
Outputs:
- displacement: float32 [8, 3, 8, 64, 128], P('load', None, 'slab')
- new_density: float32 [8, 64, 128], P('slab')
The draws below stay inside these ranges and needn't reach their ends.
Inputs may be any that keep to these rules, and one draw needn't show every extreme that they name: 1 marks an element of the design domain, 0 a void element; at least one element is in the design domain. `support`: 1 marks a node held fixed. `load_nodes`: flat node index z * 64 * 128 + x * 128 + y; a node may carry several forces of one load case.
All inputs are finite; a program needn't handle non-finite values. No bound on the sum of `support` on one device may be relied on, other than what follows from the above.
Results may differ from the reference program's by a relative error of at most 0.00024.
Values sent between devices are 32-bit elements; how exact they have to be, the bound alone decides.
No kernel may reach another device: no remote copies, remote signals or barrier semaphores. Data moves between devices by JAX's collectives and lax.ppermute only.
A program may use at most 64 MiB of HBM per device.

```python
import jax
import jax.numpy as jnp
import numpy as np
from jax import lax

NX = 64
NY = 128
LOADS = 8
POINTS = 2048
SWEEPS = 4
NZ = 8
RADIUS = 2


def draw_start_disp(key, part):
    full_shape = (LOADS, 3, NZ, NX, NY)
    depth_frac = lax.broadcasted_iota(jnp.float32, full_shape, 2) / max(NZ - 1, 1)
    values = jax.random.normal(key, full_shape, jnp.float32) * jnp.sqrt(1.0 + 2.0 * depth_frac)
    return jnp.clip(values, -10.0, 10.0)


def draw_design(key, part):
    full_shape = (NZ, NX, NY)
    layer_index = lax.broadcasted_iota(jnp.int32, full_shape, 0)
    threshold = 300 + 600 * layer_index // max(NZ - 1, 1)
    return (jax.random.randint(key, full_shape, 0, 1000) < threshold).astype(jnp.int32)


def with_ends(values, rng, smallest, largest):
    place = [jax.random.randint(jax.random.fold_in(rng, axis), (), 0, length) for axis, length in enumerate(values.shape)]
    widest = values.shape.index(max(values.shape))
    neighbour = place[:widest] + [(place[widest] + 1) % values.shape[widest]] + place[widest + 1:]
    return values.at[tuple(place)].set(smallest).at[tuple(neighbour)].set(largest)


def level_of(rng, dims, split, least, high):
    def one(axis_at, blocks):
        steps = jax.random.uniform(jax.random.fold_in(jax.random.fold_in(rng, 6), axis_at), (blocks,), jnp.float32, least / len(split), high / len(split))
        return jnp.repeat(jnp.exp(steps), dims[axis_at] // blocks).reshape((-1,) + (1,) * (len(dims) - axis_at - 1))

    loudness = one(*split[0])
    for cut in split[1:]:
        loudness = loudness * one(*cut)
    return loudness


def bell_draw(stream_key, shape, width, limit, shards=(), held_as=jnp.bfloat16):
    factor_of = level_of(stream_key, shape, shards, -0.22, 0.18) if shards else 1.0
    values = jax.random.normal(stream_key, shape, jnp.float32) * width * factor_of
    return jnp.minimum(jnp.maximum(values, -limit), limit).astype(held_as)


def setup_inputs(seed: int = 0) -> dict:
    splits = jax.random.split(jax.random.key(seed), 7)
    return {
        "start_disp": draw_start_disp(jax.random.fold_in(splits[6], 71), 0),
        "density": jnp.clip(0.05 + 0.95 * jax.random.uniform(splits[1], (NZ, NX, NY), jnp.float32) ** level_of(splits[1], (NZ, NX, NY), ((0, 8),), -0.2, 0.2), 0.05, 1.0),
        "design": draw_design(jax.random.fold_in(splits[6], 71), 0),
        "support": with_ends((jax.random.randint(splits[3], (NZ, NX, NY), 0, 16) < 1).astype(jnp.int32), jax.random.fold_in(splits[3], 1), 0, 1),
        "load_nodes": with_ends(jax.random.randint(splits[4], (LOADS, POINTS), 0, NZ * NX * NY), jax.random.fold_in(splits[4], 1), 0, (NZ * NX * NY) - 1).astype(jnp.int32),
        "load_forces": bell_draw(splits[5], (LOADS, 3, POINTS), 1.0, 6.0, ((0, 4),), jnp.float32),
    }


POISSON = 0.3
STIFF_VOID = 0.001
UPPER_FACTOR = 1.2
LOWER_RATIO = 0.1
MOVE_LIMIT = 0.2
VOLUME_TARGET = 0.5
EPSILON = 1e-06
HIGHEST = lax.Precision.HIGHEST

def hex_stiffness():
    lame_first = POISSON / ((1 + POISSON) * (1 - 2 * POISSON))
    lame_shear = 1 / (2 * (1 + POISSON))
    elastic = np.zeros((6, 6))
    elastic[:3, :3] = lame_first
    for axis_a in range(3):
        elastic[axis_a, axis_a] += 2 * lame_shear
        elastic[3 + axis_a, 3 + axis_a] = lame_shear
    shear_pairs = ((0, 1), (1, 2), (0, 2))
    gauss_point = 1 / np.sqrt(3)
    matrix = np.zeros((24, 24))
    for quad_index in range(8):
        quad_coords = [gauss_point * (2 * (quad_index >> 2 - axis_a & 1) - 1) for axis_a in range(3)]
        shape_grads = np.zeros((8, 3))
        for corner in range(8):
            corner_signs = [2 * (corner >> 2 - axis_a & 1) - 1 for axis_a in range(3)]
            for axis_a in range(3):
                deriv_value = float(corner_signs[axis_a])
                for axis_b in range(3):
                    if axis_b != axis_a:
                        deriv_value *= (1 + corner_signs[axis_b] * quad_coords[axis_b]) / 2
                shape_grads[corner, axis_a] = deriv_value
        strain = np.zeros((6, 24))
        for corner in range(8):
            for axis_a in range(3):
                strain[axis_a, 3 * corner + axis_a] = shape_grads[corner, axis_a]
            for pair_index, shear_pair in enumerate(shear_pairs):
                strain[3 + pair_index, 3 * corner + shear_pair[0]] = shape_grads[corner, shear_pair[1]]
                strain[3 + pair_index, 3 * corner + shear_pair[1]] = shape_grads[corner, shear_pair[0]]
        matrix += strain.T @ elastic @ strain / 8
    return matrix.astype(np.float32)

def ahead(field, axis):
    length = field.shape[axis]
    zero_shape = list(field.shape)
    zero_shape[axis] = 1
    inner_part = lax.slice_in_dim(field, 1, length, axis=axis)
    return jnp.concatenate([inner_part, jnp.zeros(zero_shape, field.dtype)], axis)

def behind(field, axis):
    length = field.shape[axis]
    zero_shape = list(field.shape)
    zero_shape[axis] = 1
    inner_part = lax.slice_in_dim(field, 0, length - 1, axis=axis)
    return jnp.concatenate([jnp.zeros(zero_shape, field.dtype), inner_part], axis)

def corner_block(bottom, top):
    corner_parts = []
    for corner in range(8):
        corner_part = top if corner >> 2 & 1 else bottom
        if corner >> 1 & 1:
            corner_part = ahead(corner_part, corner_part.ndim - 2)
        if corner & 1:
            corner_part = ahead(corner_part, corner_part.ndim - 1)
        corner_parts.append(corner_part)
    stacked = jnp.stack(corner_parts, -4)
    return stacked.reshape(stacked.shape[:-4] + (24, stacked.shape[-2] * stacked.shape[-1]))

def spread_block(forces, rows_x, cols_y):
    shaped = forces.reshape(forces.shape[:-2] + (8, 3, rows_x, cols_y))
    to_bottom = jnp.zeros(shaped.shape[:-4] + (3, rows_x, cols_y), jnp.float32)
    to_top = to_bottom
    for corner in range(8):
        corner_part = shaped[..., corner, :, :, :]
        if corner >> 1 & 1:
            corner_part = behind(corner_part, corner_part.ndim - 2)
        if corner & 1:
            corner_part = behind(corner_part, corner_part.ndim - 1)
        if corner >> 2 & 1:
            to_top = to_top + corner_part
        else:
            to_bottom = to_bottom + corner_part
    return (to_bottom, to_top)

def gauss_table(count):
    offsets = (lax.broadcasted_iota(jnp.int32, (count, count), 0) - lax.broadcasted_iota(jnp.int32, (count, count), 1)).astype(jnp.float32)
    return jnp.exp(-(offsets / RADIUS) ** 2)

def smooth_plane(field, table_x, table_y):
    mixed = jnp.einsum('zab,ia->zib', field, table_x, precision=HIGHEST)
    return jnp.einsum('zib,jb->zij', mixed, table_y, precision=HIGHEST)

def reference(start_disp, density, design, support, load_nodes, load_forces):
    stiff_table = hex_stiffness()
    kmatrix = jnp.asarray(stiff_table)
    diag_entry = float(stiff_table[0, 0])
    design_mask = design.astype(jnp.float32)
    fixed_mask = support.astype(jnp.float32)
    free_mask = 1.0 - fixed_mask
    solid_part = design_mask * density
    stiffness = STIFF_VOID + (1.0 - STIFF_VOID) * solid_part ** 3
    beside_all = stiffness + behind(stiffness, 0)
    beside_all = beside_all + behind(beside_all, 1)
    beside_all = beside_all + behind(beside_all, 2)
    diagonal = (free_mask * diag_entry * beside_all + fixed_mask)[:, None]
    free_nodes = free_mask[:, None]
    fixed_nodes = fixed_mask[:, None]
    stiff_flat = stiffness.reshape(NZ, 1, NX * NY)

    def apply_stiffness(nodes):
        corner_vals = corner_block(nodes, ahead(nodes, 0))
        forces = jnp.einsum('ab,zbn->zan', kmatrix, corner_vals, precision=HIGHEST) * stiff_flat
        to_bottom, to_top = spread_block(forces, NX, NY)
        return to_bottom + behind(to_top, 0)

    def operate(nodes):
        return free_nodes * apply_stiffness(free_nodes * nodes) + fixed_nodes * nodes

    def solve_one(running, inputs):
        initial, indices, values = inputs
        initial = jnp.transpose(initial, (1, 0, 2, 3))
        right_side = jnp.zeros((3, NZ * NX * NY), jnp.float32).at[:, indices].add(values)
        right_side = jnp.transpose(right_side.reshape(3, NZ, NX, NY), (1, 0, 2, 3)) * free_nodes
        residual = right_side - operate(initial)
        precond = residual / diagonal
        applied = operate(precond)
        upper_bound = UPPER_FACTOR * jnp.sum(precond * applied) / jnp.sum(precond * residual)
        lower_bound = LOWER_RATIO * upper_bound
        center = 0.5 * (upper_bound + lower_bound)
        half_width = 0.5 * (upper_bound - lower_bound)
        spread_ratio = center / half_width
        factor = 1.0 / spread_ratio
        update = precond / center
        solution = initial
        for sweep_index in range(SWEEPS):
            solution = solution + update
            if sweep_index < SWEEPS - 1:
                if sweep_index == 0:
                    product = applied / center
                else:
                    product = operate(update)
                residual = residual - product
                factor_next = 1.0 / (2.0 * spread_ratio - factor)
                update = factor_next * factor * update + 2.0 * factor_next / half_width * (residual / diagonal)
                factor = factor_next
        free_part = free_nodes * solution
        corner_vals = corner_block(free_part, ahead(free_part, 0))
        forces = jnp.einsum('ab,zbn->zan', kmatrix, corner_vals, precision=HIGHEST)
        energy = lax.optimization_barrier(jnp.sum(corner_vals * forces, axis=1)).reshape(NZ, NX, NY)
        return (running + energy, jnp.transpose(solution, (1, 0, 2, 3)))
    energy_sum, displacement = lax.scan(solve_one, jnp.zeros((NZ, NX, NY), jnp.float32), (start_disp, load_nodes, load_forces))
    numer = density * (3.0 * (1.0 - STIFF_VOID)) * solid_part ** 2 * energy_sum
    table_x = gauss_table(NX)
    table_y = gauss_table(NY)
    table_z = gauss_table(NZ)

    def smooth(field):
        plane = smooth_plane(field, table_x, table_y)
        return jnp.einsum('kz,zij->kij', table_z, plane, precision=HIGHEST)
    filtered = smooth(numer) / smooth(density)
    weighted = design_mask * filtered
    count = jnp.sum(design_mask)
    ratio = weighted / (jnp.sum(weighted) / count + EPSILON)
    trial = jnp.clip(density * jnp.sqrt(ratio), density - MOVE_LIMIT, density + MOVE_LIMIT)
    scale = VOLUME_TARGET / (jnp.sum(design_mask * trial) / count + EPSILON)
    new_density = design_mask * jnp.minimum(scale * trial, 1.0)
    return (displacement, new_density)
```

```python
import functools

import jax
import jax.numpy as jnp
import numpy as np
from jax import lax
from jax.experimental import pallas as pl
from jax.experimental.pallas import tpu as pltpu
from jax.sharding import PartitionSpec as P

RADIUS = 2
POISSON = 0.3
STIFF_VOID = 0.001
UPPER_FACTOR = 1.2
LOWER_RATIO = 0.1
MOVE_LIMIT = 0.2
VOLUME_TARGET = 0.5
EPSILON = 1e-06
HIGHEST = lax.Precision.HIGHEST
F32 = jnp.float32

HALO_LOW = 4
HALO_HIGH = 5
HALO = HALO_LOW + HALO_HIGH
VMEM_LIMIT = 24 * 1024 * 1024
UNROLL = 4


def hex_stiffness():
    lame_first = POISSON / ((1 + POISSON) * (1 - 2 * POISSON))
    lame_shear = 1 / (2 * (1 + POISSON))
    elastic = np.zeros((6, 6))
    elastic[:3, :3] = lame_first
    for axis_a in range(3):
        elastic[axis_a, axis_a] += 2 * lame_shear
        elastic[3 + axis_a, 3 + axis_a] = lame_shear
    shear_pairs = ((0, 1), (1, 2), (0, 2))
    gauss_point = 1 / np.sqrt(3)
    matrix = np.zeros((24, 24))
    for quad_index in range(8):
        quad_coords = [
            gauss_point * (2 * (quad_index >> 2 - axis_a & 1) - 1) for axis_a in range(3)
        ]
        shape_grads = np.zeros((8, 3))
        for corner in range(8):
            corner_signs = [2 * (corner >> 2 - axis_a & 1) - 1 for axis_a in range(3)]
            for axis_a in range(3):
                deriv_value = float(corner_signs[axis_a])
                for axis_b in range(3):
                    if axis_b != axis_a:
                        deriv_value *= (1 + corner_signs[axis_b] * quad_coords[axis_b]) / 2
                shape_grads[corner, axis_a] = deriv_value
        strain = np.zeros((6, 24))
        for corner in range(8):
            for axis_a in range(3):
                strain[axis_a, 3 * corner + axis_a] = shape_grads[corner, axis_a]
            for pair_index, shear_pair in enumerate(shear_pairs):
                strain[3 + pair_index, 3 * corner + shear_pair[0]] = shape_grads[
                    corner, shear_pair[1]
                ]
                strain[3 + pair_index, 3 * corner + shear_pair[1]] = shape_grads[
                    corner, shear_pair[0]
                ]
        matrix += strain.T @ elastic @ strain / 8
    return matrix.astype(np.float32)


def mode_stiffness():
    signs = np.zeros((8, 8))
    for mode in range(8):
        for corner in range(8):
            flips = bin(mode & ~corner & 7).count("1")
            signs[mode, corner] = -1.0 if flips & 1 else 1.0
    spread = np.kron(signs, np.eye(3))
    return spread @ hex_stiffness().astype(np.float64) @ spread.T / 64


MODES = mode_stiffness()
DIAG_ENTRY = float(hex_stiffness()[0, 0])


def entry(mode_a, comp_a, mode_b, comp_b):
    return float(MODES[3 * mode_a + comp_a, 3 * mode_b + comp_b])


NORMAL = ((4, 0), (2, 1), (1, 2))
SHEAR = (((2, 0), (4, 1)), ((1, 0), (4, 2)), ((1, 1), (2, 2)))
TWIST = ((3, 0), (5, 1), (6, 2))
BEND = (((3, 1), (5, 0)), ((3, 2), (6, 0)), ((5, 2), (6, 1)))
WARP = ((7, 0), (7, 1), (7, 2))
NORMAL_ON = entry(4, 0, 4, 0)
NORMAL_OFF = entry(4, 0, 2, 1)
SHEAR_ON = entry(2, 0, 4, 1)
TWIST_ON = entry(3, 0, 3, 0)
TWIST_OFF = entry(3, 0, 5, 1)
BEND_ON = entry(3, 1, 3, 1)
BEND_OFF = entry(3, 1, 5, 0)
WARP_ON = entry(7, 0, 7, 0)


def smoother_factors():
    sigma = (1 + LOWER_RATIO) / (1 - LOWER_RATIO)
    factor = 1 / sigma
    residual = np.array([1.0, 0.0, 0.0, 0.0])
    update = np.array([1.0, 0.0, 0.0, 0.0])
    total = np.zeros(4)
    for sweep in range(4):
        total = total + update
        if sweep < 3:
            residual = residual - np.concatenate([[0.0], update[:3]])
            factor_next = 1 / (2 * sigma - factor)
            update = factor_next * factor * update + 2 * factor_next * sigma * residual
            factor = factor_next
    return [float(value) for value in total]


def iota(shape, axis):
    return lax.broadcasted_iota(jnp.int32, shape, axis)


def gauss(offsets):
    return jnp.exp(-((offsets.astype(F32) / RADIUS) ** 2))


def gauss_table(count):
    return gauss(iota((count, count), 0) - iota((count, count), 1))


def shifts(shape):
    inner = {}
    for axis in (0, 1):
        index = iota(shape, axis)
        inner[axis] = (index < shape[axis] - 1, index > 0)

    def above(value, axis):
        moved = pltpu.roll(value, shape[axis] - 1, axis)
        return jnp.where(inner[axis][0], moved, 0.0)

    def below(value, axis):
        moved = pltpu.roll(value, 1, axis)
        return jnp.where(inner[axis][1], moved, 0.0)

    return above, below


def row_modes(values, above):
    modes = {}
    for comp, value in enumerate(values):
        ahead = above(value, 0)
        for bit, part in ((0, value + ahead), (4, ahead - value)):
            beside = above(part, 1)
            modes[bit, comp] = part + beside
            modes[bit + 1, comp] = beside - part
    return modes


def element_modes(low, high):
    modes = {}
    for (bits, comp), value in low.items():
        other = high[bits, comp]
        if bits:
            modes[bits, comp] = value + other
        modes[bits + 2, comp] = other - value
    return modes


def element_forces(modes, scale):
    forces = {}
    total = modes[NORMAL[0]] + modes[NORMAL[1]] + modes[NORMAL[2]]
    shared = (scale * NORMAL_OFF) * total
    own = scale * (NORMAL_ON - NORMAL_OFF)
    for key in NORMAL:
        forces[key] = shared + own * modes[key]
    shear = scale * SHEAR_ON
    for key_a, key_b in SHEAR:
        forces[key_a] = forces[key_b] = shear * (modes[key_a] + modes[key_b])
    total = modes[TWIST[0]] + modes[TWIST[1]] + modes[TWIST[2]]
    shared = (scale * TWIST_OFF) * total
    own = scale * (TWIST_ON - TWIST_OFF)
    for key in TWIST:
        forces[key] = shared + own * modes[key]
    bend_on = scale * BEND_ON
    bend_off = scale * BEND_OFF
    for key_a, key_b in BEND:
        forces[key_a] = bend_on * modes[key_a] + bend_off * modes[key_b]
        forces[key_b] = bend_on * modes[key_b] + bend_off * modes[key_a]
    warp = scale * WARP_ON
    for key in WARP:
        forces[key] = warp * modes[key]
    return forces


def element_energy(modes):
    total = modes[NORMAL[0]] + modes[NORMAL[1]] + modes[NORMAL[2]]
    squares = sum(modes[key] * modes[key] for key in NORMAL)
    energy = NORMAL_OFF * (total * total) + (NORMAL_ON - NORMAL_OFF) * squares
    shear = 0.0
    for key_a, key_b in SHEAR:
        both = modes[key_a] + modes[key_b]
        shear = shear + both * both
    energy = energy + SHEAR_ON * shear
    total = modes[TWIST[0]] + modes[TWIST[1]] + modes[TWIST[2]]
    squares = sum(modes[key] * modes[key] for key in TWIST)
    energy = energy + TWIST_OFF * (total * total) + (TWIST_ON - TWIST_OFF) * squares
    squares = sum(modes[key] * modes[key] for pair in BEND for key in pair)
    crossed = sum(modes[key_a] * modes[key_b] for key_a, key_b in BEND)
    energy = energy + BEND_ON * squares + (2 * BEND_OFF) * crossed
    squares = sum(modes[key] * modes[key] for key in WARP)
    return energy + WARP_ON * squares


ROW_KEYS = [(bits, comp) for comp in range(3) for bits in (0, 1, 4, 5)]


def split_forces(forces):
    here, there = {}, {}
    for bits, comp in ROW_KEYS:
        change = forces[bits + 2, comp]
        if bits:
            common = forces[bits, comp]
            here[bits, comp] = common - change
            there[bits, comp] = common + change
        else:
            here[bits, comp] = -change
            there[bits, comp] = change
    return here, there


def node_forces(modes, below):
    values = []
    for comp in range(3):
        parts = []
        for bit in (0, 4):
            common, change = modes[bit, comp], modes[bit + 1, comp]
            parts.append((common - change) + below(common + change, 1))
        values.append((parts[0] - parts[1]) + below(parts[0] + parts[1], 0))
    return values


def apply_rows(first, last, load_row, scale_row, emit, above, below, carry=None):
    def advance(index, low, pending):
        high = row_modes(load_row(index + 1), above)
        forces = element_forces(element_modes(low, high), scale_row(index))
        here, there = split_forces(forces)
        return high, {key: pending[key] + here[key] for key in ROW_KEYS}, there

    def pack(low, pending):
        return tuple(low[key] for key in ROW_KEYS) + tuple(pending[key] for key in ROW_KEYS)

    def unpack(state):
        count = len(ROW_KEYS)
        return dict(zip(ROW_KEYS, state[:count])), dict(zip(ROW_KEYS, state[count:]))

    low = row_modes(load_row(first), above)
    zero = {key: jnp.zeros_like(low[key]) for key in ROW_KEYS}
    low, _, pending = advance(first, low, zero)

    def step(index, state):
        carried, (low, pending) = state[0], unpack(state[1])
        low, modes, pending = advance(index, low, pending)
        carried = emit(index, node_forces(modes, below), carried)
        return carried, pack(low, pending)

    carried, _ = lax.fori_loop(
        first + 1, last, step, (carry, pack(low, pending)), unroll=UNROLL
    )
    return carried


def own_table(count):
    return gauss_table(count)


def call(body, outs, *args, scratch=(), name=None, flops=0):
    return pl.pallas_call(
        body,
        out_shape=outs,
        in_specs=[pl.BlockSpec(memory_space=pltpu.VMEM)] * len(args),
        out_specs=jax.tree.map(lambda _: pl.BlockSpec(memory_space=pltpu.VMEM), outs),
        scratch_shapes=list(scratch),
        compiler_params=pltpu.CompilerParams(vmem_limit_bytes=VMEM_LIMIT),
        cost_estimate=pl.CostEstimate(flops=flops, bytes_accessed=1 << 20, transcendentals=0),
        name=name,
    )(*args)


def exchange(message, axes, pieces):
    rows = message.shape[0]
    return lax.all_to_all(
        message.reshape(rows, 1, message.shape[1]), axes, split_axis=0, concat_axis=0, tiled=True
    ).reshape(message.shape)


def shards(start_disp, density, design, support, load_nodes, load_forces):
    slabs = lax.axis_size("slab")
    parts = lax.axis_size("load")
    loads, comps, layers, rows_x, cols_y = start_disp.shape
    points = load_nodes.shape[1]
    depth = slabs * layers
    strip = rows_x // slabs
    span = strip + HALO
    fields = loads * comps
    plane = (depth, cols_y)
    in_rows = (fields + 2) * span + rows_x
    sum_rows = 1 + strip
    out_rows = 1 + fields * strip
    row_block = lambda count: jax.ShapeDtypeStruct((count, span) + plane, F32)
    flat = lambda rows: jax.ShapeDtypeStruct((rows, cols_y), F32)
    smoother = smoother_factors()

    def pack_body(disp_ref, dens_ref, design_ref, support_ref, out_ref, pad_ref):
        solid = design_ref[0].astype(F32) * dens_ref[0]
        planes = [
            (disp_ref[load, comp, 0], 0.0) for load in range(loads) for comp in range(comps)
        ]
        planes += [(solid * solid * solid, -1.0), (support_ref[0].astype(F32), 1.0)]
        for field, (value, fill) in enumerate(planes):
            pad_ref[field, 0:HALO_LOW] = jnp.full((HALO_LOW, cols_y), fill, F32)
            pad_ref[field, HALO_LOW : HALO_LOW + rows_x] = value
            pad_ref[field, HALO_LOW + rows_x : HALO + rows_x] = jnp.full(
                (HALO_HIGH, cols_y), fill, F32
            )
        for target in range(slabs):
            base = target * in_rows
            for field in range(fields + 2):
                out_ref[base + field * span : base + (field + 1) * span] = pad_ref[
                    field, target * strip : target * strip + span
                ]
            out_ref[base + (fields + 2) * span : base + in_rows] = dens_ref[0]

    message = call(
        pack_body,
        flat(slabs * in_rows),
        start_disp,
        density,
        design,
        support,
        scratch=[pltpu.VMEM((fields + 2, rows_x + 2 * 8, cols_y), F32)],
        name="pack",
    )
    received = exchange(message, "slab", slabs)

    cells = -(-span * depth // 16) * 16
    chunk = min(256, points)

    def loads_body(nodes_ref, forces_ref, out_ref):
        first = lax.axis_index("slab") * strip - HALO_LOW
        out_ref[...] = jnp.zeros_like(out_ref)
        for load in range(loads):
            for start in range(0, points, chunk):
                part = slice(start, start + chunk)
                node = nodes_ref[load : load + 1, part]
                column = node % cols_y
                row = (node // cols_y) % rows_x - first
                layer = node // (cols_y * rows_x)
                cell = jnp.where((row >= 0) & (row < span), row * depth + layer, -1)
                hit = iota((cells, chunk), 0) == cell
                spot = (iota((cols_y, chunk), 0) == column).astype(F32).astype(jnp.bfloat16)
                for comp in range(comps):
                    rest = forces_ref[load, comp : comp + 1, part]
                    for piece in range(3):
                        rounded = rest.astype(jnp.bfloat16).astype(F32)
                        rest = rest - rounded
                        picked = jnp.where(hit, rounded, 0.0).astype(jnp.bfloat16)
                        out_ref[load * comps + comp] += lax.dot_general(
                            picked, spot, (((1,), (1,)), ((), ())), preferred_element_type=F32
                        )

    right_side = call(
        loads_body,
        jax.ShapeDtypeStruct((fields, cells, cols_y), F32),
        load_nodes,
        load_forces,
        name="point_loads",
        flops=1 << 28,
    )

    def residual_body(
        in_ref, rhs_ref, design_ref, disp_ref, cube_ref, geo_ref, zero_ref, one_ref, dens_ref, sum_ref
    ):
        above, below = shifts(plane)
        for row in range(span):
            pick = lambda field: in_ref[pl.ds(field * span + row, depth, stride=in_rows), :]
            for field in range(fields):
                disp_ref[field, row] = pick(field)
            cube = pick(fields)
            cube_ref[0, row] = cube
            geo_ref[0, row] = jnp.where(
                cube < 0.0, 0.0, STIFF_VOID + (1.0 - STIFF_VOID) * cube
            )
            geo_ref[1, row] = 1.0 - pick(fields + 1)
        diags = {}
        for row in range(1, span - 1):
            beside = geo_ref[0, row] + geo_ref[0, row - 1]
            beside = beside + below(beside, 0)
            beside = beside + below(beside, 1)
            free = geo_ref[1, row]
            geo_ref[2, row] = 1.0 / (free * DIAG_ENTRY * beside + (1.0 - free))

        scale_row = lambda row: geo_ref[0, row]
        lane = iota((1, cols_y), 1)
        sums = jnp.zeros((1, cols_y), F32)
        whole = lambda value: jnp.sum(jnp.sum(value, 0, keepdims=True), 1, keepdims=True)

        for load in range(loads):
            keys = range(load * comps, (load + 1) * comps)

            def start_row(row):
                free = geo_ref[1, row]
                return [free * disp_ref[key, row] for key in keys]

            def emit_residual(row, forces, carried):
                free, inverse = geo_ref[1, row], geo_ref[2, row]
                total = jnp.zeros(plane, F32)
                for key, force in zip(keys, forces):
                    load_row = rhs_ref[key, pl.ds(pl.multiple_of(row * depth, depth), depth), :]
                    rest = free * (load_row - force) - (1.0 - free) * disp_ref[key, row]
                    value = rest * inverse
                    zero_ref[key, row] = value
                    total = total + value * rest
                own = (row >= HALO_LOW) & (row < HALO_LOW + strip)
                return carried + jnp.where(own, total, 0.0)

            weight = apply_rows(
                0, span - 1, start_row, scale_row, emit_residual, above, below,
                jnp.zeros(plane, F32),
            )

            def zero_row(row):
                free = geo_ref[1, row]
                return [free * zero_ref[key, row] for key in keys]

            def emit_one(row, forces, carried):
                free, inverse = geo_ref[1, row], geo_ref[2, row]
                total = jnp.zeros(plane, F32)
                for key, force in zip(keys, forces):
                    value = zero_ref[key, row]
                    applied = free * force + (1.0 - free) * value
                    one_ref[key, row] = applied * inverse
                    total = total + value * applied
                own = (row >= HALO_LOW) & (row < HALO_LOW + strip)
                return carried + jnp.where(own, total, 0.0)

            curve = apply_rows(
                1, span - 2, zero_row, scale_row, emit_one, above, below, jnp.zeros(plane, F32)
            )
            sums = jnp.where(lane == 2 * load, whole(curve), sums)
            sums = jnp.where(lane == 2 * load + 1, whole(weight), sums)

        here = lax.axis_index("slab")
        mixed = jnp.zeros((rows_x, cols_y), F32)
        for layer in range(depth):
            weight = gauss(jnp.full((1, cols_y), here - layer, jnp.int32))
            base = layer * in_rows + (fields + 2) * span
            mixed = mixed + weight * in_ref[base : base + rows_x]
        table_x = gauss_table(rows_x)
        mixed = jnp.dot(table_x, mixed, precision=HIGHEST, preferred_element_type=F32)
        filtered = jnp.dot(
            mixed, gauss_table(cols_y), precision=HIGHEST, preferred_element_type=F32
        )
        dens_ref[...] = filtered
        mask = design_ref[0].astype(F32)
        sums = jnp.where(lane == 2 * loads, whole(mask), sums)
        share = jnp.dot(
            table_x, mask / filtered, precision=HIGHEST, preferred_element_type=F32
        )
        for target in range(slabs):
            base = target * sum_rows
            sum_ref[base : base + 1] = sums
            sum_ref[base + 1 : base + sum_rows] = share[target * strip : (target + 1) * strip]

    disp, cube, geometry, zeroth, first, dens_filtered, sums = call(
        residual_body,
        (
            row_block(fields),
            row_block(1),
            row_block(3),
            row_block(fields),
            row_block(fields),
            flat(rows_x),
            flat(slabs * sum_rows),
        ),
        received,
        right_side,
        design,
        name="residual",
        flops=1 << 26,
    )
    all_sums = exchange(sums, "slab", slabs)

    def powers_body(geo_ref, one_ref, two_ref, three_ref):
        above, below = shifts(plane)
        scale_row = lambda row: geo_ref[0, row]
        for load in range(loads):
            keys = range(load * comps, (load + 1) * comps)
            for source, target, edge in ((one_ref, two_ref, 2), (two_ref, three_ref, 3)):

                def load_row(row):
                    free = geo_ref[1, row]
                    return [free * source[key, row] for key in keys]

                def emit(row, forces, carried):
                    free, inverse = geo_ref[1, row], geo_ref[2, row]
                    for key, force in zip(keys, forces):
                        target[key, row] = (
                            free * force + (1.0 - free) * source[key, row]
                        ) * inverse
                    return carried

                apply_rows(
                    edge, span - 1 - edge, load_row, scale_row, emit, above, below,
                    jnp.zeros((1, 1), F32),
                )

    second, third = call(
        powers_body,
        (row_block(fields), row_block(fields)),
        geometry,
        first,
        name="powers",
        flops=1 << 26,
    )

    def energy_body(
        sums_ref, disp_ref, cube_ref, geo_ref, zero_ref, one_ref, two_ref, three_ref,
        disp_out_ref, numer_ref, count_ref, weak_ref,
    ):
        above, below = shifts(plane)
        lane = iota((1, cols_y), 1)
        sums = jnp.zeros((1, cols_y), F32)
        for layer in range(slabs):
            sums = sums + sums_ref[layer * sum_rows : layer * sum_rows + 1]
        take = lambda index: jnp.sum(jnp.where(lane == index, sums, 0.0), 1, keepdims=True)
        count_ref[...] = jnp.broadcast_to(take(2 * loads), (8, cols_y))
        inverses = []
        for load in range(loads):
            upper = UPPER_FACTOR * take(2 * load) / take(2 * load + 1)
            inverses.append(
                jnp.broadcast_to(1.0 / (0.5 * (upper + LOWER_RATIO * upper)), plane)
            )
        lower = [None] * loads
        for row in range(HALO_LOW, HALO_LOW + strip + 1):
            free = geo_ref[1, row]
            energy = 0.0
            for load in range(loads):
                inverse = inverses[load]
                values = []
                for comp in range(comps):
                    key = load * comps + comp
                    value = smoother[3] * three_ref[key, row]
                    value = smoother[2] * two_ref[key, row] + inverse * value
                    value = smoother[1] * one_ref[key, row] + inverse * value
                    value = smoother[0] * zero_ref[key, row] + inverse * value
                    value = disp_ref[key, row] + inverse * value
                    if row < HALO_LOW + strip:
                        place = key * strip + row - HALO_LOW
                        disp_out_ref[pl.ds(place, depth, stride=out_rows), :] = value
                    values.append(free * value)
                modes = row_modes(values, above)
                if lower[load] is not None:
                    energy = energy + element_energy(element_modes(lower[load], modes))
                lower[load] = modes
            if row > HALO_LOW:
                weak_ref[(row - 1 - HALO_LOW) * depth : (row - HALO_LOW) * depth] = (
                    (3.0 * (1.0 - STIFF_VOID)) * cube_ref[0, row - 1] * energy
                )
        disp_out_ref[pl.ds(out_rows - 1, depth, stride=out_rows), :] = jnp.zeros(plane, F32)
        size = strip * depth
        across = jnp.dot(
            weak_ref[...], gauss_table(cols_y), precision=HIGHEST, preferred_element_type=F32
        )
        to, source = iota((size, size), 0), iota((size, size), 1)
        table = jnp.where(
            to % strip == source // depth, gauss(to // strip - source % depth), 0.0
        )
        smooth = jnp.dot(table, across, precision=HIGHEST, preferred_element_type=F32)
        weighted = jnp.zeros((1, cols_y), F32)
        for layer in range(depth):
            piece = smooth[layer * strip : (layer + 1) * strip]
            base = layer * sum_rows
            weighted = weighted + jnp.sum(
                piece * sums_ref[base + 1 : base + sum_rows], 0, keepdims=True
            )
        for layer in range(depth):
            piece = smooth[layer * strip : (layer + 1) * strip]
            for part in range(parts):
                base = (part * slabs + layer) * sum_rows
                numer_ref[base : base + strip] = piece
                numer_ref[base + strip : base + sum_rows] = weighted

    disp_message, numer_message, count = call(
        energy_body,
        (flat(slabs * out_rows), flat(parts * slabs * sum_rows), flat(8)),
        all_sums,
        disp,
        cube,
        geometry,
        zeroth,
        first,
        second,
        third,
        scratch=[pltpu.VMEM((strip * depth, cols_y), F32)],
        name="energy",
        flops=1 << 24,
    )
    numer_pieces = exchange(numer_message, ("load", "slab"), parts * slabs)

    def trial_body(
        numer_ref, dens_ref, filtered_ref, design_ref, count_ref, disp_ref, trial_ref, out_ref, plane_ref
    ):
        weighted_row = jnp.zeros((1, cols_y), F32)
        for source in range(slabs):
            total = jnp.zeros((strip, cols_y), F32)
            for part in range(parts):
                base = (part * slabs + source) * sum_rows
                total = total + numer_ref[base : base + strip]
                weighted_row = weighted_row + numer_ref[base + strip : base + sum_rows]
            plane_ref[source * strip : (source + 1) * strip] = total
        weighted_total = jnp.sum(weighted_row, 1, keepdims=True)
        mean = weighted_total / count_ref[0:1] + EPSILON
        numer = jnp.dot(
            gauss_table(rows_x), plane_ref[...], precision=HIGHEST, preferred_element_type=F32
        )
        mask = design_ref[0].astype(F32)
        dens = dens_ref[0]
        ratio = mask * (numer / filtered_ref[...]) / mean
        trial = jnp.clip(dens * jnp.sqrt(ratio), dens - MOVE_LIMIT, dens + MOVE_LIMIT)
        trial_ref[...] = trial
        out_ref[...] = disp_ref[...]
        volume = jnp.sum(mask * trial, 0, keepdims=True)
        for target in range(slabs):
            base = (target + 1) * out_rows - 1
            out_ref[base : base + 1] = volume

    trial, out_message = call(
        trial_body,
        (flat(rows_x), flat(slabs * out_rows)),
        numer_pieces,
        density,
        dens_filtered,
        design,
        count,
        disp_message,
        scratch=[pltpu.VMEM((rows_x, cols_y), F32)],
        name="trial",
    )
    out_pieces = exchange(out_message, "slab", slabs)

    def final_body(pieces_ref, trial_ref, design_ref, count_ref, disp_ref, dens_ref):
        volume = jnp.zeros((1, cols_y), F32)
        for source in range(slabs):
            base = (source + 1) * out_rows
            volume = volume + pieces_ref[base - 1 : base]
        volume = jnp.sum(volume, 1, keepdims=True)
        scale = VOLUME_TARGET / (volume / count_ref[0:1] + EPSILON)
        mask = design_ref[0].astype(F32)
        dens_ref[0] = mask * jnp.minimum(scale * trial_ref[...], 1.0)
        for source in range(slabs):
            rows = slice(source * strip, (source + 1) * strip)
            for key in range(fields):
                base = source * out_rows + key * strip
                disp_ref[key // comps, key % comps, 0, rows] = pieces_ref[base : base + strip]

    return call(
        final_body,
        (
            jax.ShapeDtypeStruct(start_disp.shape, F32),
            jax.ShapeDtypeStruct(density.shape, F32),
        ),
        out_pieces,
        trial,
        design,
        count,
        name="final",
    )


def solution(mesh):
    return jax.shard_map(
        shards,
        mesh=mesh,
        in_specs=(
            P("load", None, "slab", None, None),
            P("slab", None, None),
            P("slab", None, None),
            P("slab", None, None),
            P("load", None),
            P("load", None, None),
        ),
        out_specs=(P("load", None, "slab", None, None), P("slab", None, None)),
        check_vma=False,
    )
```

```python
import functools

import jax
import jax.numpy as jnp
import numpy as np
from jax import lax
from jax.experimental import pallas as pl
from jax.experimental.pallas import tpu as pltpu
from jax.sharding import PartitionSpec as P

RADIUS = 2
POISSON = 0.3
STIFF_VOID = 0.001
UPPER_FACTOR = 1.2
LOWER_RATIO = 0.1
MOVE_LIMIT = 0.2
VOLUME_TARGET = 0.5
EPSILON = 1e-06
HIGHEST = lax.Precision.HIGHEST
F32 = jnp.float32

HALO_LOW = 4
HALO_HIGH = 5
HALO = HALO_LOW + HALO_HIGH
VMEM_LIMIT = 24 * 1024 * 1024
UNROLL = 4


def hex_stiffness():
    lame_first = POISSON / ((1 + POISSON) * (1 - 2 * POISSON))
    lame_shear = 1 / (2 * (1 + POISSON))
    elastic = np.zeros((6, 6))
    elastic[:3, :3] = lame_first
    for axis_a in range(3):
        elastic[axis_a, axis_a] += 2 * lame_shear
        elastic[3 + axis_a, 3 + axis_a] = lame_shear
    shear_pairs = ((0, 1), (1, 2), (0, 2))
    gauss_point = 1 / np.sqrt(3)
    matrix = np.zeros((24, 24))
    for quad_index in range(8):
        quad_coords = [
            gauss_point * (2 * (quad_index >> 2 - axis_a & 1) - 1) for axis_a in range(3)
        ]
        shape_grads = np.zeros((8, 3))
        for corner in range(8):
            corner_signs = [2 * (corner >> 2 - axis_a & 1) - 1 for axis_a in range(3)]
            for axis_a in range(3):
                deriv_value = float(corner_signs[axis_a])
                for axis_b in range(3):
                    if axis_b != axis_a:
                        deriv_value *= (1 + corner_signs[axis_b] * quad_coords[axis_b]) / 2
                shape_grads[corner, axis_a] = deriv_value
        strain = np.zeros((6, 24))
        for corner in range(8):
            for axis_a in range(3):
                strain[axis_a, 3 * corner + axis_a] = shape_grads[corner, axis_a]
            for pair_index, shear_pair in enumerate(shear_pairs):
                strain[3 + pair_index, 3 * corner + shear_pair[0]] = shape_grads[
                    corner, shear_pair[1]
                ]
                strain[3 + pair_index, 3 * corner + shear_pair[1]] = shape_grads[
                    corner, shear_pair[0]
                ]
        matrix += strain.T @ elastic @ strain / 8
    return matrix.astype(np.float32)


def mode_stiffness():
    signs = np.zeros((8, 8))
    for mode in range(8):
        for corner in range(8):
            flips = bin(mode & ~corner & 7).count("1")
            signs[mode, corner] = -1.0 if flips & 1 else 1.0
    spread = np.kron(signs, np.eye(3))
    return spread @ hex_stiffness().astype(np.float64) @ spread.T / 64


MODES = mode_stiffness()
DIAG_ENTRY = float(hex_stiffness()[0, 0])


def entry(mode_a, comp_a, mode_b, comp_b):
    return float(MODES[3 * mode_a + comp_a, 3 * mode_b + comp_b])


NORMAL = ((4, 0), (2, 1), (1, 2))
SHEAR = (((2, 0), (4, 1)), ((1, 0), (4, 2)), ((1, 1), (2, 2)))
TWIST = ((3, 0), (5, 1), (6, 2))
BEND = (((3, 1), (5, 0)), ((3, 2), (6, 0)), ((5, 2), (6, 1)))
WARP = ((7, 0), (7, 1), (7, 2))
NORMAL_ON = entry(4, 0, 4, 0)
NORMAL_OFF = entry(4, 0, 2, 1)
SHEAR_ON = entry(2, 0, 4, 1)
TWIST_ON = entry(3, 0, 3, 0)
TWIST_OFF = entry(3, 0, 5, 1)
BEND_ON = entry(3, 1, 3, 1)
BEND_OFF = entry(3, 1, 5, 0)
WARP_ON = entry(7, 0, 7, 0)


def smoother_factors():
    sigma = (1 + LOWER_RATIO) / (1 - LOWER_RATIO)
    factor = 1 / sigma
    residual = np.array([1.0, 0.0, 0.0, 0.0])
    update = np.array([1.0, 0.0, 0.0, 0.0])
    total = np.zeros(4)
    for sweep in range(4):
        total = total + update
        if sweep < 3:
            residual = residual - np.concatenate([[0.0], update[:3]])
            factor_next = 1 / (2 * sigma - factor)
            update = factor_next * factor * update + 2 * factor_next * sigma * residual
            factor = factor_next
    return [float(value) for value in total]


def iota(shape, axis):
    return lax.broadcasted_iota(jnp.int32, shape, axis)


def gauss(offsets):
    return jnp.exp(-((offsets.astype(F32) / RADIUS) ** 2))


def gauss_table(count):
    return gauss(iota((count, count), 0) - iota((count, count), 1))


def shifts(shape, rows_x):
    inner = {}
    for axis, count in ((0, shape[0]), (1, rows_x)):
        index = iota(shape, axis) % count
        inner[axis] = (index < count - 1, index > 0)

    def above(value, axis):
        moved = pltpu.roll(value, shape[axis] - 1, axis)
        return jnp.where(inner[axis][0], moved, 0.0)

    def below(value, axis):
        moved = pltpu.roll(value, 1, axis)
        return jnp.where(inner[axis][1], moved, 0.0)

    return above, below


def row_modes(values, above):
    modes = {}
    for comp, value in enumerate(values):
        ahead = above(value, 0)
        for bit, part in ((0, value + ahead), (4, ahead - value)):
            beside = above(part, 1)
            modes[bit, comp] = part + beside
            modes[bit + 2, comp] = beside - part
    return modes


def element_modes(low, high):
    modes = {}
    for (bits, comp), value in low.items():
        other = high[bits, comp]
        if bits:
            modes[bits, comp] = value + other
        modes[bits + 1, comp] = other - value
    return modes


def element_forces(modes, scale):
    forces = {}
    total = modes[NORMAL[0]] + modes[NORMAL[1]] + modes[NORMAL[2]]
    shared = (scale * NORMAL_OFF) * total
    own = scale * (NORMAL_ON - NORMAL_OFF)
    for key in NORMAL:
        forces[key] = shared + own * modes[key]
    shear = scale * SHEAR_ON
    for key_a, key_b in SHEAR:
        forces[key_a] = forces[key_b] = shear * (modes[key_a] + modes[key_b])
    total = modes[TWIST[0]] + modes[TWIST[1]] + modes[TWIST[2]]
    shared = (scale * TWIST_OFF) * total
    own = scale * (TWIST_ON - TWIST_OFF)
    for key in TWIST:
        forces[key] = shared + own * modes[key]
    bend_on = scale * BEND_ON
    bend_off = scale * BEND_OFF
    for key_a, key_b in BEND:
        forces[key_a] = bend_on * modes[key_a] + bend_off * modes[key_b]
        forces[key_b] = bend_on * modes[key_b] + bend_off * modes[key_a]
    warp = scale * WARP_ON
    for key in WARP:
        forces[key] = warp * modes[key]
    return forces


def element_energy(modes):
    total = modes[NORMAL[0]] + modes[NORMAL[1]] + modes[NORMAL[2]]
    squares = sum(modes[key] * modes[key] for key in NORMAL)
    energy = NORMAL_OFF * (total * total) + (NORMAL_ON - NORMAL_OFF) * squares
    shear = 0.0
    for key_a, key_b in SHEAR:
        both = modes[key_a] + modes[key_b]
        shear = shear + both * both
    energy = energy + SHEAR_ON * shear
    total = modes[TWIST[0]] + modes[TWIST[1]] + modes[TWIST[2]]
    squares = sum(modes[key] * modes[key] for key in TWIST)
    energy = energy + TWIST_OFF * (total * total) + (TWIST_ON - TWIST_OFF) * squares
    squares = sum(modes[key] * modes[key] for pair in BEND for key in pair)
    crossed = sum(modes[key_a] * modes[key_b] for key_a, key_b in BEND)
    energy = energy + BEND_ON * squares + (2 * BEND_OFF) * crossed
    squares = sum(modes[key] * modes[key] for key in WARP)
    return energy + WARP_ON * squares


ROW_KEYS = [(bits, comp) for comp in range(3) for bits in (0, 2, 4, 6)]


def split_forces(forces):
    here, there = {}, {}
    for bits, comp in ROW_KEYS:
        change = forces[bits + 1, comp]
        if bits:
            common = forces[bits, comp]
            here[bits, comp] = common - change
            there[bits, comp] = common + change
        else:
            here[bits, comp] = -change
            there[bits, comp] = change
    return here, there


def node_forces(modes, below):
    values = []
    for comp in range(3):
        parts = []
        for bit in (0, 4):
            common, change = modes[bit, comp], modes[bit + 2, comp]
            parts.append((common - change) + below(common + change, 1))
        values.append((parts[0] - parts[1]) + below(parts[0] + parts[1], 0))
    return values


def apply_rows(first, last, load_row, scale_row, emit, above, below, carry=None):
    def advance(index, low, pending):
        high = row_modes(load_row(index + 1), above)
        forces = element_forces(element_modes(low, high), scale_row(index))
        here, there = split_forces(forces)
        return high, {key: pending[key] + here[key] for key in ROW_KEYS}, there

    def pack(low, pending):
        return tuple(low[key] for key in ROW_KEYS) + tuple(pending[key] for key in ROW_KEYS)

    def unpack(state):
        count = len(ROW_KEYS)
        return dict(zip(ROW_KEYS, state[:count])), dict(zip(ROW_KEYS, state[count:]))

    low = row_modes(load_row(first), above)
    zero = {key: jnp.zeros_like(low[key]) for key in ROW_KEYS}
    low, _, pending = advance(first, low, zero)

    def step(index, state):
        carried, (low, pending) = state[0], unpack(state[1])
        low, modes, pending = advance(index, low, pending)
        carried = emit(index, node_forces(modes, below), carried)
        return carried, pack(low, pending)

    carried, _ = lax.fori_loop(
        first + 1, last, step, (carry, pack(low, pending)), unroll=UNROLL
    )
    return carried


def dot(left, right):
    return jnp.dot(left, right, precision=HIGHEST, preferred_element_type=F32)


def call(body, outs, *args, scratch=(), name=None, flops=0, space=pltpu.VMEM):
    return pl.pallas_call(
        body,
        out_shape=outs,
        in_specs=[pl.BlockSpec(memory_space=space)] * len(args),
        out_specs=jax.tree.map(lambda _: pl.BlockSpec(memory_space=pltpu.VMEM), outs),
        scratch_shapes=list(scratch),
        compiler_params=pltpu.CompilerParams(vmem_limit_bytes=VMEM_LIMIT),
        cost_estimate=pl.CostEstimate(flops=flops, bytes_accessed=1 << 20, transcendentals=0),
        name=name,
    )(*args)


def exchange(message, axes):
    rows = message.shape[0]
    return lax.all_to_all(
        message.reshape(rows, 1, message.shape[1]), axes, split_axis=0, concat_axis=0, tiled=True
    ).reshape(message.shape)


def shards(start_disp, density, design, support, load_nodes, load_forces):
    slabs = lax.axis_size("slab")
    parts = lax.axis_size("load")
    loads, comps, layers, rows_x, cols_y = start_disp.shape
    points = load_nodes.shape[1]
    depth = slabs * layers
    strip = cols_y // slabs
    span = strip + HALO
    width = loads * rows_x
    half = strip * rows_x // width
    plane = (depth, width)
    in_rows = (comps + 1) * span + rows_x
    sum_rows = 3 + half
    numer_rows = half + 1
    out_rows = comps * strip + 1
    block = lambda count: jax.ShapeDtypeStruct((count, span) + plane, F32)
    flat = lambda rows: jax.ShapeDtypeStruct((rows, width), F32)
    smoother = smoother_factors()

    def pack_body(
        disp_ref, dens_ref, design_ref, support_ref, out_ref,
        stage_ref, dens_in, design_in, support_in, pad_ref, sems,
    ):
        copies = [
            pltpu.make_async_copy(dens_ref.at[0], dens_in, sems.at[0]),
            pltpu.make_async_copy(design_ref.at[0], design_in, sems.at[1]),
            pltpu.make_async_copy(support_ref.at[0], support_in, sems.at[2]),
        ]
        for load in range(loads):
            copies.append(
                pltpu.make_async_copy(
                    disp_ref.at[load, :, 0],
                    stage_ref.at[:, load * rows_x : (load + 1) * rows_x],
                    sems.at[3 + load],
                )
            )
        for copy in copies:
            copy.start()
        cube_side = iota((1, width), 1) < rows_x
        for field in range(comps + 1):
            fill = jnp.zeros((1, width), F32) if field < comps else jnp.where(cube_side, -1.0, 1.0)
            pad_ref[field, 0:HALO_LOW] = jnp.broadcast_to(fill, (HALO_LOW, width))
            pad_ref[field, HALO_LOW + cols_y : HALO + cols_y] = jnp.broadcast_to(
                fill, (HALO_HIGH, width)
            )
        for copy in copies[:3]:
            copy.wait()
        solid = design_in[...].astype(F32) * dens_in[...]
        both = jnp.concatenate([solid * solid * solid, support_in[...].astype(F32)], 0)
        pad_ref[comps, HALO_LOW : HALO_LOW + cols_y] = both.T
        for copy in copies[3:]:
            copy.wait()
        for comp in range(comps):
            pad_ref[comp, HALO_LOW : HALO_LOW + cols_y] = stage_ref[comp].T
        for target in range(slabs):
            base = target * in_rows
            for field in range(comps + 1):
                out_ref[base + field * span : base + (field + 1) * span] = pad_ref[
                    field, target * strip : target * strip + span
                ]
            out_ref[base + (comps + 1) * span : base + in_rows] = dens_in[...]

    message = call(
        pack_body,
        flat(slabs * in_rows),
        start_disp,
        density,
        design,
        support,
        scratch=[
            pltpu.VMEM((comps, width, cols_y), F32),
            pltpu.VMEM((rows_x, cols_y), F32),
            pltpu.VMEM((rows_x, cols_y), jnp.int32),
            pltpu.VMEM((rows_x, cols_y), jnp.int32),
            pltpu.VMEM((comps + 1, cols_y + 2 * 8, width), F32),
            pltpu.SemaphoreType.DMA((3 + loads,)),
        ],
        name="pack",
        space=pl.ANY,
    )
    received = exchange(message, "slab")

    cells = -(-span * depth // 16) * 16
    chunk = min(256, points)

    def loads_body(nodes_ref, forces_ref, out_ref):
        first = lax.axis_index("slab") * strip - HALO_LOW
        out_ref[...] = jnp.zeros_like(out_ref)
        for load in range(loads):
            for start in range(0, points, chunk):
                part = slice(start, start + chunk)
                node = nodes_ref[load : load + 1, part]
                row = node % cols_y - first
                lane = load * rows_x + (node // cols_y) % rows_x
                layer = node // (cols_y * rows_x)
                cell = jnp.where((row >= 0) & (row < span), row * depth + layer, -1)
                hit = iota((cells, chunk), 0) == cell
                spot = (iota((width, chunk), 0) == lane).astype(F32).astype(jnp.bfloat16)
                for comp in range(comps):
                    rest = forces_ref[load, comp : comp + 1, part]
                    for piece in range(3):
                        rounded = rest.astype(jnp.bfloat16).astype(F32)
                        rest = rest - rounded
                        picked = jnp.where(hit, rounded, 0.0).astype(jnp.bfloat16)
                        out_ref[comp] += lax.dot_general(
                            picked, spot, (((1,), (1,)), ((), ())), preferred_element_type=F32
                        )

    right_side = call(
        loads_body,
        jax.ShapeDtypeStruct((comps, cells, width), F32),
        load_nodes,
        load_forces,
        name="point_loads",
        flops=1 << 28,
    )

    def own_row(row):
        return (row >= HALO_LOW) & (row < HALO_LOW + strip)

    def packed_table(part):
        shape = (slabs * half, cols_y)
        row = iota(shape, 0)
        return gauss(row // half * strip + part * half + row % half - iota(shape, 1))

    def residual_body(
        in_ref, rhs_ref, design_ref, disp_ref, cube_ref, geo_ref, zero_ref, one_ref, dens_ref, sum_ref
    ):
        above, below = shifts(plane, rows_x)
        cube_side = iota(plane, 1) < rows_x
        for row in range(span):
            pick = lambda field: in_ref[pl.ds(field * span + row, depth, stride=in_rows), :]
            for comp in range(comps):
                disp_ref[comp, row] = pick(comp)
            both = pick(comps)
            other = pltpu.roll(both, rows_x, 1)
            cube = jnp.where(cube_side, both, other)
            cube_ref[0, row] = cube
            geo_ref[0, row] = jnp.where(
                cube < 0.0, 0.0, STIFF_VOID + (1.0 - STIFF_VOID) * cube
            )
            geo_ref[1, row] = 1.0 - jnp.where(cube_side, other, both)
        for row in range(1, span - 1):
            beside = geo_ref[0, row] + geo_ref[0, row - 1]
            beside = beside + below(beside, 0)
            beside = beside + below(beside, 1)
            free = geo_ref[1, row]
            geo_ref[2, row] = 1.0 / (free * DIAG_ENTRY * beside + (1.0 - free))

        scale_row = lambda row: geo_ref[0, row]

        def start_row(row):
            free = geo_ref[1, row]
            return [free * disp_ref[comp, row] for comp in range(comps)]

        def emit_residual(row, forces, carried):
            free, inverse = geo_ref[1, row], geo_ref[2, row]
            total = jnp.zeros(plane, F32)
            for comp, force in enumerate(forces):
                load_row = rhs_ref[comp, pl.ds(pl.multiple_of(row * depth, depth), depth), :]
                rest = free * (load_row - force) - (1.0 - free) * disp_ref[comp, row]
                value = rest * inverse
                zero_ref[comp, row] = value
                total = total + value * rest
            return carried + jnp.where(own_row(row), total, 0.0)

        weight = apply_rows(
            0, span - 1, start_row, scale_row, emit_residual, above, below,
            jnp.zeros(plane, F32),
        )

        def zero_row(row):
            free = geo_ref[1, row]
            return [free * zero_ref[comp, row] for comp in range(comps)]

        def emit_one(row, forces, carried):
            free, inverse = geo_ref[1, row], geo_ref[2, row]
            total = jnp.zeros(plane, F32)
            for comp, force in enumerate(forces):
                value = zero_ref[comp, row]
                applied = free * force + (1.0 - free) * value
                one_ref[comp, row] = applied * inverse
                total = total + value * applied
            return carried + jnp.where(own_row(row), total, 0.0)

        curve = apply_rows(
            1, span - 2, zero_row, scale_row, emit_one, above, below, jnp.zeros(plane, F32)
        )

        here = lax.axis_index("slab")
        mixed = jnp.zeros((rows_x, cols_y), F32)
        for layer in range(depth):
            weight_z = gauss(jnp.full((1, cols_y), here - layer, jnp.int32))
            base = layer * in_rows + (comps + 1) * span
            mixed = mixed + weight_z * in_ref[base : base + rows_x]
        mixed = dot(gauss_table(rows_x), mixed)
        filtered = dot(mixed, gauss_table(cols_y))
        dens_ref[...] = filtered
        mask = design_ref[0].astype(F32)
        share = (mask / filtered).T
        share = jnp.concatenate(
            [dot(packed_table(part), share) for part in range(strip // half)], 1
        )
        down = lambda value: jnp.sum(value, 0, keepdims=True)
        sums = [down(curve), down(weight), down(mask)]
        for target in range(slabs):
            base = target * sum_rows
            for index, value in enumerate(sums):
                sum_ref[base + index : base + index + 1] = value
            sum_ref[base + 3 : base + sum_rows] = share[target * half : (target + 1) * half]

    disp, cube, geometry, zeroth, first, dens_filtered, sums = call(
        residual_body,
        (
            block(comps),
            block(1),
            block(3),
            block(comps),
            block(comps),
            flat(rows_x),
            flat(slabs * sum_rows),
        ),
        received,
        right_side,
        design,
        name="residual",
        flops=1 << 26,
    )
    all_sums = exchange(sums, "slab")

    def powers_body(geo_ref, one_ref, two_ref, three_ref):
        above, below = shifts(plane, rows_x)
        scale_row = lambda row: geo_ref[0, row]
        for source, target, edge in ((one_ref, two_ref, 2), (two_ref, three_ref, 3)):

            def load_row(row):
                free = geo_ref[1, row]
                return [free * source[comp, row] for comp in range(comps)]

            def emit(row, forces, carried):
                free, inverse = geo_ref[1, row], geo_ref[2, row]
                for comp, force in enumerate(forces):
                    target[comp, row] = (
                        free * force + (1.0 - free) * source[comp, row]
                    ) * inverse
                return carried

            apply_rows(
                edge, span - 1 - edge, load_row, scale_row, emit, above, below,
                jnp.zeros((1, 1), F32),
            )

    second, third = call(
        powers_body,
        (block(comps), block(comps)),
        geometry,
        first,
        name="powers",
        flops=1 << 26,
    )

    def energy_body(
        sums_ref, disp_ref, cube_ref, geo_ref, zero_ref, one_ref, two_ref, three_ref,
        disp_out_ref, numer_ref, count_ref, weak_ref,
    ):
        above, below = shifts(plane, rows_x)
        gather = lambda index: sum(
            sums_ref[layer * sum_rows + index : layer * sum_rows + index + 1]
            for layer in range(slabs)
        )
        curve, weight, count = gather(0), gather(1), gather(2)
        across = lambda value: jnp.sum(value, 1, keepdims=True)
        count_ref[...] = jnp.broadcast_to(across(count), (8, width))
        owner = iota((1, width), 1) // rows_x
        inverse = jnp.zeros((1, width), F32)
        for load in range(loads):
            mine = owner == load
            upper = UPPER_FACTOR * (
                across(jnp.where(mine, curve, 0.0)) / across(jnp.where(mine, weight, 0.0))
            )
            inverse = jnp.where(mine, 1.0 / (0.5 * (upper + LOWER_RATIO * upper)), inverse)
        inverse = jnp.broadcast_to(inverse, plane)
        lower = None
        for row in range(HALO_LOW, HALO_LOW + strip + 1):
            free = geo_ref[1, row]
            values = []
            for comp in range(comps):
                value = smoother[3] * three_ref[comp, row]
                value = smoother[2] * two_ref[comp, row] + inverse * value
                value = smoother[1] * one_ref[comp, row] + inverse * value
                value = smoother[0] * zero_ref[comp, row] + inverse * value
                value = disp_ref[comp, row] + inverse * value
                if row < HALO_LOW + strip:
                    place = comp * strip + row - HALO_LOW
                    disp_out_ref[pl.ds(place, depth, stride=out_rows), :] = value
                values.append(free * value)
            modes = row_modes(values, above)
            if lower is not None:
                weak_ref[(row - 1 - HALO_LOW) * depth : (row - HALO_LOW) * depth] = (
                    (3.0 * (1.0 - STIFF_VOID))
                    * cube_ref[0, row - 1]
                    * element_energy(element_modes(lower, modes))
                )
            lower = modes
        disp_out_ref[pl.ds(out_rows - 1, depth, stride=out_rows), :] = jnp.zeros(plane, F32)
        weak = weak_ref[...]
        smooth = jnp.zeros((depth * half, width), F32)
        for part in range(strip // half):
            shape = (depth * half, strip * depth)
            to, source = iota(shape, 0), iota(shape, 1)
            table = jnp.where(
                to % half + part * half == source // depth,
                gauss(to // half - source % depth),
                0.0,
            )
            shape = (width, width)
            to, source = iota(shape, 1), iota(shape, 0)
            table_x = jnp.where(
                to // rows_x == part, gauss(to % rows_x - source % rows_x), 0.0
            )
            smooth = smooth + dot(dot(table, weak), table_x)
        weighted = jnp.zeros((1, width), F32)
        for layer in range(depth):
            piece = smooth[layer * half : (layer + 1) * half]
            base = layer * sum_rows
            weighted = weighted + jnp.sum(
                piece * sums_ref[base + 3 : base + sum_rows], 0, keepdims=True
            )
        for layer in range(depth):
            piece = smooth[layer * half : (layer + 1) * half]
            for part in range(parts):
                base = (part * slabs + layer) * numer_rows
                numer_ref[base : base + half] = piece
                numer_ref[base + half : base + numer_rows] = weighted

    disp_message, numer_message, count = call(
        energy_body,
        (flat(slabs * out_rows), flat(parts * slabs * numer_rows), flat(8)),
        all_sums,
        disp,
        cube,
        geometry,
        zeroth,
        first,
        second,
        third,
        scratch=[pltpu.VMEM((strip * depth, width), F32)],
        name="energy",
        flops=1 << 24,
    )
    numer_pieces = exchange(numer_message, ("load", "slab"))

    def trial_body(
        numer_ref, dens_ref, filtered_ref, design_ref, count_ref, disp_ref, trial_ref, out_ref, plane_ref
    ):
        weighted = jnp.zeros((1, width), F32)
        for source in range(slabs):
            total = jnp.zeros((half, width), F32)
            for part in range(parts):
                base = (part * slabs + source) * numer_rows
                total = total + numer_ref[base : base + half]
                weighted = weighted + numer_ref[base + half : base + numer_rows]
            plane_ref[source * half : (source + 1) * half] = total
        mean = jnp.sum(weighted, 1, keepdims=True) / count_ref[0:1] + EPSILON
        packed = plane_ref[...].T
        numer = jnp.zeros((rows_x, cols_y), F32)
        for part in range(strip // half):
            shape = (slabs * half, cols_y)
            row = iota(shape, 0)
            table = gauss(row // half * strip + part * half + row % half - iota(shape, 1))
            numer = numer + dot(packed[part * rows_x : (part + 1) * rows_x], table)
        mask = design_ref[0].astype(F32)
        dens = dens_ref[0]
        ratio = mask * (numer / filtered_ref[...]) / mean
        trial = jnp.clip(dens * jnp.sqrt(ratio), dens - MOVE_LIMIT, dens + MOVE_LIMIT)
        trial_ref[...] = trial
        out_ref[...] = disp_ref[...]
        volume = jnp.sum(mask * trial, 0, keepdims=True)
        for target in range(slabs):
            base = (target + 1) * out_rows - 1
            out_ref[base : base + 1] = volume

    trial, out_message = call(
        trial_body,
        (flat(rows_x), flat(slabs * out_rows)),
        numer_pieces,
        density,
        dens_filtered,
        design,
        count,
        disp_message,
        scratch=[pltpu.VMEM((slabs * half, width), F32)],
        name="trial",
    )
    out_pieces = exchange(out_message, "slab")

    def final_body(pieces_ref, trial_ref, design_ref, count_ref, disp_ref, dens_ref, whole_ref):
        volume = jnp.zeros((1, width), F32)
        for source in range(slabs):
            base = (source + 1) * out_rows
            volume = volume + pieces_ref[base - 1 : base]
            for comp in range(comps):
                base = source * out_rows + comp * strip
                whole_ref[comp, source * strip : (source + 1) * strip] = pieces_ref[
                    base : base + strip
                ]
        volume = jnp.sum(volume, 1, keepdims=True)
        scale = VOLUME_TARGET / (volume / count_ref[0:1] + EPSILON)
        mask = design_ref[0].astype(F32)
        dens_ref[0] = mask * jnp.minimum(scale * trial_ref[...], 1.0)
        for comp in range(comps):
            turned = whole_ref[comp].T
            for load in range(loads):
                disp_ref[load, comp, 0] = turned[load * rows_x : (load + 1) * rows_x]

    return call(
        final_body,
        (
            jax.ShapeDtypeStruct(start_disp.shape, F32),
            jax.ShapeDtypeStruct(density.shape, F32),
        ),
        out_pieces,
        trial,
        design,
        count,
        scratch=[pltpu.VMEM((comps, cols_y, width), F32)],
        name="final",
    )


def solution(mesh):
    return jax.shard_map(
        shards,
        mesh=mesh,
        in_specs=(
            P("load", None, "slab", None, None),
            P("slab", None, None),
            P("slab", None, None),
            P("slab", None, None),
            P("load", None),
            P("load", None, None),
        ),
        out_specs=(P("load", None, "slab", None, None), P("slab", None, None)),
        check_vma=False,
    )
```

```python
import functools

import jax
import jax.numpy as jnp
import numpy as np
from jax import lax
from jax.experimental import pallas as pl
from jax.experimental.pallas import tpu as pltpu
from jax.sharding import PartitionSpec as P

RADIUS = 2
POISSON = 0.3
STIFF_VOID = 0.001
UPPER_FACTOR = 1.2
LOWER_RATIO = 0.1
MOVE_LIMIT = 0.2
VOLUME_TARGET = 0.5
EPSILON = 1e-06
HIGHEST = lax.Precision.HIGHEST
F32 = jnp.float32

HALO_LOW = 4
HALO_HIGH = 5
HALO = HALO_LOW + HALO_HIGH
VMEM_LIMIT = 24 * 1024 * 1024


def hex_stiffness():
    lame_first = POISSON / ((1 + POISSON) * (1 - 2 * POISSON))
    lame_shear = 1 / (2 * (1 + POISSON))
    elastic = np.zeros((6, 6))
    elastic[:3, :3] = lame_first
    for axis_a in range(3):
        elastic[axis_a, axis_a] += 2 * lame_shear
        elastic[3 + axis_a, 3 + axis_a] = lame_shear
    shear_pairs = ((0, 1), (1, 2), (0, 2))
    gauss_point = 1 / np.sqrt(3)
    matrix = np.zeros((24, 24))
    for quad_index in range(8):
        quad_coords = [
            gauss_point * (2 * (quad_index >> 2 - axis_a & 1) - 1) for axis_a in range(3)
        ]
        shape_grads = np.zeros((8, 3))
        for corner in range(8):
            corner_signs = [2 * (corner >> 2 - axis_a & 1) - 1 for axis_a in range(3)]
            for axis_a in range(3):
                deriv_value = float(corner_signs[axis_a])
                for axis_b in range(3):
                    if axis_b != axis_a:
                        deriv_value *= (1 + corner_signs[axis_b] * quad_coords[axis_b]) / 2
                shape_grads[corner, axis_a] = deriv_value
        strain = np.zeros((6, 24))
        for corner in range(8):
            for axis_a in range(3):
                strain[axis_a, 3 * corner + axis_a] = shape_grads[corner, axis_a]
            for pair_index, shear_pair in enumerate(shear_pairs):
                strain[3 + pair_index, 3 * corner + shear_pair[0]] = shape_grads[
                    corner, shear_pair[1]
                ]
                strain[3 + pair_index, 3 * corner + shear_pair[1]] = shape_grads[
                    corner, shear_pair[0]
                ]
        matrix += strain.T @ elastic @ strain / 8
    return matrix.astype(np.float32)


def mode_stiffness():
    signs = np.zeros((8, 8))
    for mode in range(8):
        for corner in range(8):
            flips = bin(mode & ~corner & 7).count("1")
            signs[mode, corner] = -1.0 if flips & 1 else 1.0
    spread = np.kron(signs, np.eye(3))
    return spread @ hex_stiffness().astype(np.float64) @ spread.T / 64


MODES = mode_stiffness()
DIAG_ENTRY = float(hex_stiffness()[0, 0])


def entry(mode_a, comp_a, mode_b, comp_b):
    return float(MODES[3 * mode_a + comp_a, 3 * mode_b + comp_b])


NORMAL = ((4, 0), (2, 1), (1, 2))
SHEAR = (((2, 0), (4, 1)), ((1, 0), (4, 2)), ((1, 1), (2, 2)))
TWIST = ((3, 0), (5, 1), (6, 2))
BEND = (((3, 1), (5, 0)), ((3, 2), (6, 0)), ((5, 2), (6, 1)))
WARP = ((7, 0), (7, 1), (7, 2))
NORMAL_ON = entry(4, 0, 4, 0)
NORMAL_OFF = entry(4, 0, 2, 1)
SHEAR_ON = entry(2, 0, 4, 1)
TWIST_ON = entry(3, 0, 3, 0)
TWIST_OFF = entry(3, 0, 5, 1)
BEND_ON = entry(3, 1, 3, 1)
BEND_OFF = entry(3, 1, 5, 0)
WARP_ON = entry(7, 0, 7, 0)


def smoother_factors():
    sigma = (1 + LOWER_RATIO) / (1 - LOWER_RATIO)
    factor = 1 / sigma
    residual = np.array([1.0, 0.0, 0.0, 0.0])
    update = np.array([1.0, 0.0, 0.0, 0.0])
    total = np.zeros(4)
    for sweep in range(4):
        total = total + update
        if sweep < 3:
            residual = residual - np.concatenate([[0.0], update[:3]])
            factor_next = 1 / (2 * sigma - factor)
            update = factor_next * factor * update + 2 * factor_next * sigma * residual
            factor = factor_next
    return [float(value) for value in total]


def iota(shape, axis):
    return lax.broadcasted_iota(jnp.int32, shape, axis)


def gauss(offsets):
    return jnp.exp(-((offsets.astype(F32) / RADIUS) ** 2))


def gauss_table(count):
    return gauss(iota((count, count), 0) - iota((count, count), 1))


def shifts(shape, rows_x):
    inner = {}
    for axis, count in ((0, shape[0]), (1, rows_x)):
        index = iota(shape, axis) % count
        inner[axis] = (index < count - 1, index > 0)

    def above(value, axis):
        moved = pltpu.roll(value, shape[axis] - 1, axis)
        return jnp.where(inner[axis][0], moved, 0.0)

    def below(value, axis):
        moved = pltpu.roll(value, 1, axis)
        return jnp.where(inner[axis][1], moved, 0.0)

    return above, below


def row_modes(values, above):
    modes = {}
    for comp, value in enumerate(values):
        beside = above(value, 1)
        for bit, part in ((0, value + beside), (2, beside - value)):
            ahead = above(part, 0)
            modes[bit, comp] = part + ahead
            modes[bit + 4, comp] = ahead - part
    return modes


def element_modes(low, high):
    modes = {}
    for (bits, comp), value in low.items():
        other = high[bits, comp]
        if bits:
            modes[bits, comp] = value + other
        modes[bits + 1, comp] = other - value
    return modes


def element_forces(modes, scale):
    forces = {}
    total = modes[NORMAL[0]] + modes[NORMAL[1]] + modes[NORMAL[2]]
    shared = (scale * NORMAL_OFF) * total
    own = scale * (NORMAL_ON - NORMAL_OFF)
    for key in NORMAL:
        forces[key] = shared + own * modes[key]
    shear = scale * SHEAR_ON
    for key_a, key_b in SHEAR:
        forces[key_a] = forces[key_b] = shear * (modes[key_a] + modes[key_b])
    total = modes[TWIST[0]] + modes[TWIST[1]] + modes[TWIST[2]]
    shared = (scale * TWIST_OFF) * total
    own = scale * (TWIST_ON - TWIST_OFF)
    for key in TWIST:
        forces[key] = shared + own * modes[key]
    bend_on = scale * BEND_ON
    bend_off = scale * BEND_OFF
    for key_a, key_b in BEND:
        forces[key_a] = bend_on * modes[key_a] + bend_off * modes[key_b]
        forces[key_b] = bend_on * modes[key_b] + bend_off * modes[key_a]
    warp = scale * WARP_ON
    for key in WARP:
        forces[key] = warp * modes[key]
    return forces


def element_energy(modes):
    total = modes[NORMAL[0]] + modes[NORMAL[1]] + modes[NORMAL[2]]
    squares = sum(modes[key] * modes[key] for key in NORMAL)
    energy = NORMAL_OFF * (total * total) + (NORMAL_ON - NORMAL_OFF) * squares
    shear = 0.0
    for key_a, key_b in SHEAR:
        both = modes[key_a] + modes[key_b]
        shear = shear + both * both
    energy = energy + SHEAR_ON * shear
    total = modes[TWIST[0]] + modes[TWIST[1]] + modes[TWIST[2]]
    squares = sum(modes[key] * modes[key] for key in TWIST)
    energy = energy + TWIST_OFF * (total * total) + (TWIST_ON - TWIST_OFF) * squares
    squares = sum(modes[key] * modes[key] for pair in BEND for key in pair)
    crossed = sum(modes[key_a] * modes[key_b] for key_a, key_b in BEND)
    energy = energy + BEND_ON * squares + (2 * BEND_OFF) * crossed
    squares = sum(modes[key] * modes[key] for key in WARP)
    return energy + WARP_ON * squares


ROW_KEYS = [(bits, comp) for comp in range(3) for bits in (0, 2, 4, 6)]


def split_forces(forces):
    here, there = {}, {}
    for bits, comp in ROW_KEYS:
        change = forces[bits + 1, comp]
        if bits:
            common = forces[bits, comp]
            here[bits, comp] = common - change
            there[bits, comp] = common + change
        else:
            here[bits, comp] = -change
            there[bits, comp] = change
    return here, there


def node_forces(modes, below):
    values = []
    for comp in range(3):
        parts = []
        for bit in (0, 2):
            common, change = modes[bit, comp], modes[bit + 4, comp]
            parts.append((common - change) + below(common + change, 0))
        values.append((parts[0] - parts[1]) + below(parts[0] + parts[1], 1))
    return values


def apply_rows(first, last, load_row, scale_row, emit, above, below, carry=None):
    def advance(index, low, pending):
        high = row_modes(load_row(index + 1), above)
        forces = element_forces(element_modes(low, high), scale_row(index))
        here, there = split_forces(forces)
        return high, {key: pending[key] + here[key] for key in ROW_KEYS}, there

    def pack(low, pending):
        return tuple(low[key] for key in ROW_KEYS) + tuple(pending[key] for key in ROW_KEYS)

    def unpack(state):
        count = len(ROW_KEYS)
        return dict(zip(ROW_KEYS, state[:count])), dict(zip(ROW_KEYS, state[count:]))

    low = row_modes(load_row(first), above)
    zero = {key: jnp.zeros_like(low[key]) for key in ROW_KEYS}
    low, _, pending = advance(first, low, zero)

    def step(index, state):
        carried, (low, pending) = state[0], unpack(state[1])
        low, modes, pending = advance(index, low, pending)
        carried = emit(index, node_forces(modes, below), carried)
        return carried, pack(low, pending)

    for index in range(first + 1, last):
        low, modes, pending = advance(index, low, pending)
        carry = emit(index, node_forces(modes, below), carry)
    return carry


def dot(left, right):
    return jnp.dot(left, right, precision=HIGHEST, preferred_element_type=F32)


def call(body, outs, *args, scratch=(), name=None, flops=0, space=pltpu.VMEM):
    return pl.pallas_call(
        body,
        out_shape=outs,
        in_specs=[pl.BlockSpec(memory_space=space)] * len(args),
        out_specs=jax.tree.map(lambda _: pl.BlockSpec(memory_space=pltpu.VMEM), outs),
        scratch_shapes=list(scratch),
        compiler_params=pltpu.CompilerParams(vmem_limit_bytes=VMEM_LIMIT),
        cost_estimate=pl.CostEstimate(flops=flops, bytes_accessed=1 << 20, transcendentals=0),
        name=name,
    )(*args)


def exchange(message, axes):
    rows = message.shape[0]
    return lax.all_to_all(
        message.reshape(rows, 1, message.shape[1]), axes, split_axis=0, concat_axis=0, tiled=True
    ).reshape(message.shape)


def shards(start_disp, density, design, support, load_nodes, load_forces):
    slabs = lax.axis_size("slab")
    parts = lax.axis_size("load")
    loads, comps, layers, rows_x, cols_y = start_disp.shape
    points = load_nodes.shape[1]
    depth = slabs * layers
    strip = cols_y // slabs
    span = strip + HALO
    width = loads * rows_x
    half = strip * rows_x // width
    plane = (depth, width)
    in_rows = (comps + 1) * span + rows_x
    sum_rows = 3 + half
    numer_rows = half + 1
    out_rows = comps * strip + 1
    block = lambda count: jax.ShapeDtypeStruct((count, span) + plane, F32)
    flat = lambda rows: jax.ShapeDtypeStruct((rows, width), F32)
    smoother = smoother_factors()

    def pack_body(
        disp_ref, dens_ref, design_ref, support_ref, out_ref,
        stage_ref, dens_in, design_in, support_in, pad_ref, sems,
    ):
        copies = [
            pltpu.make_async_copy(dens_ref.at[0], dens_in, sems.at[0]),
            pltpu.make_async_copy(design_ref.at[0], design_in, sems.at[1]),
            pltpu.make_async_copy(support_ref.at[0], support_in, sems.at[2]),
        ]
        for load in range(loads):
            copies.append(
                pltpu.make_async_copy(
                    disp_ref.at[load, :, 0],
                    stage_ref.at[:, load * rows_x : (load + 1) * rows_x],
                    sems.at[3 + load],
                )
            )
        for copy in copies:
            copy.start()
        cube_side = iota((1, width), 1) < rows_x
        for field in range(comps + 1):
            fill = jnp.zeros((1, width), F32) if field < comps else jnp.where(cube_side, -1.0, 1.0)
            pad_ref[field, 0:HALO_LOW] = jnp.broadcast_to(fill, (HALO_LOW, width))
            pad_ref[field, HALO_LOW + cols_y : HALO + cols_y] = jnp.broadcast_to(
                fill, (HALO_HIGH, width)
            )
        for copy in copies[:3]:
            copy.wait()
        solid = design_in[...].astype(F32) * dens_in[...]
        both = jnp.concatenate([solid * solid * solid, support_in[...].astype(F32)], 0)
        pad_ref[comps, HALO_LOW : HALO_LOW + cols_y] = both.T
        for copy in copies[3:]:
            copy.wait()
        for comp in range(comps):
            pad_ref[comp, HALO_LOW : HALO_LOW + cols_y] = stage_ref[comp].T
        for target in range(slabs):
            base = target * in_rows
            for field in range(comps + 1):
                out_ref[base + field * span : base + (field + 1) * span] = pad_ref[
                    field, target * strip : target * strip + span
                ]
            out_ref[base + (comps + 1) * span : base + in_rows] = dens_in[...]

    message = call(
        pack_body,
        flat(slabs * in_rows),
        *(
            pltpu.with_memory_space_constraint(value, pltpu.HBM)
            for value in (start_disp, density, design, support)
        ),
        scratch=[
            pltpu.VMEM((comps, width, cols_y), F32),
            pltpu.VMEM((rows_x, cols_y), F32),
            pltpu.VMEM((rows_x, cols_y), jnp.int32),
            pltpu.VMEM((rows_x, cols_y), jnp.int32),
            pltpu.VMEM((comps + 1, cols_y + 2 * 8, width), F32),
            pltpu.SemaphoreType.DMA((3 + loads,)),
        ],
        name="pack",
        space=pltpu.HBM,
    )
    received = exchange(message, "slab")

    cells = -(-span * depth // 16) * 16
    chunk = min(256, points)

    def loads_body(nodes_ref, forces_ref, out_ref):
        first = lax.axis_index("slab") * strip - HALO_LOW
        out_ref[...] = jnp.zeros_like(out_ref)
        for load in range(loads):
            for start in range(0, points, chunk):
                part = slice(start, start + chunk)
                node = nodes_ref[load : load + 1, part]
                row = node % cols_y - first
                lane = load * rows_x + (node // cols_y) % rows_x
                layer = node // (cols_y * rows_x)
                cell = jnp.where((row >= 0) & (row < span), row * depth + layer, -1)
                hit = iota((cells, chunk), 0) == cell
                spot = (iota((width, chunk), 0) == lane).astype(F32).astype(jnp.bfloat16)
                for comp in range(comps):
                    rest = forces_ref[load, comp : comp + 1, part]
                    for piece in range(3):
                        rounded = rest.astype(jnp.bfloat16).astype(F32)
                        rest = rest - rounded
                        picked = jnp.where(hit, rounded, 0.0).astype(jnp.bfloat16)
                        out_ref[comp] += lax.dot_general(
                            picked, spot, (((1,), (1,)), ((), ())), preferred_element_type=F32
                        )

    right_side = call(
        loads_body,
        jax.ShapeDtypeStruct((comps, cells, width), F32),
        load_nodes,
        load_forces,
        name="point_loads",
        flops=1 << 28,
    )

    def own_row(row):
        return (row >= HALO_LOW) & (row < HALO_LOW + strip)

    def packed_table(part):
        shape = (slabs * half, cols_y)
        row = iota(shape, 0)
        return gauss(row // half * strip + part * half + row % half - iota(shape, 1))

    def residual_body(
        in_ref, rhs_ref, design_ref, disp_ref, cube_ref, geo_ref, zero_ref, one_ref, dens_ref, sum_ref
    ):
        above, below = shifts(plane, rows_x)
        cube_side = iota(plane, 1) < rows_x
        for row in range(span):
            pick = lambda field: in_ref[pl.ds(field * span + row, depth, stride=in_rows), :]
            for comp in range(comps):
                disp_ref[comp, row] = pick(comp)
            both = pick(comps)
            other = pltpu.roll(both, rows_x, 1)
            cube = jnp.where(cube_side, both, other)
            cube_ref[0, row] = cube
            geo_ref[0, row] = jnp.where(
                cube < 0.0, 0.0, STIFF_VOID + (1.0 - STIFF_VOID) * cube
            )
            geo_ref[1, row] = 1.0 - jnp.where(cube_side, other, both)
        for row in range(1, span - 1):
            beside = geo_ref[0, row] + geo_ref[0, row - 1]
            beside = beside + below(beside, 0)
            beside = beside + below(beside, 1)
            free = geo_ref[1, row]
            geo_ref[2, row] = 1.0 / (free * DIAG_ENTRY * beside + (1.0 - free))

        scale_row = lambda row: geo_ref[0, row]

        def start_row(row):
            free = geo_ref[1, row]
            return [free * disp_ref[comp, row] for comp in range(comps)]

        def emit_residual(row, forces, carried):
            free, inverse = geo_ref[1, row], geo_ref[2, row]
            total = jnp.zeros(plane, F32)
            for comp, force in enumerate(forces):
                load_row = rhs_ref[comp, pl.ds(row * depth, depth), :]
                rest = free * (load_row - force) - (1.0 - free) * disp_ref[comp, row]
                value = rest * inverse
                zero_ref[comp, row] = value
                total = total + value * rest
            return carried + total if own_row(row) else carried

        weight = apply_rows(
            0, span - 1, start_row, scale_row, emit_residual, above, below,
            jnp.zeros(plane, F32),
        )

        def zero_row(row):
            free = geo_ref[1, row]
            return [free * zero_ref[comp, row] for comp in range(comps)]

        def emit_one(row, forces, carried):
            free, inverse = geo_ref[1, row], geo_ref[2, row]
            total = jnp.zeros(plane, F32)
            for comp, force in enumerate(forces):
                value = zero_ref[comp, row]
                applied = free * force + (1.0 - free) * value
                one_ref[comp, row] = applied * inverse
                total = total + value * applied
            return carried + total if own_row(row) else carried

        curve = apply_rows(
            1, span - 2, zero_row, scale_row, emit_one, above, below, jnp.zeros(plane, F32)
        )

        here = lax.axis_index("slab")
        mixed = jnp.zeros((rows_x, cols_y), F32)
        for layer in range(depth):
            weight_z = gauss(jnp.full((1, cols_y), here - layer, jnp.int32))
            base = layer * in_rows + (comps + 1) * span
            mixed = mixed + weight_z * in_ref[base : base + rows_x]
        mixed = dot(gauss_table(rows_x), mixed)
        filtered = dot(mixed, gauss_table(cols_y))
        dens_ref[...] = filtered
        mask = design_ref[0].astype(F32)
        share = (mask / filtered).T
        share = jnp.concatenate(
            [dot(packed_table(part), share) for part in range(strip // half)], 1
        )
        down = lambda value: jnp.sum(value, 0, keepdims=True)
        sums = [down(curve), down(weight), down(mask)]
        for target in range(slabs):
            base = target * sum_rows
            for index, value in enumerate(sums):
                sum_ref[base + index : base + index + 1] = value
            sum_ref[base + 3 : base + sum_rows] = share[target * half : (target + 1) * half]

    disp, cube, geometry, zeroth, first, dens_filtered, sums = call(
        residual_body,
        (
            block(comps),
            block(1),
            block(3),
            block(comps),
            block(comps),
            flat(rows_x),
            flat(slabs * sum_rows),
        ),
        received,
        right_side,
        design,
        name="residual",
        flops=1 << 26,
    )
    all_sums = exchange(sums, "slab")

    def powers_body(geo_ref, one_ref, two_ref, three_ref):
        above, below = shifts(plane, rows_x)
        scale_row = lambda row: geo_ref[0, row]
        for source, target, edge in ((one_ref, two_ref, 2), (two_ref, three_ref, 3)):

            def load_row(row):
                free = geo_ref[1, row]
                return [free * source[comp, row] for comp in range(comps)]

            def emit(row, forces, carried):
                free, inverse = geo_ref[1, row], geo_ref[2, row]
                for comp, force in enumerate(forces):
                    target[comp, row] = (
                        free * force + (1.0 - free) * source[comp, row]
                    ) * inverse
                return carried

            apply_rows(
                edge, span - 1 - edge, load_row, scale_row, emit, above, below,
                jnp.zeros((1, 1), F32),
            )

    second, third = call(
        powers_body,
        (block(comps), block(comps)),
        geometry,
        first,
        name="powers",
        flops=1 << 26,
    )

    def energy_body(
        sums_ref, disp_ref, cube_ref, geo_ref, zero_ref, one_ref, two_ref, three_ref,
        disp_out_ref, numer_ref, count_ref, weak_ref,
    ):
        above, below = shifts(plane, rows_x)
        gather = lambda index: sum(
            sums_ref[layer * sum_rows + index : layer * sum_rows + index + 1]
            for layer in range(slabs)
        )
        curve, weight, count = gather(0), gather(1), gather(2)
        across = lambda value: jnp.sum(value, 1, keepdims=True)
        count_ref[...] = jnp.broadcast_to(across(count), (8, width))
        owner = iota((1, width), 1) // rows_x
        inverse = jnp.zeros((1, width), F32)
        for load in range(loads):
            mine = owner == load
            upper = UPPER_FACTOR * (
                across(jnp.where(mine, curve, 0.0)) / across(jnp.where(mine, weight, 0.0))
            )
            inverse = jnp.where(mine, 1.0 / (0.5 * (upper + LOWER_RATIO * upper)), inverse)
        inverse = jnp.broadcast_to(inverse, plane)
        lower = None
        for row in range(HALO_LOW, HALO_LOW + strip + 1):
            free = geo_ref[1, row]
            values = []
            for comp in range(comps):
                value = smoother[3] * three_ref[comp, row]
                value = smoother[2] * two_ref[comp, row] + inverse * value
                value = smoother[1] * one_ref[comp, row] + inverse * value
                value = smoother[0] * zero_ref[comp, row] + inverse * value
                value = disp_ref[comp, row] + inverse * value
                if row < HALO_LOW + strip:
                    place = comp * strip + row - HALO_LOW
                    disp_out_ref[pl.ds(place, depth, stride=out_rows), :] = value
                values.append(free * value)
            modes = row_modes(values, above)
            if lower is not None:
                weak_ref[(row - 1 - HALO_LOW) * depth : (row - HALO_LOW) * depth] = (
                    (3.0 * (1.0 - STIFF_VOID))
                    * cube_ref[0, row - 1]
                    * element_energy(element_modes(lower, modes))
                )
            lower = modes
        disp_out_ref[pl.ds(out_rows - 1, depth, stride=out_rows), :] = jnp.zeros(plane, F32)
        weak = weak_ref[...]
        smooth = jnp.zeros((depth * half, width), F32)
        for part in range(strip // half):
            shape = (depth * half, strip * depth)
            to, source = iota(shape, 0), iota(shape, 1)
            table = jnp.where(
                to % half + part * half == source // depth,
                gauss(to // half - source % depth),
                0.0,
            )
            shape = (width, width)
            to, source = iota(shape, 1), iota(shape, 0)
            table_x = jnp.where(
                to // rows_x == part, gauss(to % rows_x - source % rows_x), 0.0
            )
            smooth = smooth + dot(dot(table, weak), table_x)
        weighted = jnp.zeros((1, width), F32)
        for layer in range(depth):
            piece = smooth[layer * half : (layer + 1) * half]
            base = layer * sum_rows
            weighted = weighted + jnp.sum(
                piece * sums_ref[base + 3 : base + sum_rows], 0, keepdims=True
            )
        for layer in range(depth):
            piece = smooth[layer * half : (layer + 1) * half]
            for part in range(parts):
                base = (part * slabs + layer) * numer_rows
                numer_ref[base : base + half] = piece
                numer_ref[base + half : base + numer_rows] = weighted

    disp_message, numer_message, count = call(
        energy_body,
        (flat(slabs * out_rows), flat(parts * slabs * numer_rows), flat(8)),
        all_sums,
        disp,
        cube,
        geometry,
        zeroth,
        first,
        second,
        third,
        scratch=[pltpu.VMEM((strip * depth, width), F32)],
        name="energy",
        flops=1 << 24,
    )
    numer_pieces = exchange(numer_message, ("load", "slab"))

    def trial_body(
        numer_ref, dens_ref, filtered_ref, design_ref, count_ref, disp_ref, trial_ref, out_ref, plane_ref
    ):
        weighted = jnp.zeros((1, width), F32)
        for source in range(slabs):
            total = jnp.zeros((half, width), F32)
            for part in range(parts):
                base = (part * slabs + source) * numer_rows
                total = total + numer_ref[base : base + half]
                weighted = weighted + numer_ref[base + half : base + numer_rows]
            plane_ref[source * half : (source + 1) * half] = total
        mean = jnp.sum(weighted, 1, keepdims=True) / count_ref[0:1] + EPSILON
        packed = plane_ref[...].T
        numer = jnp.zeros((rows_x, cols_y), F32)
        for part in range(strip // half):
            shape = (slabs * half, cols_y)
            row = iota(shape, 0)
            table = gauss(row // half * strip + part * half + row % half - iota(shape, 1))
            numer = numer + dot(packed[part * rows_x : (part + 1) * rows_x], table)
        mask = design_ref[0].astype(F32)
        dens = dens_ref[0]
        ratio = mask * (numer / filtered_ref[...]) / mean
        trial = jnp.clip(dens * jnp.sqrt(ratio), dens - MOVE_LIMIT, dens + MOVE_LIMIT)
        trial_ref[...] = trial
        out_ref[...] = disp_ref[...]
        volume = jnp.sum(mask * trial, 0, keepdims=True)
        for target in range(slabs):
            base = (target + 1) * out_rows - 1
            out_ref[base : base + 1] = volume

    trial, out_message = call(
        trial_body,
        (flat(rows_x), flat(slabs * out_rows)),
        numer_pieces,
        density,
        dens_filtered,
        design,
        count,
        disp_message,
        scratch=[pltpu.VMEM((slabs * half, width), F32)],
        name="trial",
    )
    out_pieces = exchange(out_message, "slab")

    def final_body(pieces_ref, trial_ref, design_ref, count_ref, disp_ref, dens_ref, whole_ref):
        volume = jnp.zeros((1, width), F32)
        for source in range(slabs):
            base = (source + 1) * out_rows
            volume = volume + pieces_ref[base - 1 : base]
            for comp in range(comps):
                base = source * out_rows + comp * strip
                whole_ref[comp, source * strip : (source + 1) * strip] = pieces_ref[
                    base : base + strip
                ]
        volume = jnp.sum(volume, 1, keepdims=True)
        scale = VOLUME_TARGET / (volume / count_ref[0:1] + EPSILON)
        mask = design_ref[0].astype(F32)
        dens_ref[0] = mask * jnp.minimum(scale * trial_ref[...], 1.0)
        for comp in range(comps):
            turned = whole_ref[comp].T
            for load in range(loads):
                disp_ref[load, comp, 0] = turned[load * rows_x : (load + 1) * rows_x]

    return call(
        final_body,
        (
            jax.ShapeDtypeStruct(start_disp.shape, F32),
            jax.ShapeDtypeStruct(density.shape, F32),
        ),
        out_pieces,
        trial,
        design,
        count,
        scratch=[pltpu.VMEM((comps, cols_y, width), F32)],
        name="final",
    )


def solution(mesh):
    return jax.shard_map(
        shards,
        mesh=mesh,
        in_specs=(
            P("load", None, "slab", None, None),
            P("slab", None, None),
            P("slab", None, None),
            P("slab", None, None),
            P("load", None),
            P("load", None, None),
        ),
        out_specs=(P("load", None, "slab", None, None), P("slab", None, None)),
        check_vma=False,
    )
```

```python
import functools

import jax
import jax.numpy as jnp
import numpy as np
from jax import lax
from jax.experimental import pallas as pl
from jax.experimental.pallas import tpu as pltpu
from jax.sharding import PartitionSpec as P

RADIUS = 2
POISSON = 0.3
STIFF_VOID = 0.001
UPPER_FACTOR = 1.2
LOWER_RATIO = 0.1
MOVE_LIMIT = 0.2
VOLUME_TARGET = 0.5
EPSILON = 1e-06
F32 = jnp.float32

HALO_LOW = 4
HALO_HIGH = 5
HALO = HALO_LOW + HALO_HIGH
VMEM_LIMIT = 24 * 1024 * 1024


def hex_stiffness():
    lame_first = POISSON / ((1 + POISSON) * (1 - 2 * POISSON))
    lame_shear = 1 / (2 * (1 + POISSON))
    elastic = np.zeros((6, 6))
    elastic[:3, :3] = lame_first
    for axis_a in range(3):
        elastic[axis_a, axis_a] += 2 * lame_shear
        elastic[3 + axis_a, 3 + axis_a] = lame_shear
    shear_pairs = ((0, 1), (1, 2), (0, 2))
    gauss_point = 1 / np.sqrt(3)
    matrix = np.zeros((24, 24))
    for quad_index in range(8):
        quad_coords = [
            gauss_point * (2 * (quad_index >> 2 - axis_a & 1) - 1) for axis_a in range(3)
        ]
        shape_grads = np.zeros((8, 3))
        for corner in range(8):
            corner_signs = [2 * (corner >> 2 - axis_a & 1) - 1 for axis_a in range(3)]
            for axis_a in range(3):
                deriv_value = float(corner_signs[axis_a])
                for axis_b in range(3):
                    if axis_b != axis_a:
                        deriv_value *= (1 + corner_signs[axis_b] * quad_coords[axis_b]) / 2
                shape_grads[corner, axis_a] = deriv_value
        strain = np.zeros((6, 24))
        for corner in range(8):
            for axis_a in range(3):
                strain[axis_a, 3 * corner + axis_a] = shape_grads[corner, axis_a]
            for pair_index, shear_pair in enumerate(shear_pairs):
                strain[3 + pair_index, 3 * corner + shear_pair[0]] = shape_grads[
                    corner, shear_pair[1]
                ]
                strain[3 + pair_index, 3 * corner + shear_pair[1]] = shape_grads[
                    corner, shear_pair[0]
                ]
        matrix += strain.T @ elastic @ strain / 8
    return matrix.astype(np.float32)


def mode_stiffness():
    signs = np.zeros((8, 8))
    for mode in range(8):
        for corner in range(8):
            flips = bin(mode & ~corner & 7).count("1")
            signs[mode, corner] = -1.0 if flips & 1 else 1.0
    spread = np.kron(signs, np.eye(3))
    return spread @ hex_stiffness().astype(np.float64) @ spread.T / 64


MODES = mode_stiffness()
DIAG_ENTRY = float(hex_stiffness()[0, 0])


def entry(mode_a, comp_a, mode_b, comp_b):
    return float(MODES[3 * mode_a + comp_a, 3 * mode_b + comp_b])


NORMAL = ((4, 0), (2, 1), (1, 2))
SHEAR = (((2, 0), (4, 1)), ((1, 0), (4, 2)), ((1, 1), (2, 2)))
TWIST = ((3, 0), (5, 1), (6, 2))
BEND = (((3, 1), (5, 0)), ((3, 2), (6, 0)), ((5, 2), (6, 1)))
WARP = ((7, 0), (7, 1), (7, 2))
NORMAL_ON = entry(4, 0, 4, 0)
NORMAL_OFF = entry(4, 0, 2, 1)
SHEAR_ON = entry(2, 0, 4, 1)
TWIST_ON = entry(3, 0, 3, 0)
TWIST_OFF = entry(3, 0, 5, 1)
BEND_ON = entry(3, 1, 3, 1)
BEND_OFF = entry(3, 1, 5, 0)
WARP_ON = entry(7, 0, 7, 0)


def smoother_factors():
    sigma = (1 + LOWER_RATIO) / (1 - LOWER_RATIO)
    factor = 1 / sigma
    residual = np.array([1.0, 0.0, 0.0, 0.0])
    update = np.array([1.0, 0.0, 0.0, 0.0])
    total = np.zeros(4)
    for sweep in range(4):
        total = total + update
        if sweep < 3:
            residual = residual - np.concatenate([[0.0], update[:3]])
            factor_next = 1 / (2 * sigma - factor)
            update = factor_next * factor * update + 2 * factor_next * sigma * residual
            factor = factor_next
    return [float(value) for value in total]


def iota(shape, axis):
    return lax.broadcasted_iota(jnp.int32, shape, axis)


def gauss(offsets):
    return jnp.exp(-((offsets.astype(F32) / RADIUS) ** 2))


def gauss_table(count):
    return gauss(iota((count, count), 0) - iota((count, count), 1))


def shifts(shape, rows_x):
    inner = {}
    for axis, count in ((0, shape[0]), (1, rows_x)):
        index = iota(shape, axis) % count
        inner[axis] = (index < count - 1, index > 0)

    def above(value, axis):
        moved = pltpu.roll(value, shape[axis] - 1, axis)
        return jnp.where(inner[axis][0], moved, 0.0)

    def below(value, axis):
        moved = pltpu.roll(value, 1, axis)
        return jnp.where(inner[axis][1], moved, 0.0)

    return above, below


def row_modes(values, above):
    modes = {}
    for comp, value in enumerate(values):
        beside = above(value, 1)
        for bit, part in ((0, value + beside), (2, beside - value)):
            ahead = above(part, 0)
            modes[bit, comp] = part + ahead
            modes[bit + 4, comp] = ahead - part
    return modes


def element_modes(low, high):
    modes = {}
    for (bits, comp), value in low.items():
        other = high[bits, comp]
        if bits:
            modes[bits, comp] = value + other
        modes[bits + 1, comp] = other - value
    return modes


def element_forces(modes, scale):
    forces = {}
    total = modes[NORMAL[0]] + modes[NORMAL[1]] + modes[NORMAL[2]]
    shared = (scale * NORMAL_OFF) * total
    own = scale * (NORMAL_ON - NORMAL_OFF)
    for key in NORMAL:
        forces[key] = shared + own * modes[key]
    shear = scale * SHEAR_ON
    for key_a, key_b in SHEAR:
        forces[key_a] = forces[key_b] = shear * (modes[key_a] + modes[key_b])
    total = modes[TWIST[0]] + modes[TWIST[1]] + modes[TWIST[2]]
    shared = (scale * TWIST_OFF) * total
    own = scale * (TWIST_ON - TWIST_OFF)
    for key in TWIST:
        forces[key] = shared + own * modes[key]
    bend_on = scale * BEND_ON
    bend_off = scale * BEND_OFF
    for key_a, key_b in BEND:
        forces[key_a] = bend_on * modes[key_a] + bend_off * modes[key_b]
        forces[key_b] = bend_on * modes[key_b] + bend_off * modes[key_a]
    warp = scale * WARP_ON
    for key in WARP:
        forces[key] = warp * modes[key]
    return forces


def element_energy(modes):
    total = modes[NORMAL[0]] + modes[NORMAL[1]] + modes[NORMAL[2]]
    squares = sum(modes[key] * modes[key] for key in NORMAL)
    energy = NORMAL_OFF * (total * total) + (NORMAL_ON - NORMAL_OFF) * squares
    shear = 0.0
    for key_a, key_b in SHEAR:
        both = modes[key_a] + modes[key_b]
        shear = shear + both * both
    energy = energy + SHEAR_ON * shear
    total = modes[TWIST[0]] + modes[TWIST[1]] + modes[TWIST[2]]
    squares = sum(modes[key] * modes[key] for key in TWIST)
    energy = energy + TWIST_OFF * (total * total) + (TWIST_ON - TWIST_OFF) * squares
    squares = sum(modes[key] * modes[key] for pair in BEND for key in pair)
    crossed = sum(modes[key_a] * modes[key_b] for key_a, key_b in BEND)
    energy = energy + BEND_ON * squares + (2 * BEND_OFF) * crossed
    squares = sum(modes[key] * modes[key] for key in WARP)
    return energy + WARP_ON * squares


ROW_KEYS = [(bits, comp) for comp in range(3) for bits in (0, 2, 4, 6)]


def split_forces(forces):
    here, there = {}, {}
    for bits, comp in ROW_KEYS:
        change = forces[bits + 1, comp]
        if bits:
            common = forces[bits, comp]
            here[bits, comp] = common - change
            there[bits, comp] = common + change
        else:
            here[bits, comp] = -change
            there[bits, comp] = change
    return here, there


def node_forces(modes, below):
    values = []
    for comp in range(3):
        parts = []
        for bit in (0, 2):
            common, change = modes[bit, comp], modes[bit + 4, comp]
            parts.append((common - change) + below(common + change, 0))
        values.append((parts[0] - parts[1]) + below(parts[0] + parts[1], 1))
    return values


def apply_rows(first, last, load_row, scale_row, emit, above, below, carry=None):
    def advance(index, low, pending):
        high = row_modes(load_row(index + 1), above)
        forces = element_forces(element_modes(low, high), scale_row(index))
        here, there = split_forces(forces)
        return high, {key: pending[key] + here[key] for key in ROW_KEYS}, there

    low = row_modes(load_row(first), above)
    zero = {key: jnp.zeros_like(low[key]) for key in ROW_KEYS}
    low, _, pending = advance(first, low, zero)

    for index in range(first + 1, last):
        low, modes, pending = advance(index, low, pending)
        carry = emit(index, node_forces(modes, below), carry)
    return carry


def dot(left, right, turned=False):
    dims = (((1,), (1 if turned else 0,)), ((), ()))

    def halves(value):
        high = value.astype(jnp.bfloat16)
        return high, (value - high.astype(F32)).astype(jnp.bfloat16)

    def product(a, b):
        return lax.dot_general(a, b, dims, preferred_element_type=F32)

    left_high, left_low = halves(left)
    right_high, right_low = halves(right)
    return product(left_high, right_high) + (
        product(left_high, right_low) + product(left_low, right_high)
    )


def swap_blocks(values, block):
    values = list(values)
    lanes = values[0].shape[1]
    place = iota(values[0].shape, 1) // block
    bit = 1
    while bit < len(values):
        lower = (place & bit) == 0
        for index in range(len(values)):
            if not index & bit:
                low, high = values[index], values[index + bit]
                values[index] = jnp.where(lower, low, pltpu.roll(high, bit * block, 1))
                values[index + bit] = jnp.where(
                    lower, pltpu.roll(low, lanes - bit * block, 1), high
                )
        bit *= 2
    return values


def depth_table(depth, inner):
    shape = (depth * inner, depth * inner)
    to, source = iota(shape, 0), iota(shape, 1)
    return jnp.where(to % inner == source % inner, gauss(to // inner - source // inner), 0.0)


def call(body, outs, *args, scratch=(), name=None, flops=0, space=pltpu.VMEM):
    return pl.pallas_call(
        body,
        out_shape=outs,
        in_specs=[pl.BlockSpec(memory_space=space)] * len(args),
        out_specs=jax.tree.map(lambda _: pl.BlockSpec(memory_space=pltpu.VMEM), outs),
        scratch_shapes=list(scratch),
        compiler_params=pltpu.CompilerParams(vmem_limit_bytes=VMEM_LIMIT),
        cost_estimate=pl.CostEstimate(flops=flops, bytes_accessed=1 << 20, transcendentals=0),
        name=name,
    )(*args)


def exchange(message, axes):
    rows = message.shape[0]
    return lax.all_to_all(
        message.reshape(rows, 1, message.shape[1]), axes, split_axis=0, concat_axis=0, tiled=True
    ).reshape(message.shape)


def shards(start_disp, density, design, support, load_nodes, load_forces):
    slabs = lax.axis_size("slab")
    parts = lax.axis_size("load")
    loads, comps, layers, rows_x, cols_y = start_disp.shape
    points = load_nodes.shape[1]
    depth = slabs * layers
    strip = cols_y // slabs
    span = strip + HALO
    width = loads * rows_x
    half = rows_x // slabs
    plane = (depth, width)
    in_rows = (comps + 1) * span + 2 * half
    sum_rows = 3 + 2 * half
    numer_rows = half + 1
    out_rows = comps * strip + 1
    block = lambda count: jax.ShapeDtypeStruct((count, span) + plane, F32)
    flat = lambda rows: jax.ShapeDtypeStruct((rows, width), F32)
    smoother = smoother_factors()

    def pack_body(
        disp_ref, dens_ref, design_ref, support_ref, out_ref,
        stage_ref, dens_in, design_in, support_in, pad_ref, sems,
    ):
        copies = [
            pltpu.make_async_copy(dens_ref.at[0], dens_in, sems.at[0]),
            pltpu.make_async_copy(design_ref.at[0], design_in, sems.at[1]),
            pltpu.make_async_copy(support_ref.at[0], support_in, sems.at[2]),
        ]
        for load in range(loads):
            copies.append(
                pltpu.make_async_copy(
                    disp_ref.at[load, :, 0],
                    stage_ref.at[:, load * rows_x : (load + 1) * rows_x],
                    sems.at[3 + load],
                )
            )
        for copy in copies:
            copy.start()
        cube_side = iota((1, width), 1) < rows_x
        for field in range(comps + 1):
            fill = jnp.zeros((1, width), F32) if field < comps else jnp.where(cube_side, -1.0, 1.0)
            pad_ref[field, 0:HALO_LOW] = jnp.broadcast_to(fill, (HALO_LOW, width))
            pad_ref[field, HALO_LOW + cols_y : HALO + cols_y] = jnp.broadcast_to(
                fill, (HALO_HIGH, width)
            )
        for copy in copies[:3]:
            copy.wait()
        spread = dot(gauss_table(rows_x), dens_in[...])
        solid = design_in[...].astype(F32) * dens_in[...]
        both = jnp.concatenate([solid * solid * solid, support_in[...].astype(F32)], 0)
        pad_ref[comps, HALO_LOW : HALO_LOW + cols_y] = both.T
        for copy in copies[3:]:
            copy.wait()
        for comp in range(comps):
            pad_ref[comp, HALO_LOW : HALO_LOW + cols_y] = stage_ref[comp].T
        for target in range(slabs):
            base = target * in_rows
            for field in range(comps + 1):
                out_ref[base + field * span : base + (field + 1) * span] = pad_ref[
                    field, target * strip : target * strip + span
                ]
            rows = slice(target * half, (target + 1) * half)
            base = base + (comps + 1) * span
            out_ref[base : base + half] = spread[rows]
            out_ref[base + half : base + 2 * half] = design_in[rows].astype(F32)

    message = call(
        pack_body,
        flat(slabs * in_rows),
        *(
            pltpu.with_memory_space_constraint(value, pltpu.HBM)
            for value in (start_disp, density, design, support)
        ),
        scratch=[
            pltpu.VMEM((comps, width, cols_y), F32),
            pltpu.VMEM((rows_x, cols_y), F32),
            pltpu.VMEM((rows_x, cols_y), jnp.int32),
            pltpu.VMEM((rows_x, cols_y), jnp.int32),
            pltpu.VMEM((comps + 1, cols_y + 2 * 8, width), F32),
            pltpu.SemaphoreType.DMA((3 + loads,)),
        ],
        name="pack",
        space=pltpu.HBM,
    )
    received = exchange(message, "slab")

    cells = -(-span * depth // 16) * 16
    chunk = min(256, points)

    def loads_body(nodes_ref, forces_ref, out_ref):
        first = lax.axis_index("slab") * strip - HALO_LOW
        out_ref[...] = jnp.zeros_like(out_ref)
        for load in range(loads):
            for start in range(0, points, chunk):
                part = slice(start, start + chunk)
                node = nodes_ref[load : load + 1, part]
                row = node % cols_y - first
                lane = load * rows_x + (node // cols_y) % rows_x
                layer = node // (cols_y * rows_x)
                cell = jnp.where((row >= 0) & (row < span), row * depth + layer, -1)
                hit = iota((cells, chunk), 0) == cell
                spot = (iota((width, chunk), 0) == lane).astype(F32).astype(jnp.bfloat16)
                for comp in range(comps):
                    rest = forces_ref[load, comp : comp + 1, part]
                    for piece in range(3):
                        rounded = rest.astype(jnp.bfloat16).astype(F32)
                        rest = rest - rounded
                        picked = jnp.where(hit, rounded, 0.0).astype(jnp.bfloat16)
                        out_ref[comp] += lax.dot_general(
                            picked, spot, (((1,), (1,)), ((), ())), preferred_element_type=F32
                        )

    right_side = call(
        loads_body,
        jax.ShapeDtypeStruct((comps, cells, width), F32),
        load_nodes,
        load_forces,
        name="point_loads",
        flops=1 << 28,
    )

    def own_row(row):
        return (row >= HALO_LOW) & (row < HALO_LOW + strip)

    def residual_body(
        in_ref, rhs_ref, disp_ref, cube_ref, geo_ref, zero_ref, one_ref, sum_ref
    ):
        above, below = shifts(plane, rows_x)
        cube_side = iota(plane, 1) < rows_x
        for row in range(span):
            pick = lambda field: in_ref[pl.ds(field * span + row, depth, stride=in_rows), :]
            for comp in range(comps):
                disp_ref[comp, row] = pick(comp)
            both = pick(comps)
            other = pltpu.roll(both, rows_x, 1)
            cube = jnp.where(cube_side, both, other)
            cube_ref[0, row] = cube
            geo_ref[0, row] = jnp.where(
                cube < 0.0, 0.0, STIFF_VOID + (1.0 - STIFF_VOID) * cube
            )
            geo_ref[1, row] = 1.0 - jnp.where(cube_side, other, both)
        for row in range(1, span - 1):
            beside = geo_ref[0, row] + geo_ref[0, row - 1]
            beside = beside + below(beside, 0)
            beside = beside + below(beside, 1)
            free = geo_ref[1, row]
            geo_ref[2, row] = 1.0 / (free * DIAG_ENTRY * beside + (1.0 - free))

        scale_row = lambda row: geo_ref[0, row]

        def start_row(row):
            free = geo_ref[1, row]
            return [free * disp_ref[comp, row] for comp in range(comps)]

        def emit_residual(row, forces, carried):
            free, inverse = geo_ref[1, row], geo_ref[2, row]
            total = jnp.zeros(plane, F32)
            for comp, force in enumerate(forces):
                load_row = rhs_ref[comp, pl.ds(row * depth, depth), :]
                rest = free * (load_row - force) - (1.0 - free) * disp_ref[comp, row]
                value = rest * inverse
                zero_ref[comp, row] = value
                total = total + value * rest
            return carried + total if own_row(row) else carried

        weight = apply_rows(
            0, span - 1, start_row, scale_row, emit_residual, above, below,
            jnp.zeros(plane, F32),
        )

        def zero_row(row):
            free = geo_ref[1, row]
            return [free * zero_ref[comp, row] for comp in range(comps)]

        def emit_one(row, forces, carried):
            free, inverse = geo_ref[1, row], geo_ref[2, row]
            total = jnp.zeros(plane, F32)
            for comp, force in enumerate(forces):
                value = zero_ref[comp, row]
                applied = free * force + (1.0 - free) * value
                one_ref[comp, row] = applied * inverse
                total = total + value * applied
            return carried + total if own_row(row) else carried

        curve = apply_rows(
            1, span - 2, zero_row, scale_row, emit_one, above, below, jnp.zeros(plane, F32)
        )

        def gather(offset):
            offset = offset + (comps + 1) * span
            return jnp.concatenate(
                [
                    in_ref[layer * in_rows + offset : layer * in_rows + offset + half]
                    for layer in range(depth)
                ],
                0,
            )

        table_z = depth_table(depth, half)
        table_y = gauss_table(cols_y)
        mask = gather(half)
        filtered = dot(table_z, dot(gather(0), table_y))
        share = dot(table_z, dot(mask / filtered, table_y))
        share = swap_blocks(
            [share[layer * half : (layer + 1) * half] for layer in range(depth)], strip
        )
        down = lambda value: jnp.sum(value, 0, keepdims=True)
        sums = [down(curve), down(weight), down(mask)]
        for target in range(slabs):
            base = target * sum_rows
            for index, value in enumerate(sums):
                sum_ref[base + index : base + index + 1] = value
            sum_ref[base + 3 : base + 3 + half] = share[target]
            sum_ref[base + 3 + half : base + sum_rows] = filtered[
                target * half : (target + 1) * half
            ]

    disp, cube, geometry, zeroth, first, sums = call(
        residual_body,
        (
            block(comps),
            block(1),
            block(3),
            block(comps),
            block(comps),
            flat(slabs * sum_rows),
        ),
        received,
        right_side,
        name="residual",
        flops=1 << 26,
    )
    all_sums = exchange(sums, "slab")

    def powers_body(geo_ref, one_ref, two_ref, three_ref):
        above, below = shifts(plane, rows_x)
        scale_row = lambda row: geo_ref[0, row]
        for source, target, edge in ((one_ref, two_ref, 2), (two_ref, three_ref, 3)):

            def load_row(row):
                free = geo_ref[1, row]
                return [free * source[comp, row] for comp in range(comps)]

            def emit(row, forces, carried):
                free, inverse = geo_ref[1, row], geo_ref[2, row]
                for comp, force in enumerate(forces):
                    target[comp, row] = (
                        free * force + (1.0 - free) * source[comp, row]
                    ) * inverse
                return carried

            apply_rows(
                edge, span - 1 - edge, load_row, scale_row, emit, above, below,
                jnp.zeros((1, 1), F32),
            )

    second, third = call(
        powers_body,
        (block(comps), block(comps)),
        geometry,
        first,
        name="powers",
        flops=1 << 26,
    )

    def energy_body(
        sums_ref, disp_ref, cube_ref, geo_ref, zero_ref, one_ref, two_ref, three_ref,
        disp_out_ref, numer_ref, count_ref, weak_ref,
    ):
        above, below = shifts(plane, rows_x)
        gather = lambda index: sum(
            sums_ref[layer * sum_rows + index : layer * sum_rows + index + 1]
            for layer in range(slabs)
        )
        curve, weight, count = gather(0), gather(1), gather(2)
        across = lambda value: jnp.sum(value, 1, keepdims=True)
        count_ref[...] = jnp.broadcast_to(across(count), (8, width))
        owner = iota((1, width), 1) // rows_x
        inverse = jnp.zeros((1, width), F32)
        for load in range(loads):
            mine = owner == load
            upper = UPPER_FACTOR * (
                across(jnp.where(mine, curve, 0.0)) / across(jnp.where(mine, weight, 0.0))
            )
            inverse = jnp.where(mine, 1.0 / (0.5 * (upper + LOWER_RATIO * upper)), inverse)
        inverse = jnp.broadcast_to(inverse, plane)
        lower = None
        for row in range(HALO_LOW, HALO_LOW + strip + 1):
            free = geo_ref[1, row]
            values = []
            for comp in range(comps):
                value = smoother[3] * three_ref[comp, row]
                value = smoother[2] * two_ref[comp, row] + inverse * value
                value = smoother[1] * one_ref[comp, row] + inverse * value
                value = smoother[0] * zero_ref[comp, row] + inverse * value
                value = disp_ref[comp, row] + inverse * value
                if row < HALO_LOW + strip:
                    place = comp * strip + row - HALO_LOW
                    disp_out_ref[pl.ds(place, depth, stride=out_rows), :] = value
                values.append(free * value)
            modes = row_modes(values, above)
            if lower is not None:
                weak_ref[pl.ds(row - 1 - HALO_LOW, depth, stride=strip), :] = (
                    (3.0 * (1.0 - STIFF_VOID))
                    * cube_ref[0, row - 1]
                    * element_energy(element_modes(lower, modes))
                )
            lower = modes
        disp_out_ref[pl.ds(out_rows - 1, depth, stride=out_rows), :] = jnp.zeros(plane, F32)
        shape = (rows_x, width)
        table_x = gauss(iota(shape, 0) - iota(shape, 1) % rows_x)
        across_x = dot(table_x, weak_ref[...], turned=True)
        smooth = dot(across_x, depth_table(depth, strip))
        weighted = jnp.zeros((1, width), F32)
        for source in range(slabs):
            base = source * sum_rows + 3
            weighted = weighted + jnp.sum(
                across_x[source * half : (source + 1) * half] * sums_ref[base : base + half],
                0,
                keepdims=True,
            )
        pieces = swap_blocks(
            [smooth[index * half : (index + 1) * half] for index in range(slabs)], strip
        )
        for layer in range(depth):
            for part in range(parts):
                base = (part * slabs + layer) * numer_rows
                numer_ref[base : base + half] = pieces[layer]
                numer_ref[base + half : base + numer_rows] = weighted

    disp_message, numer_message, count = call(
        energy_body,
        (flat(slabs * out_rows), flat(parts * slabs * numer_rows), flat(8)),
        all_sums,
        disp,
        cube,
        geometry,
        zeroth,
        first,
        second,
        third,
        scratch=[pltpu.VMEM((strip * depth, width), F32)],
        name="energy",
        flops=1 << 24,
    )
    numer_pieces = exchange(numer_message, ("load", "slab"))

    def trial_body(
        numer_ref, dens_ref, sums_ref, design_ref, count_ref, disp_ref, trial_ref, out_ref,
        plane_ref, filtered_ref,
    ):
        weighted = jnp.zeros((1, width), F32)
        totals = []
        for source in range(slabs):
            total = jnp.zeros((half, width), F32)
            for part in range(parts):
                base = (part * slabs + source) * numer_rows
                total = total + numer_ref[base : base + half]
                weighted = weighted + numer_ref[base + half : base + numer_rows]
            totals.append(total)
            base = source * sum_rows + 3 + half
            filtered_ref[source * half : (source + 1) * half] = sums_ref[base : base + half]
        for index, value in enumerate(swap_blocks(totals, strip)):
            plane_ref[index * half : (index + 1) * half] = value
        mean = jnp.sum(weighted, 1, keepdims=True) / count_ref[0:1] + EPSILON
        numer = dot(plane_ref[...], gauss_table(cols_y))
        mask = design_ref[0].astype(F32)
        dens = dens_ref[0]
        ratio = mask * (numer / filtered_ref[...]) / mean
        trial = jnp.clip(dens * jnp.sqrt(ratio), dens - MOVE_LIMIT, dens + MOVE_LIMIT)
        trial_ref[...] = trial
        out_ref[...] = disp_ref[...]
        volume = jnp.sum(mask * trial, 0, keepdims=True)
        for target in range(slabs):
            base = (target + 1) * out_rows - 1
            out_ref[base : base + 1] = volume

    trial, out_message = call(
        trial_body,
        (flat(rows_x), flat(slabs * out_rows)),
        numer_pieces,
        density,
        all_sums,
        design,
        count,
        disp_message,
        scratch=[pltpu.VMEM((rows_x, cols_y), F32)] * 2,
        name="trial",
    )
    out_pieces = exchange(out_message, "slab")

    def final_body(pieces_ref, trial_ref, design_ref, count_ref, disp_ref, dens_ref, whole_ref):
        volume = jnp.zeros((1, width), F32)
        for source in range(slabs):
            base = (source + 1) * out_rows
            volume = volume + pieces_ref[base - 1 : base]
            for comp in range(comps):
                base = source * out_rows + comp * strip
                whole_ref[comp, source * strip : (source + 1) * strip] = pieces_ref[
                    base : base + strip
                ]
        volume = jnp.sum(volume, 1, keepdims=True)
        scale = VOLUME_TARGET / (volume / count_ref[0:1] + EPSILON)
        mask = design_ref[0].astype(F32)
        dens_ref[0] = mask * jnp.minimum(scale * trial_ref[...], 1.0)
        for comp in range(comps):
            turned = whole_ref[comp].T
            for load in range(loads):
                disp_ref[load, comp, 0] = turned[load * rows_x : (load + 1) * rows_x]

    return call(
        final_body,
        (
            jax.ShapeDtypeStruct(start_disp.shape, F32),
            jax.ShapeDtypeStruct(density.shape, F32),
        ),
        out_pieces,
        trial,
        design,
        count,
        scratch=[pltpu.VMEM((comps, cols_y, width), F32)],
        name="final",
    )


def solution(mesh):
    return jax.shard_map(
        shards,
        mesh=mesh,
        in_specs=(
            P("load", None, "slab", None, None),
            P("slab", None, None),
            P("slab", None, None),
            P("slab", None, None),
            P("load", None),
            P("load", None, None),
        ),
        out_specs=(P("load", None, "slab", None, None), P("slab", None, None)),
        check_vma=False,
    )
```

```python
import functools

import jax
import jax.numpy as jnp
import numpy as np
from jax import lax
from jax.experimental import pallas as pl
from jax.experimental.pallas import tpu as pltpu
from jax.sharding import PartitionSpec as P

RADIUS = 2
POISSON = 0.3
STIFF_VOID = 0.001
UPPER_FACTOR = 1.2
LOWER_RATIO = 0.1
MOVE_LIMIT = 0.2
VOLUME_TARGET = 0.5
EPSILON = 1e-06
F32 = jnp.float32

HALO_LOW = 4
HALO_HIGH = 5
HALO = HALO_LOW + HALO_HIGH
VMEM_LIMIT = 24 * 1024 * 1024


def hex_stiffness():
    lame_first = POISSON / ((1 + POISSON) * (1 - 2 * POISSON))
    lame_shear = 1 / (2 * (1 + POISSON))
    elastic = np.zeros((6, 6))
    elastic[:3, :3] = lame_first
    for axis_a in range(3):
        elastic[axis_a, axis_a] += 2 * lame_shear
        elastic[3 + axis_a, 3 + axis_a] = lame_shear
    shear_pairs = ((0, 1), (1, 2), (0, 2))
    gauss_point = 1 / np.sqrt(3)
    matrix = np.zeros((24, 24))
    for quad_index in range(8):
        quad_coords = [
            gauss_point * (2 * (quad_index >> 2 - axis_a & 1) - 1) for axis_a in range(3)
        ]
        shape_grads = np.zeros((8, 3))
        for corner in range(8):
            corner_signs = [2 * (corner >> 2 - axis_a & 1) - 1 for axis_a in range(3)]
            for axis_a in range(3):
                deriv_value = float(corner_signs[axis_a])
                for axis_b in range(3):
                    if axis_b != axis_a:
                        deriv_value *= (1 + corner_signs[axis_b] * quad_coords[axis_b]) / 2
                shape_grads[corner, axis_a] = deriv_value
        strain = np.zeros((6, 24))
        for corner in range(8):
            for axis_a in range(3):
                strain[axis_a, 3 * corner + axis_a] = shape_grads[corner, axis_a]
            for pair_index, shear_pair in enumerate(shear_pairs):
                strain[3 + pair_index, 3 * corner + shear_pair[0]] = shape_grads[
                    corner, shear_pair[1]
                ]
                strain[3 + pair_index, 3 * corner + shear_pair[1]] = shape_grads[
                    corner, shear_pair[0]
                ]
        matrix += strain.T @ elastic @ strain / 8
    return matrix.astype(np.float32)


def mode_stiffness():
    signs = np.zeros((8, 8))
    for mode in range(8):
        for corner in range(8):
            flips = bin(mode & ~corner & 7).count("1")
            signs[mode, corner] = -1.0 if flips & 1 else 1.0
    spread = np.kron(signs, np.eye(3))
    return spread @ hex_stiffness().astype(np.float64) @ spread.T / 64


MODES = mode_stiffness()
DIAG_ENTRY = float(hex_stiffness()[0, 0])


def entry(mode_a, comp_a, mode_b, comp_b):
    return float(MODES[3 * mode_a + comp_a, 3 * mode_b + comp_b])


NORMAL = ((4, 0), (2, 1), (1, 2))
SHEAR = (((2, 0), (4, 1)), ((1, 0), (4, 2)), ((1, 1), (2, 2)))
TWIST = ((3, 0), (5, 1), (6, 2))
BEND = (((3, 1), (5, 0)), ((3, 2), (6, 0)), ((5, 2), (6, 1)))
WARP = ((7, 0), (7, 1), (7, 2))
NORMAL_ON = entry(4, 0, 4, 0)
NORMAL_OFF = entry(4, 0, 2, 1)
SHEAR_ON = entry(2, 0, 4, 1)
TWIST_ON = entry(3, 0, 3, 0)
TWIST_OFF = entry(3, 0, 5, 1)
BEND_ON = entry(3, 1, 3, 1)
BEND_OFF = entry(3, 1, 5, 0)
WARP_ON = entry(7, 0, 7, 0)


def smoother_factors():
    sigma = (1 + LOWER_RATIO) / (1 - LOWER_RATIO)
    factor = 1 / sigma
    residual = np.array([1.0, 0.0, 0.0, 0.0])
    update = np.array([1.0, 0.0, 0.0, 0.0])
    total = np.zeros(4)
    for sweep in range(4):
        total = total + update
        if sweep < 3:
            residual = residual - np.concatenate([[0.0], update[:3]])
            factor_next = 1 / (2 * sigma - factor)
            update = factor_next * factor * update + 2 * factor_next * sigma * residual
            factor = factor_next
    return [float(value) for value in total]


def iota(shape, axis):
    return lax.broadcasted_iota(jnp.int32, shape, axis)


def gauss(offsets):
    return jnp.exp(-((offsets.astype(F32) / RADIUS) ** 2))


def gauss_table(count):
    return gauss(iota((count, count), 0) - iota((count, count), 1))


def shifts(shape, rows_x):
    inner = {}
    for axis, count in ((0, shape[0]), (1, rows_x)):
        index = iota(shape, axis) % count
        inner[axis] = (index < count - 1, index > 0)

    def above(value, axis):
        moved = pltpu.roll(value, shape[axis] - 1, axis)
        return jnp.where(inner[axis][0], moved, 0.0)

    def below(value, axis):
        moved = pltpu.roll(value, 1, axis)
        return jnp.where(inner[axis][1], moved, 0.0)

    return above, below


def row_modes(values, above):
    modes = {}
    for comp, value in enumerate(values):
        beside = above(value, 1)
        for bit, part in ((0, value + beside), (2, beside - value)):
            ahead = above(part, 0)
            modes[bit, comp] = part + ahead
            modes[bit + 4, comp] = ahead - part
    return modes


def element_modes(low, high):
    modes = {}
    for (bits, comp), value in low.items():
        other = high[bits, comp]
        if bits:
            modes[bits, comp] = value + other
        modes[bits + 1, comp] = other - value
    return modes


def element_forces(modes, scale):
    forces = {}
    total = modes[NORMAL[0]] + modes[NORMAL[1]] + modes[NORMAL[2]]
    shared = (scale * NORMAL_OFF) * total
    own = scale * (NORMAL_ON - NORMAL_OFF)
    for key in NORMAL:
        forces[key] = shared + own * modes[key]
    shear = scale * SHEAR_ON
    for key_a, key_b in SHEAR:
        forces[key_a] = forces[key_b] = shear * (modes[key_a] + modes[key_b])
    total = modes[TWIST[0]] + modes[TWIST[1]] + modes[TWIST[2]]
    shared = (scale * TWIST_OFF) * total
    own = scale * (TWIST_ON - TWIST_OFF)
    for key in TWIST:
        forces[key] = shared + own * modes[key]
    bend_on = scale * BEND_ON
    bend_off = scale * BEND_OFF
    for key_a, key_b in BEND:
        forces[key_a] = bend_on * modes[key_a] + bend_off * modes[key_b]
        forces[key_b] = bend_on * modes[key_b] + bend_off * modes[key_a]
    warp = scale * WARP_ON
    for key in WARP:
        forces[key] = warp * modes[key]
    return forces


def element_energy(modes):
    total = modes[NORMAL[0]] + modes[NORMAL[1]] + modes[NORMAL[2]]
    squares = sum(modes[key] * modes[key] for key in NORMAL)
    energy = NORMAL_OFF * (total * total) + (NORMAL_ON - NORMAL_OFF) * squares
    shear = 0.0
    for key_a, key_b in SHEAR:
        both = modes[key_a] + modes[key_b]
        shear = shear + both * both
    energy = energy + SHEAR_ON * shear
    total = modes[TWIST[0]] + modes[TWIST[1]] + modes[TWIST[2]]
    squares = sum(modes[key] * modes[key] for key in TWIST)
    energy = energy + TWIST_OFF * (total * total) + (TWIST_ON - TWIST_OFF) * squares
    squares = sum(modes[key] * modes[key] for pair in BEND for key in pair)
    crossed = sum(modes[key_a] * modes[key_b] for key_a, key_b in BEND)
    energy = energy + BEND_ON * squares + (2 * BEND_OFF) * crossed
    squares = sum(modes[key] * modes[key] for key in WARP)
    return energy + WARP_ON * squares


ROW_KEYS = [(bits, comp) for comp in range(3) for bits in (0, 2, 4, 6)]


def split_forces(forces):
    here, there = {}, {}
    for bits, comp in ROW_KEYS:
        change = forces[bits + 1, comp]
        if bits:
            common = forces[bits, comp]
            here[bits, comp] = common - change
            there[bits, comp] = common + change
        else:
            here[bits, comp] = -change
            there[bits, comp] = change
    return here, there


def node_forces(modes, below):
    values = []
    for comp in range(3):
        parts = []
        for bit in (0, 2):
            common, change = modes[bit, comp], modes[bit + 4, comp]
            parts.append((common - change) + below(common + change, 0))
        values.append((parts[0] - parts[1]) + below(parts[0] + parts[1], 1))
    return values


def apply_rows(first, last, load_row, scale_row, emit, above, below, carry=None):
    def advance(index, low, pending):
        high = row_modes(load_row(index + 1), above)
        forces = element_forces(element_modes(low, high), scale_row(index))
        here, there = split_forces(forces)
        return high, {key: pending[key] + here[key] for key in ROW_KEYS}, there

    low = row_modes(load_row(first), above)
    zero = {key: jnp.zeros_like(low[key]) for key in ROW_KEYS}
    low, _, pending = advance(first, low, zero)

    for index in range(first + 1, last):
        low, modes, pending = advance(index, low, pending)
        carry = emit(index, node_forces(modes, below), carry)
    return carry


def dot(left, right, turned=False):
    dims = (((1,), (1 if turned else 0,)), ((), ()))

    def halves(value):
        high = value.astype(jnp.bfloat16)
        return high, (value - high.astype(F32)).astype(jnp.bfloat16)

    def product(a, b):
        return lax.dot_general(a, b, dims, preferred_element_type=F32)

    left_high, left_low = halves(left)
    right_high, right_low = halves(right)
    return product(left_high, right_high) + (
        product(left_high, right_low) + product(left_low, right_high)
    )


def swap_blocks(values, block):
    values = list(values)
    lanes = values[0].shape[1]
    place = iota(values[0].shape, 1) // block
    bit = 1
    while bit < len(values):
        lower = (place & bit) == 0
        for index in range(len(values)):
            if not index & bit:
                low, high = values[index], values[index + bit]
                values[index] = jnp.where(lower, low, pltpu.roll(high, bit * block, 1))
                values[index + bit] = jnp.where(
                    lower, pltpu.roll(low, lanes - bit * block, 1), high
                )
        bit *= 2
    return values


def depth_table(depth, inner):
    shape = (depth * inner, depth * inner)
    to, source = iota(shape, 0), iota(shape, 1)
    return jnp.where(to % inner == source % inner, gauss(to // inner - source // inner), 0.0)


def call(body, outs, *args, scratch=(), name=None, flops=0, space=pltpu.VMEM, aliases=None):
    return pl.pallas_call(
        body,
        out_shape=outs,
        in_specs=[pl.BlockSpec(memory_space=space)] * len(args),
        out_specs=jax.tree.map(lambda _: pl.BlockSpec(memory_space=pltpu.VMEM), outs),
        scratch_shapes=list(scratch),
        compiler_params=pltpu.CompilerParams(vmem_limit_bytes=VMEM_LIMIT),
        cost_estimate=pl.CostEstimate(flops=flops, bytes_accessed=1 << 20, transcendentals=0),
        input_output_aliases=aliases or {},
        name=name,
    )(*args)


def exchange(message, axes):
    rows = message.shape[0]
    return lax.all_to_all(
        message.reshape(rows, 1, message.shape[1]), axes, split_axis=0, concat_axis=0, tiled=True
    ).reshape(message.shape)


def shards(start_disp, density, design, support, load_nodes, load_forces):
    slabs = lax.axis_size("slab")
    parts = lax.axis_size("load")
    loads, comps, layers, rows_x, cols_y = start_disp.shape
    points = load_nodes.shape[1]
    depth = slabs * layers
    strip = cols_y // slabs
    span = strip + HALO
    width = loads * rows_x
    half = rows_x // slabs
    plane = (depth, width)
    in_rows = (comps + 1) * span + 2 * half
    sum_rows = 3 + 2 * half
    numer_rows = half + 1
    out_rows = comps * strip + 1
    block = lambda count: jax.ShapeDtypeStruct((count, span) + plane, F32)
    flat = lambda rows: jax.ShapeDtypeStruct((rows, width), F32)
    smoother = smoother_factors()

    def pack_body(
        disp_ref, dens_ref, design_ref, support_ref, out_ref,
        stage_ref, dens_in, design_in, support_in, pad_ref, sems,
    ):
        copies = [
            pltpu.make_async_copy(dens_ref.at[0], dens_in, sems.at[0]),
            pltpu.make_async_copy(design_ref.at[0], design_in, sems.at[1]),
            pltpu.make_async_copy(support_ref.at[0], support_in, sems.at[2]),
        ]
        for load in range(loads):
            copies.append(
                pltpu.make_async_copy(
                    disp_ref.at[load, :, 0],
                    stage_ref.at[:, load * rows_x : (load + 1) * rows_x],
                    sems.at[3 + load],
                )
            )
        for copy in copies:
            copy.start()
        cube_side = iota((1, width), 1) < rows_x
        for field in range(comps + 1):
            fill = jnp.zeros((1, width), F32) if field < comps else jnp.where(cube_side, -1.0, 1.0)
            pad_ref[field, 0:HALO_LOW] = jnp.broadcast_to(fill, (HALO_LOW, width))
            pad_ref[field, HALO_LOW + cols_y : HALO + cols_y] = jnp.broadcast_to(
                fill, (HALO_HIGH, width)
            )
        for copy in copies[:3]:
            copy.wait()
        spread = dot(gauss_table(rows_x), dens_in[...])
        solid = design_in[...].astype(F32) * dens_in[...]
        both = jnp.concatenate([solid * solid * solid, support_in[...].astype(F32)], 0)
        pad_ref[comps, HALO_LOW : HALO_LOW + cols_y] = both.T
        for copy in copies[3:]:
            copy.wait()
        for comp in range(comps):
            pad_ref[comp, HALO_LOW : HALO_LOW + cols_y] = stage_ref[comp].T
        for target in range(slabs):
            base = target * in_rows
            for field in range(comps + 1):
                out_ref[base + field * span : base + (field + 1) * span] = pad_ref[
                    field, target * strip : target * strip + span
                ]
            rows = slice(target * half, (target + 1) * half)
            base = base + (comps + 1) * span
            out_ref[base : base + half] = spread[rows]
            out_ref[base + half : base + 2 * half] = design_in[rows].astype(F32)

    message = call(
        pack_body,
        flat(slabs * in_rows),
        *(
            pltpu.with_memory_space_constraint(value, pltpu.HBM)
            for value in (start_disp, density, design, support)
        ),
        scratch=[
            pltpu.VMEM((comps, width, cols_y), F32),
            pltpu.VMEM((rows_x, cols_y), F32),
            pltpu.VMEM((rows_x, cols_y), jnp.int32),
            pltpu.VMEM((rows_x, cols_y), jnp.int32),
            pltpu.VMEM((comps + 1, cols_y + 2 * 8, width), F32),
            pltpu.SemaphoreType.DMA((3 + loads,)),
        ],
        name="pack",
        space=pltpu.HBM,
    )
    received = exchange(message, "slab")

    cells = -(-span * depth // 16) * 16
    chunk = min(256, points)

    def loads_body(nodes_ref, forces_ref, out_ref):
        first = lax.axis_index("slab") * strip - HALO_LOW
        out_ref[...] = jnp.zeros_like(out_ref)
        for load in range(loads):
            for start in range(0, points, chunk):
                part = slice(start, start + chunk)
                node = nodes_ref[load : load + 1, part]
                row = node % cols_y - first
                lane = load * rows_x + (node // cols_y) % rows_x
                layer = node // (cols_y * rows_x)
                cell = jnp.where((row >= 0) & (row < span), row * depth + layer, -1)
                hit = iota((cells, chunk), 0) == cell
                spot = (iota((width, chunk), 0) == lane).astype(F32).astype(jnp.bfloat16)
                for comp in range(comps):
                    rest = forces_ref[load, comp : comp + 1, part]
                    for piece in range(3):
                        rounded = rest.astype(jnp.bfloat16).astype(F32)
                        rest = rest - rounded
                        picked = jnp.where(hit, rounded, 0.0).astype(jnp.bfloat16)
                        out_ref[comp] += lax.dot_general(
                            picked, spot, (((1,), (1,)), ((), ())), preferred_element_type=F32
                        )

    right_side = call(
        loads_body,
        jax.ShapeDtypeStruct((comps, cells, width), F32),
        load_nodes,
        load_forces,
        name="point_loads",
        flops=1 << 28,
    )

    def own_row(row):
        return (row >= HALO_LOW) & (row < HALO_LOW + strip)

    def residual_body(
        in_ref, rhs_ref, disp_ref, cube_ref, geo_ref, zero_ref, one_ref, sum_ref
    ):
        above, below = shifts(plane, rows_x)
        def gather(offset):
            offset = offset + (comps + 1) * span
            return jnp.concatenate(
                [
                    in_ref[layer * in_rows + offset : layer * in_rows + offset + half]
                    for layer in range(depth)
                ],
                0,
            )

        table_z = depth_table(depth, half)
        table_y = gauss_table(cols_y)
        mask = gather(half)
        filtered = dot(table_z, dot(gather(0), table_y))
        share = dot(table_z, dot(mask / filtered, table_y))
        share = swap_blocks(
            [share[layer * half : (layer + 1) * half] for layer in range(depth)], strip
        )
        cube_side = iota(plane, 1) < rows_x
        for row in range(span):
            pick = lambda field: in_ref[pl.ds(field * span + row, depth, stride=in_rows), :]
            for comp in range(comps):
                disp_ref[comp, row] = pick(comp)
            both = pick(comps)
            other = pltpu.roll(both, rows_x, 1)
            cube = jnp.where(cube_side, both, other)
            cube_ref[0, row] = cube
            geo_ref[0, row] = jnp.where(
                cube < 0.0, 0.0, STIFF_VOID + (1.0 - STIFF_VOID) * cube
            )
            geo_ref[1, row] = 1.0 - jnp.where(cube_side, other, both)
        for row in range(1, span - 1):
            beside = geo_ref[0, row] + geo_ref[0, row - 1]
            beside = beside + below(beside, 0)
            beside = beside + below(beside, 1)
            free = geo_ref[1, row]
            geo_ref[2, row] = 1.0 / (free * DIAG_ENTRY * beside + (1.0 - free))

        scale_row = lambda row: geo_ref[0, row]

        def start_row(row):
            free = geo_ref[1, row]
            return [free * disp_ref[comp, row] for comp in range(comps)]

        def emit_residual(row, forces, carried):
            free, inverse = geo_ref[1, row], geo_ref[2, row]
            total = jnp.zeros(plane, F32)
            for comp, force in enumerate(forces):
                load_row = rhs_ref[comp, pl.ds(row * depth, depth), :]
                rest = free * (load_row - force) - (1.0 - free) * disp_ref[comp, row]
                value = rest * inverse
                zero_ref[comp, row] = value
                total = total + value * rest
            return carried + total if own_row(row) else carried

        weight = apply_rows(
            0, span - 1, start_row, scale_row, emit_residual, above, below,
            jnp.zeros(plane, F32),
        )

        def zero_row(row):
            free = geo_ref[1, row]
            return [free * zero_ref[comp, row] for comp in range(comps)]

        def emit_one(row, forces, carried):
            free, inverse = geo_ref[1, row], geo_ref[2, row]
            total = jnp.zeros(plane, F32)
            for comp, force in enumerate(forces):
                value = zero_ref[comp, row]
                applied = free * force + (1.0 - free) * value
                one_ref[comp, row] = applied * inverse
                total = total + value * applied
            return carried + total if own_row(row) else carried

        curve = apply_rows(
            1, span - 2, zero_row, scale_row, emit_one, above, below, jnp.zeros(plane, F32)
        )

        down = lambda value: jnp.sum(value, 0, keepdims=True)
        sums = [down(curve), down(weight), down(mask)]
        for target in range(slabs):
            base = target * sum_rows
            for index, value in enumerate(sums):
                sum_ref[base + index : base + index + 1] = value
            sum_ref[base + 3 : base + 3 + half] = share[target]
            sum_ref[base + 3 + half : base + sum_rows] = filtered[
                target * half : (target + 1) * half
            ]

    disp, cube, geometry, zeroth, first, sums = call(
        residual_body,
        (
            block(comps),
            block(1),
            block(3),
            block(comps),
            block(comps),
            flat(slabs * sum_rows),
        ),
        received,
        right_side,
        name="residual",
        flops=1 << 26,
    )
    all_sums = exchange(sums, "slab")

    def powers_body(geo_ref, one_ref, two_ref, three_ref):
        above, below = shifts(plane, rows_x)
        scale_row = lambda row: geo_ref[0, row]
        for source, target, edge in ((one_ref, two_ref, 2), (two_ref, three_ref, 3)):

            def load_row(row):
                free = geo_ref[1, row]
                return [free * source[comp, row] for comp in range(comps)]

            def emit(row, forces, carried):
                free, inverse = geo_ref[1, row], geo_ref[2, row]
                for comp, force in enumerate(forces):
                    target[comp, row] = (
                        free * force + (1.0 - free) * source[comp, row]
                    ) * inverse
                return carried

            apply_rows(
                edge, span - 1 - edge, load_row, scale_row, emit, above, below,
                jnp.zeros((1, 1), F32),
            )

    second, third = call(
        powers_body,
        (block(comps), block(comps)),
        geometry,
        first,
        name="powers",
        flops=1 << 26,
    )

    def energy_body(
        sums_ref, disp_ref, cube_ref, geo_ref, zero_ref, one_ref, two_ref, three_ref,
        disp_out_ref, numer_ref, count_ref, weak_ref,
    ):
        above, below = shifts(plane, rows_x)
        gather = lambda index: sum(
            sums_ref[layer * sum_rows + index : layer * sum_rows + index + 1]
            for layer in range(slabs)
        )
        curve, weight, count = gather(0), gather(1), gather(2)
        across = lambda value: jnp.sum(value, 1, keepdims=True)
        count_ref[...] = jnp.broadcast_to(across(count), (8, width))
        owner = iota((1, width), 1) // rows_x
        inverse = jnp.zeros((1, width), F32)
        for load in range(loads):
            mine = owner == load
            upper = UPPER_FACTOR * (
                across(jnp.where(mine, curve, 0.0)) / across(jnp.where(mine, weight, 0.0))
            )
            inverse = jnp.where(mine, 1.0 / (0.5 * (upper + LOWER_RATIO * upper)), inverse)
        inverse = jnp.broadcast_to(inverse, plane)
        lower = None
        for row in range(HALO_LOW, HALO_LOW + strip + 1):
            free = geo_ref[1, row]
            values = []
            for comp in range(comps):
                value = smoother[3] * three_ref[comp, row]
                value = smoother[2] * two_ref[comp, row] + inverse * value
                value = smoother[1] * one_ref[comp, row] + inverse * value
                value = smoother[0] * zero_ref[comp, row] + inverse * value
                value = disp_ref[comp, row] + inverse * value
                if row < HALO_LOW + strip:
                    place = comp * strip + row - HALO_LOW
                    disp_out_ref[pl.ds(place, depth, stride=out_rows), :] = value
                values.append(free * value)
            modes = row_modes(values, above)
            if lower is not None:
                weak_ref[pl.ds(row - 1 - HALO_LOW, depth, stride=strip), :] = (
                    (3.0 * (1.0 - STIFF_VOID))
                    * cube_ref[0, row - 1]
                    * element_energy(element_modes(lower, modes))
                )
            lower = modes
        disp_out_ref[pl.ds(out_rows - 1, depth, stride=out_rows), :] = jnp.zeros(plane, F32)
        shape = (rows_x, width)
        table_x = gauss(iota(shape, 0) - iota(shape, 1) % rows_x)
        weak = weak_ref[...]
        across_x = dot(table_x, weak, turned=True)
        shape = (width, width)
        table_x = gauss(iota(shape, 0) % rows_x - iota(shape, 1) % rows_x)
        smooth = dot(depth_table(depth, strip), dot(weak, table_x))
        weighted = jnp.zeros((1, width), F32)
        for source in range(slabs):
            base = source * sum_rows + 3
            weighted = weighted + jnp.sum(
                across_x[source * half : (source + 1) * half] * sums_ref[base : base + half],
                0,
                keepdims=True,
            )
        block_of = iota((half, width), 1) // rows_x
        for layer in range(depth):
            piece = smooth[layer * strip : layer * strip + half]
            for block_at in range(1, strip // half):
                rows = layer * strip + block_at * half
                piece = jnp.where(block_of == block_at, smooth[rows : rows + half], piece)
            for part in range(parts):
                base = (part * slabs + layer) * numer_rows
                numer_ref[base : base + half] = piece
                numer_ref[base + half : base + numer_rows] = weighted

    disp_message, numer_message, count = call(
        energy_body,
        (flat(slabs * out_rows), flat(parts * slabs * numer_rows), flat(8)),
        all_sums,
        disp,
        cube,
        geometry,
        zeroth,
        first,
        second,
        third,
        scratch=[pltpu.VMEM((strip * depth, width), F32)],
        name="energy",
        flops=1 << 24,
    )
    numer_pieces = exchange(numer_message, ("load", "slab"))

    def trial_body(
        numer_ref, dens_ref, sums_ref, design_ref, count_ref, disp_ref, trial_ref, out_ref,
        plane_ref, filtered_ref,
    ):
        weighted = jnp.zeros((1, width), F32)
        for source in range(slabs):
            total = jnp.zeros((half, width), F32)
            for part in range(parts):
                base = (part * slabs + source) * numer_rows
                total = total + numer_ref[base : base + half]
                weighted = weighted + numer_ref[base + half : base + numer_rows]
            base = source * sum_rows + 3 + half
            filtered_ref[source * half : (source + 1) * half] = sums_ref[base : base + half]
            plane_ref[source * half : (source + 1) * half] = total
        mean = jnp.sum(weighted, 1, keepdims=True) / count_ref[0:1] + EPSILON
        packed = plane_ref[...].T
        numer = 0.0
        for block_at in range(strip // half):
            shape = (slabs * half, cols_y)
            row = iota(shape, 0)
            table = gauss(row // half * strip + block_at * half + row % half - iota(shape, 1))
            numer = numer + dot(packed[block_at * rows_x : (block_at + 1) * rows_x], table)
        mask = design_ref[0].astype(F32)
        dens = dens_ref[0]
        ratio = mask * (numer / filtered_ref[...]) / mean
        trial = jnp.clip(dens * jnp.sqrt(ratio), dens - MOVE_LIMIT, dens + MOVE_LIMIT)
        trial_ref[...] = trial
        volume = jnp.sum(mask * trial, 0, keepdims=True)
        for target in range(slabs):
            base = (target + 1) * out_rows - 1
            out_ref[base : base + 1] = volume

    trial, out_message = call(
        trial_body,
        (flat(rows_x), flat(slabs * out_rows)),
        numer_pieces,
        density,
        all_sums,
        design,
        count,
        disp_message,
        scratch=[pltpu.VMEM((rows_x, cols_y), F32)] * 2,
        name="trial",
        aliases={5: 1},
    )
    out_pieces = exchange(out_message, "slab")

    def final_body(pieces_ref, trial_ref, design_ref, count_ref, disp_ref, dens_ref, whole_ref):
        volume = jnp.zeros((1, width), F32)
        for source in range(slabs):
            base = (source + 1) * out_rows
            volume = volume + pieces_ref[base - 1 : base]
            for comp in range(comps):
                base = source * out_rows + comp * strip
                whole_ref[comp, source * strip : (source + 1) * strip] = pieces_ref[
                    base : base + strip
                ]
        volume = jnp.sum(volume, 1, keepdims=True)
        scale = VOLUME_TARGET / (volume / count_ref[0:1] + EPSILON)
        mask = design_ref[0].astype(F32)
        dens_ref[0] = mask * jnp.minimum(scale * trial_ref[...], 1.0)
        for comp in range(comps):
            turned = whole_ref[comp].T
            for load in range(loads):
                disp_ref[load, comp, 0] = turned[load * rows_x : (load + 1) * rows_x]

    return call(
        final_body,
        (
            jax.ShapeDtypeStruct(start_disp.shape, F32),
            jax.ShapeDtypeStruct(density.shape, F32),
        ),
        out_pieces,
        trial,
        design,
        count,
        scratch=[pltpu.VMEM((comps, cols_y, width), F32)],
        name="final",
    )


def solution(mesh):
    return jax.shard_map(
        shards,
        mesh=mesh,
        in_specs=(
            P("load", None, "slab", None, None),
            P("slab", None, None),
            P("slab", None, None),
            P("slab", None, None),
            P("load", None),
            P("load", None, None),
        ),
        out_specs=(P("load", None, "slab", None, None), P("slab", None, None)),
        check_vma=False,
    )
```

```python
import functools

import jax
import jax.numpy as jnp
import numpy as np
from jax import lax
from jax.experimental import pallas as pl
from jax.experimental.pallas import tpu as pltpu
from jax.sharding import PartitionSpec as P

RADIUS = 2
POISSON = 0.3
STIFF_VOID = 0.001
UPPER_FACTOR = 1.2
LOWER_RATIO = 0.1
MOVE_LIMIT = 0.2
VOLUME_TARGET = 0.5
EPSILON = 1e-06
F32 = jnp.float32

HALO_LOW = 4
HALO_HIGH = 5
HALO = HALO_LOW + HALO_HIGH
VMEM_LIMIT = 24 * 1024 * 1024


def hex_stiffness():
    lame_first = POISSON / ((1 + POISSON) * (1 - 2 * POISSON))
    lame_shear = 1 / (2 * (1 + POISSON))
    elastic = np.zeros((6, 6))
    elastic[:3, :3] = lame_first
    for axis_a in range(3):
        elastic[axis_a, axis_a] += 2 * lame_shear
        elastic[3 + axis_a, 3 + axis_a] = lame_shear
    shear_pairs = ((0, 1), (1, 2), (0, 2))
    gauss_point = 1 / np.sqrt(3)
    matrix = np.zeros((24, 24))
    for quad_index in range(8):
        quad_coords = [
            gauss_point * (2 * (quad_index >> 2 - axis_a & 1) - 1) for axis_a in range(3)
        ]
        shape_grads = np.zeros((8, 3))
        for corner in range(8):
            corner_signs = [2 * (corner >> 2 - axis_a & 1) - 1 for axis_a in range(3)]
            for axis_a in range(3):
                deriv_value = float(corner_signs[axis_a])
                for axis_b in range(3):
                    if axis_b != axis_a:
                        deriv_value *= (1 + corner_signs[axis_b] * quad_coords[axis_b]) / 2
                shape_grads[corner, axis_a] = deriv_value
        strain = np.zeros((6, 24))
        for corner in range(8):
            for axis_a in range(3):
                strain[axis_a, 3 * corner + axis_a] = shape_grads[corner, axis_a]
            for pair_index, shear_pair in enumerate(shear_pairs):
                strain[3 + pair_index, 3 * corner + shear_pair[0]] = shape_grads[
                    corner, shear_pair[1]
                ]
                strain[3 + pair_index, 3 * corner + shear_pair[1]] = shape_grads[
                    corner, shear_pair[0]
                ]
        matrix += strain.T @ elastic @ strain / 8
    return matrix.astype(np.float32)


def mode_stiffness():
    signs = np.zeros((8, 8))
    for mode in range(8):
        for corner in range(8):
            flips = bin(mode & ~corner & 7).count("1")
            signs[mode, corner] = -1.0 if flips & 1 else 1.0
    spread = np.kron(signs, np.eye(3))
    return spread @ hex_stiffness().astype(np.float64) @ spread.T / 64


MODES = mode_stiffness()
DIAG_ENTRY = float(hex_stiffness()[0, 0])


def entry(mode_a, comp_a, mode_b, comp_b):
    return float(MODES[3 * mode_a + comp_a, 3 * mode_b + comp_b])


NORMAL = ((4, 0), (2, 1), (1, 2))
SHEAR = (((2, 0), (4, 1)), ((1, 0), (4, 2)), ((1, 1), (2, 2)))
TWIST = ((3, 0), (5, 1), (6, 2))
BEND = (((3, 1), (5, 0)), ((3, 2), (6, 0)), ((5, 2), (6, 1)))
WARP = ((7, 0), (7, 1), (7, 2))
NORMAL_ON = entry(4, 0, 4, 0)
NORMAL_OFF = entry(4, 0, 2, 1)
SHEAR_ON = entry(2, 0, 4, 1)
TWIST_ON = entry(3, 0, 3, 0)
TWIST_OFF = entry(3, 0, 5, 1)
BEND_ON = entry(3, 1, 3, 1)
BEND_OFF = entry(3, 1, 5, 0)
WARP_ON = entry(7, 0, 7, 0)


def smoother_factors():
    sigma = (1 + LOWER_RATIO) / (1 - LOWER_RATIO)
    factor = 1 / sigma
    residual = np.array([1.0, 0.0, 0.0, 0.0])
    update = np.array([1.0, 0.0, 0.0, 0.0])
    total = np.zeros(4)
    for sweep in range(4):
        total = total + update
        if sweep < 3:
            residual = residual - np.concatenate([[0.0], update[:3]])
            factor_next = 1 / (2 * sigma - factor)
            update = factor_next * factor * update + 2 * factor_next * sigma * residual
            factor = factor_next
    return [float(value) for value in total]


def iota(shape, axis):
    return lax.broadcasted_iota(jnp.int32, shape, axis)


def gauss(offsets):
    return jnp.exp(-((offsets.astype(F32) / RADIUS) ** 2))


def gauss_table(count):
    return gauss(iota((count, count), 0) - iota((count, count), 1))


def shifts(shape, rows_x, first):
    inner = {}
    for axis, start, count in ((0, first, shape[0]), (1, 0, rows_x)):
        index = (iota(shape, axis) + start) % count
        inner[axis] = (index < count - 1, index > 0)

    def above(value, axis):
        moved = pltpu.roll(value, shape[axis] - 1, axis)
        return jnp.where(inner[axis][0], moved, 0.0)

    def below(value, axis):
        moved = pltpu.roll(value, 1, axis)
        return jnp.where(inner[axis][1], moved, 0.0)

    return above, below


def row_modes(values, above):
    modes = {}
    for comp, value in enumerate(values):
        beside = above(value, 1)
        for bit, part in ((0, value + beside), (2, beside - value)):
            ahead = above(part, 0)
            modes[bit, comp] = part + ahead
            modes[bit + 4, comp] = ahead - part
    return modes


def element_modes(low, high):
    modes = {}
    for (bits, comp), value in low.items():
        other = high[bits, comp]
        if bits:
            modes[bits, comp] = value + other
        modes[bits + 1, comp] = other - value
    return modes


def element_forces(modes, scale):
    forces = {}
    total = modes[NORMAL[0]] + modes[NORMAL[1]] + modes[NORMAL[2]]
    shared = (scale * NORMAL_OFF) * total
    own = scale * (NORMAL_ON - NORMAL_OFF)
    for key in NORMAL:
        forces[key] = shared + own * modes[key]
    shear = scale * SHEAR_ON
    for key_a, key_b in SHEAR:
        forces[key_a] = forces[key_b] = shear * (modes[key_a] + modes[key_b])
    total = modes[TWIST[0]] + modes[TWIST[1]] + modes[TWIST[2]]
    shared = (scale * TWIST_OFF) * total
    own = scale * (TWIST_ON - TWIST_OFF)
    for key in TWIST:
        forces[key] = shared + own * modes[key]
    bend_on = scale * BEND_ON
    bend_off = scale * BEND_OFF
    for key_a, key_b in BEND:
        forces[key_a] = bend_on * modes[key_a] + bend_off * modes[key_b]
        forces[key_b] = bend_on * modes[key_b] + bend_off * modes[key_a]
    warp = scale * WARP_ON
    for key in WARP:
        forces[key] = warp * modes[key]
    return forces


def element_energy(modes):
    total = modes[NORMAL[0]] + modes[NORMAL[1]] + modes[NORMAL[2]]
    squares = sum(modes[key] * modes[key] for key in NORMAL)
    energy = NORMAL_OFF * (total * total) + (NORMAL_ON - NORMAL_OFF) * squares
    shear = 0.0
    for key_a, key_b in SHEAR:
        both = modes[key_a] + modes[key_b]
        shear = shear + both * both
    energy = energy + SHEAR_ON * shear
    total = modes[TWIST[0]] + modes[TWIST[1]] + modes[TWIST[2]]
    squares = sum(modes[key] * modes[key] for key in TWIST)
    energy = energy + TWIST_OFF * (total * total) + (TWIST_ON - TWIST_OFF) * squares
    squares = sum(modes[key] * modes[key] for pair in BEND for key in pair)
    crossed = sum(modes[key_a] * modes[key_b] for key_a, key_b in BEND)
    energy = energy + BEND_ON * squares + (2 * BEND_OFF) * crossed
    squares = sum(modes[key] * modes[key] for key in WARP)
    return energy + WARP_ON * squares


ROW_KEYS = [(bits, comp) for comp in range(3) for bits in (0, 2, 4, 6)]


def split_forces(forces):
    here, there = {}, {}
    for bits, comp in ROW_KEYS:
        change = forces[bits + 1, comp]
        if bits:
            common = forces[bits, comp]
            here[bits, comp] = common - change
            there[bits, comp] = common + change
        else:
            here[bits, comp] = -change
            there[bits, comp] = change
    return here, there


def node_forces(modes, below):
    values = []
    for comp in range(3):
        parts = []
        for bit in (0, 2):
            common, change = modes[bit, comp], modes[bit + 4, comp]
            parts.append((common - change) + below(common + change, 0))
        values.append((parts[0] - parts[1]) + below(parts[0] + parts[1], 1))
    return values


def apply_rows(first, last, load_row, scale_row, emit, above, below, carry=None):
    def advance(index, low, pending):
        high = row_modes(load_row(index + 1), above)
        forces = element_forces(element_modes(low, high), scale_row(index))
        here, there = split_forces(forces)
        return high, {key: pending[key] + here[key] for key in ROW_KEYS}, there

    low = row_modes(load_row(first), above)
    zero = {key: jnp.zeros_like(low[key]) for key in ROW_KEYS}
    low, _, pending = advance(first, low, zero)

    for index in range(first + 1, last):
        low, modes, pending = advance(index, low, pending)
        carry = emit(index, node_forces(modes, below), carry)
    return carry


def dot(left, right, turned=False):
    dims = (((1,), (1 if turned else 0,)), ((), ()))

    def halves(value):
        high = value.astype(jnp.bfloat16)
        return high, (value - high.astype(F32)).astype(jnp.bfloat16)

    def product(a, b):
        return lax.dot_general(a, b, dims, preferred_element_type=F32)

    left_high, left_low = halves(left)
    right_high, right_low = halves(right)
    return product(left_high, right_high) + (
        product(left_high, right_low) + product(left_low, right_high)
    )


def swap_blocks(values, block):
    values = list(values)
    lanes = values[0].shape[1]
    place = iota(values[0].shape, 1) // block
    bit = 1
    while bit < len(values):
        lower = (place & bit) == 0
        for index in range(len(values)):
            if not index & bit:
                low, high = values[index], values[index + bit]
                values[index] = jnp.where(lower, low, pltpu.roll(high, bit * block, 1))
                values[index + bit] = jnp.where(
                    lower, pltpu.roll(low, lanes - bit * block, 1), high
                )
        bit *= 2
    return values


def filter_depth(layers):
    depth = len(layers)
    if depth <= 16:
        weights = [float(np.exp(-((step / RADIUS) ** 2))) for step in range(depth)]
        return [
            sum(weights[abs(to - source)] * layers[source] for source in range(depth))
            for to in range(depth)
        ]
    rows = layers[0].shape[0]
    shape = (depth * rows, depth * rows)
    to, source = iota(shape, 0), iota(shape, 1)
    table = jnp.where(to % rows == source % rows, gauss(to // rows - source // rows), 0.0)
    mixed = dot(table, jnp.concatenate(layers, 0))
    return [mixed[layer * rows : (layer + 1) * rows] for layer in range(depth)]


def call(body, outs, *args, scratch=(), name=None, flops=0, space=pltpu.VMEM, aliases=None):
    return pl.pallas_call(
        body,
        out_shape=outs,
        in_specs=[pl.BlockSpec(memory_space=space)] * len(args),
        out_specs=jax.tree.map(lambda _: pl.BlockSpec(memory_space=pltpu.VMEM), outs),
        scratch_shapes=list(scratch),
        compiler_params=pltpu.CompilerParams(vmem_limit_bytes=VMEM_LIMIT),
        cost_estimate=pl.CostEstimate(flops=flops, bytes_accessed=1 << 20, transcendentals=0),
        input_output_aliases=aliases or {},
        name=name,
    )(*args)


def exchange(message, axes, order=None):
    rows = message.shape[0]
    return lax.all_to_all(
        message.reshape(rows, 1, message.shape[1]),
        axes,
        split_axis=0,
        concat_axis=0,
        tiled=True,
        axis_index_groups=order and [order],
    ).reshape(message.shape)


def shards(start_disp, density, design, support, load_nodes, load_forces):
    slabs = lax.axis_size("slab")
    parts = lax.axis_size("load")
    loads, comps, layers, rows_x, cols_y = start_disp.shape
    points = load_nodes.shape[1]
    depth = slabs * layers
    strip = cols_y // slabs
    span = strip + HALO
    width = loads * rows_x
    half = rows_x // slabs
    plane = (depth, width)
    in_rows = (comps + 1) * span + 2 * half
    sum_rows = 3 + 2 * half
    numer_rows = half + 1
    out_rows = comps * strip + 1
    block = lambda count: jax.ShapeDtypeStruct((count, span) + plane, F32)
    flat = lambda rows: jax.ShapeDtypeStruct((rows, width), F32)
    smoother = smoother_factors()
    ring_start = slabs // 2 - 1
    ring = [(at + ring_start) % slabs for at in range(slabs)]
    place = lambda index: (index - ring_start) % slabs

    def pack_body(
        disp_ref, dens_ref, design_ref, support_ref, out_ref,
        stage_ref, dens_in, design_in, support_in, pad_ref, sems,
    ):
        copies = [
            pltpu.make_async_copy(dens_ref.at[0], dens_in, sems.at[0]),
            pltpu.make_async_copy(design_ref.at[0], design_in, sems.at[1]),
            pltpu.make_async_copy(support_ref.at[0], support_in, sems.at[2]),
        ]
        for load in range(loads):
            copies.append(
                pltpu.make_async_copy(
                    disp_ref.at[load, :, 0],
                    stage_ref.at[:, load * rows_x : (load + 1) * rows_x],
                    sems.at[3 + load],
                )
            )
        for copy in copies:
            copy.start()
        cube_side = iota((1, width), 1) < rows_x
        for field in range(comps + 1):
            fill = jnp.zeros((1, width), F32) if field < comps else jnp.where(cube_side, -1.0, 1.0)
            pad_ref[field, 0:HALO_LOW] = jnp.broadcast_to(fill, (HALO_LOW, width))
            pad_ref[field, HALO_LOW + cols_y : HALO + cols_y] = jnp.broadcast_to(
                fill, (HALO_HIGH, width)
            )
        for copy in copies[:3]:
            copy.wait()
        spread = dot(dot(gauss_table(rows_x), dens_in[...]), gauss_table(cols_y))
        solid = design_in[...].astype(F32) * dens_in[...]
        both = jnp.concatenate([solid * solid * solid, support_in[...].astype(F32)], 0)
        pad_ref[comps, HALO_LOW : HALO_LOW + cols_y] = both.T
        for copy in copies[3:]:
            copy.wait()
        for comp in range(comps):
            pad_ref[comp, HALO_LOW : HALO_LOW + cols_y] = stage_ref[comp].T
        for target in range(slabs):
            base = place(target) * in_rows
            for field in range(comps + 1):
                out_ref[base + field * span : base + (field + 1) * span] = pad_ref[
                    field, target * strip : target * strip + span
                ]
            rows = slice(target * half, (target + 1) * half)
            base = base + (comps + 1) * span
            out_ref[base : base + half] = spread[rows]
            out_ref[base + half : base + 2 * half] = design_in[rows].astype(F32)

    message = call(
        pack_body,
        flat(slabs * in_rows),
        *(
            pltpu.with_memory_space_constraint(value, pltpu.HBM)
            for value in (start_disp, density, design, support)
        ),
        scratch=[
            pltpu.VMEM((comps, width, cols_y), F32),
            pltpu.VMEM((rows_x, cols_y), F32),
            pltpu.VMEM((rows_x, cols_y), jnp.int32),
            pltpu.VMEM((rows_x, cols_y), jnp.int32),
            pltpu.VMEM((comps + 1, cols_y + 2 * 8, width), F32),
            pltpu.SemaphoreType.DMA((3 + loads,)),
        ],
        name="pack",
        space=pltpu.HBM,
    )
    received = exchange(message, "slab", ring)

    cells = -(-span * depth // 16) * 16
    chunk = min(256, points)

    def loads_body(nodes_ref, forces_ref, out_ref):
        first = lax.axis_index("slab") * strip - HALO_LOW
        out_ref[...] = jnp.zeros_like(out_ref)
        for load in range(loads):
            for start in range(0, points, chunk):
                part = slice(start, start + chunk)
                node = nodes_ref[load : load + 1, part]
                row = node % cols_y - first
                lane = load * rows_x + (node // cols_y) % rows_x
                layer = (node // (cols_y * rows_x) + depth - ring_start) % depth
                cell = jnp.where((row >= 0) & (row < span), row * depth + layer, -1)
                hit = iota((cells, chunk), 0) == cell
                spot = (iota((width, chunk), 0) == lane).astype(F32).astype(jnp.bfloat16)
                for comp in range(comps):
                    rest = forces_ref[load, comp : comp + 1, part]
                    for piece in range(3):
                        rounded = rest.astype(jnp.bfloat16).astype(F32)
                        rest = rest - rounded
                        picked = jnp.where(hit, rounded, 0.0).astype(jnp.bfloat16)
                        out_ref[comp] += lax.dot_general(
                            picked, spot, (((1,), (1,)), ((), ())), preferred_element_type=F32
                        )

    right_side = call(
        loads_body,
        jax.ShapeDtypeStruct((comps, cells, width), F32),
        load_nodes,
        load_forces,
        name="point_loads",
        flops=1 << 28,
    )

    def own_row(row):
        return (row >= HALO_LOW) & (row < HALO_LOW + strip)

    def residual_body(
        in_ref, rhs_ref, disp_ref, cube_ref, geo_ref, zero_ref, one_ref, sum_ref
    ):
        above, below = shifts(plane, rows_x, ring_start)
        def gather(offset):
            offset = offset + (comps + 1) * span
            return [
                in_ref[place(layer) * in_rows + offset : place(layer) * in_rows + offset + half]
                for layer in range(depth)
            ]

        mask = jnp.concatenate(gather(half), 0)
        filtered = jnp.concatenate(filter_depth(gather(0)), 0)
        share = dot(mask / filtered, gauss_table(cols_y))
        share = filter_depth([share[layer * half : (layer + 1) * half] for layer in range(depth)])
        share = swap_blocks([share[layer] for layer in ring], strip)
        cube_side = iota(plane, 1) < rows_x
        for row in range(span):
            pick = lambda field: in_ref[pl.ds(field * span + row, depth, stride=in_rows), :]
            for comp in range(comps):
                disp_ref[comp, row] = pick(comp)
            both = pick(comps)
            other = pltpu.roll(both, rows_x, 1)
            cube = jnp.where(cube_side, both, other)
            cube_ref[0, row] = cube
            geo_ref[0, row] = jnp.where(
                cube < 0.0, 0.0, STIFF_VOID + (1.0 - STIFF_VOID) * cube
            )
            geo_ref[1, row] = 1.0 - jnp.where(cube_side, other, both)
        for row in range(1, span - 1):
            beside = geo_ref[0, row] + geo_ref[0, row - 1]
            beside = beside + below(beside, 0)
            beside = beside + below(beside, 1)
            free = geo_ref[1, row]
            geo_ref[2, row] = 1.0 / (free * DIAG_ENTRY * beside + (1.0 - free))

        scale_row = lambda row: geo_ref[0, row]

        def start_row(row):
            free = geo_ref[1, row]
            return [free * disp_ref[comp, row] for comp in range(comps)]

        def emit_residual(row, forces, carried):
            free, inverse = geo_ref[1, row], geo_ref[2, row]
            total = jnp.zeros(plane, F32)
            for comp, force in enumerate(forces):
                load_row = rhs_ref[comp, pl.ds(row * depth, depth), :]
                rest = free * (load_row - force) - (1.0 - free) * disp_ref[comp, row]
                value = rest * inverse
                zero_ref[comp, row] = value
                total = total + value * rest
            return carried + total if own_row(row) else carried

        weight = apply_rows(
            0, span - 1, start_row, scale_row, emit_residual, above, below,
            jnp.zeros(plane, F32),
        )

        def zero_row(row):
            free = geo_ref[1, row]
            return [free * zero_ref[comp, row] for comp in range(comps)]

        def emit_one(row, forces, carried):
            free, inverse = geo_ref[1, row], geo_ref[2, row]
            total = jnp.zeros(plane, F32)
            for comp, force in enumerate(forces):
                value = zero_ref[comp, row]
                applied = free * force + (1.0 - free) * value
                one_ref[comp, row] = applied * inverse
                total = total + value * applied
            return carried + total if own_row(row) else carried

        curve = apply_rows(
            1, span - 2, zero_row, scale_row, emit_one, above, below, jnp.zeros(plane, F32)
        )

        down = lambda value: jnp.sum(value, 0, keepdims=True)
        sums = [down(curve), down(weight), down(mask)]
        for target in range(slabs):
            base = place(target) * sum_rows
            for index, value in enumerate(sums):
                sum_ref[base + index : base + index + 1] = value
            sum_ref[base + 3 : base + 3 + half] = share[target]
            sum_ref[base + 3 + half : base + sum_rows] = filtered[
                target * half : (target + 1) * half
            ]

    disp, cube, geometry, zeroth, first, sums = call(
        residual_body,
        (
            block(comps),
            block(1),
            block(3),
            block(comps),
            block(comps),
            flat(slabs * sum_rows),
        ),
        received,
        right_side,
        name="residual",
        flops=1 << 26,
    )
    all_sums = exchange(sums, "slab", ring)

    def powers_body(geo_ref, one_ref, two_ref, three_ref):
        above, below = shifts(plane, rows_x, ring_start)
        scale_row = lambda row: geo_ref[0, row]
        for source, target, edge in ((one_ref, two_ref, 2), (two_ref, three_ref, 3)):

            def load_row(row):
                free = geo_ref[1, row]
                return [free * source[comp, row] for comp in range(comps)]

            def emit(row, forces, carried):
                free, inverse = geo_ref[1, row], geo_ref[2, row]
                for comp, force in enumerate(forces):
                    target[comp, row] = (
                        free * force + (1.0 - free) * source[comp, row]
                    ) * inverse
                return carried

            apply_rows(
                edge, span - 1 - edge, load_row, scale_row, emit, above, below,
                jnp.zeros((1, 1), F32),
            )

    second, third = call(
        powers_body,
        (block(comps), block(comps)),
        geometry,
        first,
        name="powers",
        flops=1 << 26,
    )

    def energy_body(
        sums_ref, disp_ref, cube_ref, geo_ref, zero_ref, one_ref, two_ref, three_ref,
        disp_out_ref, numer_ref, count_ref, weak_ref,
    ):
        above, below = shifts(plane, rows_x, ring_start)
        gather = lambda index: sum(
            sums_ref[layer * sum_rows + index : layer * sum_rows + index + 1]
            for layer in range(slabs)
        )
        curve, weight, count = gather(0), gather(1), gather(2)
        across = lambda value: jnp.sum(value, 1, keepdims=True)
        count_ref[...] = jnp.broadcast_to(across(count), (8, width))
        owner = iota((1, width), 1) // rows_x
        inverse = jnp.zeros((1, width), F32)
        for load in range(loads):
            mine = owner == load
            upper = UPPER_FACTOR * (
                across(jnp.where(mine, curve, 0.0)) / across(jnp.where(mine, weight, 0.0))
            )
            inverse = jnp.where(mine, 1.0 / (0.5 * (upper + LOWER_RATIO * upper)), inverse)
        inverse = jnp.broadcast_to(inverse, plane)
        lower = None
        for row in range(HALO_LOW, HALO_LOW + strip + 1):
            free = geo_ref[1, row]
            values = []
            for comp in range(comps):
                value = smoother[3] * three_ref[comp, row]
                value = smoother[2] * two_ref[comp, row] + inverse * value
                value = smoother[1] * one_ref[comp, row] + inverse * value
                value = smoother[0] * zero_ref[comp, row] + inverse * value
                value = disp_ref[comp, row] + inverse * value
                if row < HALO_LOW + strip:
                    start = comp * strip + row - HALO_LOW
                    disp_out_ref[pl.ds(start, depth, stride=out_rows), :] = value
                values.append(free * value)
            modes = row_modes(values, above)
            if lower is not None:
                weak_ref[pl.ds(row - 1 - HALO_LOW, depth, stride=strip), :] = (
                    (3.0 * (1.0 - STIFF_VOID))
                    * cube_ref[0, row - 1]
                    * element_energy(element_modes(lower, modes))
                )
            lower = modes
        disp_out_ref[pl.ds(out_rows - 1, depth, stride=out_rows), :] = jnp.zeros(plane, F32)
        shape = (rows_x, width)
        table_x = gauss(iota(shape, 0) - iota(shape, 1) % rows_x)
        weak = weak_ref[...]
        across_x = dot(table_x, weak, turned=True)
        shape = (width, width)
        table_x = gauss(iota(shape, 0) % rows_x - iota(shape, 1) % rows_x)
        smooth = dot(weak, table_x)
        weighted = jnp.zeros((1, width), F32)
        for source in range(slabs):
            base = place(source) * sum_rows + 3
            weighted = weighted + jnp.sum(
                across_x[source * half : (source + 1) * half] * sums_ref[base : base + half],
                0,
                keepdims=True,
            )
        block_of = iota((half, width), 1) // rows_x
        pieces = []
        for layer in range(depth):
            rows = place(layer) * strip
            piece = smooth[rows : rows + half]
            for block_at in range(1, strip // half):
                rows = rows + half
                piece = jnp.where(block_of == block_at, smooth[rows : rows + half], piece)
            pieces.append(piece)
        for layer, piece in enumerate(filter_depth(pieces)):
            for part in range(parts):
                base = (part * slabs + layer) * numer_rows
                numer_ref[base : base + half] = piece
                numer_ref[base + half : base + numer_rows] = weighted

    disp_message, numer_message, count = call(
        energy_body,
        (flat(slabs * out_rows), flat(parts * slabs * numer_rows), flat(8)),
        all_sums,
        disp,
        cube,
        geometry,
        zeroth,
        first,
        second,
        third,
        scratch=[pltpu.VMEM((strip * depth, width), F32)],
        name="energy",
        flops=1 << 24,
    )
    numer_pieces = exchange(numer_message, ("load", "slab"))

    def trial_body(
        numer_ref, dens_ref, sums_ref, design_ref, count_ref, disp_ref, trial_ref, out_ref,
        plane_ref, filtered_ref,
    ):
        weighted = jnp.zeros((1, width), F32)
        for source in range(slabs):
            total = jnp.zeros((half, width), F32)
            for part in range(parts):
                base = (part * slabs + source) * numer_rows
                total = total + numer_ref[base : base + half]
                weighted = weighted + numer_ref[base + half : base + numer_rows]
            base = place(source) * sum_rows + 3 + half
            filtered_ref[source * half : (source + 1) * half] = sums_ref[base : base + half]
            plane_ref[source * half : (source + 1) * half] = total
        mean = jnp.sum(weighted, 1, keepdims=True) / count_ref[0:1] + EPSILON
        packed = plane_ref[...].T
        numer = 0.0
        for block_at in range(strip // half):
            shape = (slabs * half, cols_y)
            row = iota(shape, 0)
            table = gauss(row // half * strip + block_at * half + row % half - iota(shape, 1))
            numer = numer + dot(packed[block_at * rows_x : (block_at + 1) * rows_x], table)
        mask = design_ref[0].astype(F32)
        dens = dens_ref[0]
        ratio = mask * (numer / filtered_ref[...]) / mean
        trial = jnp.clip(dens * jnp.sqrt(ratio), dens - MOVE_LIMIT, dens + MOVE_LIMIT)
        trial_ref[...] = trial
        volume = jnp.sum(mask * trial, 0, keepdims=True)
        for target in range(slabs):
            base = (target + 1) * out_rows - 1
            out_ref[base : base + 1] = volume

    trial, out_message = call(
        trial_body,
        (flat(rows_x), flat(slabs * out_rows)),
        numer_pieces,
        density,
        all_sums,
        design,
        count,
        disp_message,
        scratch=[pltpu.VMEM((rows_x, cols_y), F32)] * 2,
        name="trial",
        aliases={5: 1},
    )
    out_pieces = exchange(out_message, "slab", ring)

    def final_body(pieces_ref, trial_ref, design_ref, count_ref, disp_ref, dens_ref, whole_ref):
        volume = jnp.zeros((1, width), F32)
        for source in range(slabs):
            base = (place(source) + 1) * out_rows
            volume = volume + pieces_ref[base - 1 : base]
            for comp in range(comps):
                base = place(source) * out_rows + comp * strip
                whole_ref[comp, source * strip : (source + 1) * strip] = pieces_ref[
                    base : base + strip
                ]
        volume = jnp.sum(volume, 1, keepdims=True)
        scale = VOLUME_TARGET / (volume / count_ref[0:1] + EPSILON)
        mask = design_ref[0].astype(F32)
        dens_ref[0] = mask * jnp.minimum(scale * trial_ref[...], 1.0)
        for comp in range(comps):
            turned = whole_ref[comp].T
            for load in range(loads):
                disp_ref[load, comp, 0] = turned[load * rows_x : (load + 1) * rows_x]

    return call(
        final_body,
        (
            jax.ShapeDtypeStruct(start_disp.shape, F32),
            jax.ShapeDtypeStruct(density.shape, F32),
        ),
        out_pieces,
        trial,
        design,
        count,
        scratch=[pltpu.VMEM((comps, cols_y, width), F32)],
        name="final",
    )


def solution(mesh):
    return jax.shard_map(
        shards,
        mesh=mesh,
        in_specs=(
            P("load", None, "slab", None, None),
            P("slab", None, None),
            P("slab", None, None),
            P("slab", None, None),
            P("load", None),
            P("load", None, None),
        ),
        out_specs=(P("load", None, "slab", None, None), P("slab", None, None)),
        check_vma=False,
    )
```

```python
import functools

import jax
import jax.numpy as jnp
import numpy as np
from jax import lax
from jax.experimental import pallas as pl
from jax.experimental.pallas import tpu as pltpu
from jax.sharding import PartitionSpec as P

RADIUS = 2
POISSON = 0.3
STIFF_VOID = 0.001
UPPER_FACTOR = 1.2
LOWER_RATIO = 0.1
MOVE_LIMIT = 0.2
VOLUME_TARGET = 0.5
EPSILON = 1e-06
F32 = jnp.float32

HALO_LOW = 4
HALO_HIGH = 5
HALO = HALO_LOW + HALO_HIGH
VMEM_LIMIT = 24 * 1024 * 1024


def hex_stiffness():
    lame_first = POISSON / ((1 + POISSON) * (1 - 2 * POISSON))
    lame_shear = 1 / (2 * (1 + POISSON))
    elastic = np.zeros((6, 6))
    elastic[:3, :3] = lame_first
    for axis_a in range(3):
        elastic[axis_a, axis_a] += 2 * lame_shear
        elastic[3 + axis_a, 3 + axis_a] = lame_shear
    shear_pairs = ((0, 1), (1, 2), (0, 2))
    gauss_point = 1 / np.sqrt(3)
    matrix = np.zeros((24, 24))
    for quad_index in range(8):
        quad_coords = [
            gauss_point * (2 * (quad_index >> 2 - axis_a & 1) - 1) for axis_a in range(3)
        ]
        shape_grads = np.zeros((8, 3))
        for corner in range(8):
            corner_signs = [2 * (corner >> 2 - axis_a & 1) - 1 for axis_a in range(3)]
            for axis_a in range(3):
                deriv_value = float(corner_signs[axis_a])
                for axis_b in range(3):
                    if axis_b != axis_a:
                        deriv_value *= (1 + corner_signs[axis_b] * quad_coords[axis_b]) / 2
                shape_grads[corner, axis_a] = deriv_value
        strain = np.zeros((6, 24))
        for corner in range(8):
            for axis_a in range(3):
                strain[axis_a, 3 * corner + axis_a] = shape_grads[corner, axis_a]
            for pair_index, shear_pair in enumerate(shear_pairs):
                strain[3 + pair_index, 3 * corner + shear_pair[0]] = shape_grads[
                    corner, shear_pair[1]
                ]
                strain[3 + pair_index, 3 * corner + shear_pair[1]] = shape_grads[
                    corner, shear_pair[0]
                ]
        matrix += strain.T @ elastic @ strain / 8
    return matrix.astype(np.float32)


def mode_stiffness():
    signs = np.zeros((8, 8))
    for mode in range(8):
        for corner in range(8):
            flips = bin(mode & ~corner & 7).count("1")
            signs[mode, corner] = -1.0 if flips & 1 else 1.0
    spread = np.kron(signs, np.eye(3))
    return spread @ hex_stiffness().astype(np.float64) @ spread.T / 64


MODES = mode_stiffness()
DIAG_ENTRY = float(hex_stiffness()[0, 0])


def entry(mode_a, comp_a, mode_b, comp_b):
    return float(MODES[3 * mode_a + comp_a, 3 * mode_b + comp_b])


NORMAL = ((4, 0), (2, 1), (1, 2))
SHEAR = (((2, 0), (4, 1)), ((1, 0), (4, 2)), ((1, 1), (2, 2)))
TWIST = ((3, 0), (5, 1), (6, 2))
BEND = (((3, 1), (5, 0)), ((3, 2), (6, 0)), ((5, 2), (6, 1)))
WARP = ((7, 0), (7, 1), (7, 2))
NORMAL_ON = entry(4, 0, 4, 0)
NORMAL_OFF = entry(4, 0, 2, 1)
SHEAR_ON = entry(2, 0, 4, 1)
TWIST_ON = entry(3, 0, 3, 0)
TWIST_OFF = entry(3, 0, 5, 1)
BEND_ON = entry(3, 1, 3, 1)
BEND_OFF = entry(3, 1, 5, 0)
WARP_ON = entry(7, 0, 7, 0)


def smoother_factors():
    sigma = (1 + LOWER_RATIO) / (1 - LOWER_RATIO)
    factor = 1 / sigma
    residual = np.array([1.0, 0.0, 0.0, 0.0])
    update = np.array([1.0, 0.0, 0.0, 0.0])
    total = np.zeros(4)
    for sweep in range(4):
        total = total + update
        if sweep < 3:
            residual = residual - np.concatenate([[0.0], update[:3]])
            factor_next = 1 / (2 * sigma - factor)
            update = factor_next * factor * update + 2 * factor_next * sigma * residual
            factor = factor_next
    return [float(value) for value in total]


def iota(shape, axis):
    return lax.broadcasted_iota(jnp.int32, shape, axis)


def gauss(offsets):
    return jnp.exp(-((offsets.astype(F32) / RADIUS) ** 2))


def gauss_table(count):
    return gauss(iota((count, count), 0) - iota((count, count), 1))


def shifts(shape, rows_x, first):
    inner = {}
    for axis, start, count in ((0, first, shape[0]), (1, 0, rows_x)):
        index = (iota(shape, axis) + start) % count
        inner[axis] = (index < count - 1, index > 0)

    def above(value, axis):
        moved = pltpu.roll(value, shape[axis] - 1, axis)
        return jnp.where(inner[axis][0], moved, 0.0)

    def below(value, axis):
        moved = pltpu.roll(value, 1, axis)
        return jnp.where(inner[axis][1], moved, 0.0)

    return above, below


def row_modes(values, above):
    modes = {}
    for comp, value in enumerate(values):
        beside = above(value, 1)
        for bit, part in ((0, value + beside), (2, beside - value)):
            ahead = above(part, 0)
            modes[bit, comp] = part + ahead
            modes[bit + 4, comp] = ahead - part
    return modes


def element_modes(low, high):
    modes = {}
    for (bits, comp), value in low.items():
        other = high[bits, comp]
        if bits:
            modes[bits, comp] = value + other
        modes[bits + 1, comp] = other - value
    return modes


def element_forces(modes, scale):
    forces = {}
    total = modes[NORMAL[0]] + modes[NORMAL[1]] + modes[NORMAL[2]]
    shared = (scale * NORMAL_OFF) * total
    own = scale * (NORMAL_ON - NORMAL_OFF)
    for key in NORMAL:
        forces[key] = shared + own * modes[key]
    shear = scale * SHEAR_ON
    for key_a, key_b in SHEAR:
        forces[key_a] = forces[key_b] = shear * (modes[key_a] + modes[key_b])
    total = modes[TWIST[0]] + modes[TWIST[1]] + modes[TWIST[2]]
    shared = (scale * TWIST_OFF) * total
    own = scale * (TWIST_ON - TWIST_OFF)
    for key in TWIST:
        forces[key] = shared + own * modes[key]
    bend_on = scale * BEND_ON
    bend_off = scale * BEND_OFF
    for key_a, key_b in BEND:
        forces[key_a] = bend_on * modes[key_a] + bend_off * modes[key_b]
        forces[key_b] = bend_on * modes[key_b] + bend_off * modes[key_a]
    warp = scale * WARP_ON
    for key in WARP:
        forces[key] = warp * modes[key]
    return forces


def element_energy(modes):
    total = modes[NORMAL[0]] + modes[NORMAL[1]] + modes[NORMAL[2]]
    squares = sum(modes[key] * modes[key] for key in NORMAL)
    energy = NORMAL_OFF * (total * total) + (NORMAL_ON - NORMAL_OFF) * squares
    shear = 0.0
    for key_a, key_b in SHEAR:
        both = modes[key_a] + modes[key_b]
        shear = shear + both * both
    energy = energy + SHEAR_ON * shear
    total = modes[TWIST[0]] + modes[TWIST[1]] + modes[TWIST[2]]
    squares = sum(modes[key] * modes[key] for key in TWIST)
    energy = energy + TWIST_OFF * (total * total) + (TWIST_ON - TWIST_OFF) * squares
    squares = sum(modes[key] * modes[key] for pair in BEND for key in pair)
    crossed = sum(modes[key_a] * modes[key_b] for key_a, key_b in BEND)
    energy = energy + BEND_ON * squares + (2 * BEND_OFF) * crossed
    squares = sum(modes[key] * modes[key] for key in WARP)
    return energy + WARP_ON * squares


ROW_KEYS = [(bits, comp) for comp in range(3) for bits in (0, 2, 4, 6)]


def split_forces(forces):
    here, there = {}, {}
    for bits, comp in ROW_KEYS:
        change = forces[bits + 1, comp]
        if bits:
            common = forces[bits, comp]
            here[bits, comp] = common - change
            there[bits, comp] = common + change
        else:
            here[bits, comp] = -change
            there[bits, comp] = change
    return here, there


def node_forces(modes, below):
    values = []
    for comp in range(3):
        parts = []
        for bit in (0, 2):
            common, change = modes[bit, comp], modes[bit + 4, comp]
            parts.append((common - change) + below(common + change, 0))
        values.append((parts[0] - parts[1]) + below(parts[0] + parts[1], 1))
    return values


def apply_rows(first, last, load_row, scale_row, emit, above, below, carry=None):
    def advance(index, low, pending):
        high = row_modes(load_row(index + 1), above)
        forces = element_forces(element_modes(low, high), scale_row(index))
        here, there = split_forces(forces)
        return high, {key: pending[key] + here[key] for key in ROW_KEYS}, there

    low = row_modes(load_row(first), above)
    zero = {key: jnp.zeros_like(low[key]) for key in ROW_KEYS}
    low, _, pending = advance(first, low, zero)

    for index in range(first + 1, last):
        low, modes, pending = advance(index, low, pending)
        carry = emit(index, node_forces(modes, below), carry)
    return carry


def dot(left, right, turned=False):
    dims = (((1,), (1 if turned else 0,)), ((), ()))

    def halves(value):
        high = value.astype(jnp.bfloat16)
        return high, (value - high.astype(F32)).astype(jnp.bfloat16)

    def product(a, b):
        return lax.dot_general(a, b, dims, preferred_element_type=F32)

    left_high, left_low = halves(left)
    right_high, right_low = halves(right)
    return product(left_high, right_high) + (
        product(left_high, right_low) + product(left_low, right_high)
    )


def swap_blocks(values, block):
    values = list(values)
    lanes = values[0].shape[1]
    place = iota(values[0].shape, 1) // block
    bit = 1
    while bit < len(values):
        lower = (place & bit) == 0
        for index in range(len(values)):
            if not index & bit:
                low, high = values[index], values[index + bit]
                values[index] = jnp.where(lower, low, pltpu.roll(high, bit * block, 1))
                values[index + bit] = jnp.where(
                    lower, pltpu.roll(low, lanes - bit * block, 1), high
                )
        bit *= 2
    return values


def filter_depth(layers):
    depth = len(layers)
    if depth <= 16:
        weights = [float(np.exp(-((step / RADIUS) ** 2))) for step in range(depth)]
        return [
            sum(weights[abs(to - source)] * layers[source] for source in range(depth))
            for to in range(depth)
        ]
    rows = layers[0].shape[0]
    shape = (depth * rows, depth * rows)
    to, source = iota(shape, 0), iota(shape, 1)
    table = jnp.where(to % rows == source % rows, gauss(to // rows - source // rows), 0.0)
    mixed = dot(table, jnp.concatenate(layers, 0))
    return [mixed[layer * rows : (layer + 1) * rows] for layer in range(depth)]


def call(body, outs, *args, scratch=(), name=None, flops=0, space=pltpu.VMEM, aliases=None):
    return pl.pallas_call(
        body,
        out_shape=outs,
        in_specs=[pl.BlockSpec(memory_space=space)] * len(args),
        out_specs=jax.tree.map(lambda _: pl.BlockSpec(memory_space=pltpu.VMEM), outs),
        scratch_shapes=list(scratch),
        compiler_params=pltpu.CompilerParams(vmem_limit_bytes=VMEM_LIMIT),
        cost_estimate=pl.CostEstimate(flops=flops, bytes_accessed=1 << 20, transcendentals=0),
        input_output_aliases=aliases or {},
        name=name,
    )(*args)


def exchange(message, axes, order=None):
    rows = message.shape[0]
    return lax.all_to_all(
        message.reshape(rows, 1, message.shape[1]),
        axes,
        split_axis=0,
        concat_axis=0,
        tiled=True,
        axis_index_groups=order and [order],
    ).reshape(message.shape)


def shards(start_disp, density, design, support, load_nodes, load_forces):
    slabs = lax.axis_size("slab")
    parts = lax.axis_size("load")
    loads, comps, layers, rows_x, cols_y = start_disp.shape
    points = load_nodes.shape[1]
    depth = slabs * layers
    strip = cols_y // slabs
    span = strip + HALO
    width = loads * rows_x
    half = rows_x // slabs
    plane = (depth, width)
    in_rows = (comps + 1) * span + 2 * half
    sum_rows = 3 + 2 * half
    numer_rows = half + 1
    out_rows = comps * strip + 1
    block = lambda count: jax.ShapeDtypeStruct((count, span) + plane, F32)
    flat = lambda rows: jax.ShapeDtypeStruct((rows, width), F32)
    smoother = smoother_factors()
    ring_start = slabs // 2 - 1
    ring = [(at + ring_start) % slabs for at in range(slabs)]
    place = lambda index: (index - ring_start) % slabs
    sums_start = slabs // 2 - 2
    sums_ring = [(at + sums_start) % slabs for at in range(slabs)]
    sums_place = lambda index: (index - sums_start) % slabs

    def pack_body(
        disp_ref, dens_ref, design_ref, support_ref, out_ref,
        stage_ref, dens_in, design_in, support_in, pad_ref, sems,
    ):
        copies = [
            pltpu.make_async_copy(dens_ref.at[0], dens_in, sems.at[0]),
            pltpu.make_async_copy(design_ref.at[0], design_in, sems.at[1]),
            pltpu.make_async_copy(support_ref.at[0], support_in, sems.at[2]),
        ]
        for load in range(loads):
            copies.append(
                pltpu.make_async_copy(
                    disp_ref.at[load, :, 0],
                    stage_ref.at[:, load * rows_x : (load + 1) * rows_x],
                    sems.at[3 + load],
                )
            )
        for copy in copies:
            copy.start()
        cube_side = iota((1, width), 1) < rows_x
        for field in range(comps + 1):
            fill = jnp.zeros((1, width), F32) if field < comps else jnp.where(cube_side, -1.0, 1.0)
            pad_ref[field, 0:HALO_LOW] = jnp.broadcast_to(fill, (HALO_LOW, width))
            pad_ref[field, HALO_LOW + cols_y : HALO + cols_y] = jnp.broadcast_to(
                fill, (HALO_HIGH, width)
            )
        for copy in copies[:3]:
            copy.wait()
        spread = dot(dot(gauss_table(rows_x), dens_in[...]), gauss_table(cols_y))
        solid = design_in[...].astype(F32) * dens_in[...]
        both = jnp.concatenate([solid * solid * solid, support_in[...].astype(F32)], 0)
        pad_ref[comps, HALO_LOW : HALO_LOW + cols_y] = both.T
        for copy in copies[3:]:
            copy.wait()
        for comp in range(comps):
            pad_ref[comp, HALO_LOW : HALO_LOW + cols_y] = stage_ref[comp].T
        for target in range(slabs):
            base = place(target) * in_rows
            for field in range(comps + 1):
                out_ref[base + field * span : base + (field + 1) * span] = pad_ref[
                    field, target * strip : target * strip + span
                ]
            rows = slice(target * half, (target + 1) * half)
            base = base + (comps + 1) * span
            out_ref[base : base + half] = spread[rows]
            out_ref[base + half : base + 2 * half] = design_in[rows].astype(F32)

    message = call(
        pack_body,
        flat(slabs * in_rows),
        *(
            pltpu.with_memory_space_constraint(value, pltpu.HBM)
            for value in (start_disp, density, design, support)
        ),
        scratch=[
            pltpu.VMEM((comps, width, cols_y), F32),
            pltpu.VMEM((rows_x, cols_y), F32),
            pltpu.VMEM((rows_x, cols_y), jnp.int32),
            pltpu.VMEM((rows_x, cols_y), jnp.int32),
            pltpu.VMEM((comps + 1, cols_y + 2 * 8, width), F32),
            pltpu.SemaphoreType.DMA((3 + loads,)),
        ],
        name="pack",
        space=pltpu.HBM,
    )
    received = exchange(message, "slab", ring)

    cells = -(-span * depth // 16) * 16
    chunk = min(256, points)

    def loads_body(nodes_ref, forces_ref, out_ref):
        first = lax.axis_index("slab") * strip - HALO_LOW
        out_ref[...] = jnp.zeros_like(out_ref)
        for load in range(loads):
            for start in range(0, points, chunk):
                part = slice(start, start + chunk)
                node = nodes_ref[load : load + 1, part]
                row = node % cols_y - first
                lane = load * rows_x + (node // cols_y) % rows_x
                layer = (node // (cols_y * rows_x) + depth - ring_start) % depth
                cell = jnp.where((row >= 0) & (row < span), row * depth + layer, -1)
                hit = iota((cells, chunk), 0) == cell
                spot = (iota((width, chunk), 0) == lane).astype(F32).astype(jnp.bfloat16)
                for comp in range(comps):
                    rest = forces_ref[load, comp : comp + 1, part]
                    for piece in range(3):
                        rounded = rest.astype(jnp.bfloat16).astype(F32)
                        rest = rest - rounded
                        picked = jnp.where(hit, rounded, 0.0).astype(jnp.bfloat16)
                        out_ref[comp] += lax.dot_general(
                            picked, spot, (((1,), (1,)), ((), ())), preferred_element_type=F32
                        )

    right_side = call(
        loads_body,
        jax.ShapeDtypeStruct((comps, cells, width), F32),
        load_nodes,
        load_forces,
        name="point_loads",
        flops=1 << 28,
    )

    def own_row(row):
        return HALO_LOW <= row < HALO_LOW + strip

    last_row = HALO_LOW + strip
    near_nodes = range(HALO_LOW - 2, last_row + 3)
    near_zero = range(HALO_LOW - 1, last_row + 2)
    near_one = range(HALO_LOW, last_row + 1)

    def strip_rows(disp, geo, inverse, zero, one, in_ref, rhs_ref):
        above, below = shifts(plane, rows_x, ring_start)
        cube_side = iota(plane, 1) < rows_x
        scale_row = lambda row: geo(row)[0, row]

        def read(rows, cube_ref=None):
            for row in rows:
                pick = lambda field: in_ref[pl.ds(field * span + row, depth, stride=in_rows), :]
                for comp in range(comps):
                    disp(row)[comp, row] = pick(comp)
                both = pick(comps)
                other = pltpu.roll(both, rows_x, 1)
                cube = jnp.where(cube_side, both, other)
                if cube_ref is not None:
                    cube_ref[0, row] = cube
                geo(row)[0, row] = jnp.where(
                    cube < 0.0, 0.0, STIFF_VOID + (1.0 - STIFF_VOID) * cube
                )
                geo(row)[1, row] = 1.0 - jnp.where(cube_side, other, both)

        def invert(rows):
            for row in rows:
                beside = geo(row)[0, row] + geo(row - 1)[0, row - 1]
                beside = beside + below(beside, 0)
                beside = beside + below(beside, 1)
                free = geo(row)[1, row]
                inverse(row)[0, row] = 1.0 / (free * DIAG_ENTRY * beside + (1.0 - free))

        def masked(source):
            def load_row(row):
                free = geo(row)[1, row]
                return [free * source(row)[comp, row] for comp in range(comps)]

            return load_row

        def residual(first, last):
            def emit(row, forces, carried):
                free, inverted = geo(row)[1, row], inverse(row)[0, row]
                total = jnp.zeros(plane, F32)
                for comp, force in enumerate(forces):
                    load_row = rhs_ref[comp, row * depth : (row + 1) * depth, :]
                    rest = free * (load_row - force) - (1.0 - free) * disp(row)[comp, row]
                    value = rest * inverted
                    zero(row)[comp, row] = value
                    total = total + value * rest
                return carried + total if own_row(row) else carried

            return apply_rows(
                first, last, masked(disp), scale_row, emit, above, below, jnp.zeros(plane, F32)
            )

        def power(source, target, first, last):
            def emit(row, forces, carried):
                free, inverted = geo(row)[1, row], inverse(row)[0, row]
                total = jnp.zeros(plane, F32)
                for comp, force in enumerate(forces):
                    value = source(row)[comp, row]
                    applied = free * force + (1.0 - free) * value
                    target(row)[comp, row] = applied * inverted
                    total = total + value * applied
                return carried + total if own_row(row) else carried

            return apply_rows(
                first, last, masked(source), scale_row, emit, above, below, jnp.zeros(plane, F32)
            )

        return read, invert, residual, power

    def residual_body(
        in_ref, rhs_ref, disp_ref, cube_ref, geo_ref, inv_ref, zero_ref, one_ref, sum_ref
    ):
        def gather(offset):
            offset = offset + (comps + 1) * span
            return [
                in_ref[place(layer) * in_rows + offset : place(layer) * in_rows + offset + half]
                for layer in range(depth)
            ]

        mask = jnp.concatenate(gather(half), 0)
        filtered = jnp.concatenate(filter_depth(gather(0)), 0)
        share = dot(mask / filtered, gauss_table(cols_y))
        share = filter_depth([share[layer * half : (layer + 1) * half] for layer in range(depth)])
        share = swap_blocks([share[layer] for layer in ring], strip)
        here = lambda ref: lambda row: ref
        zero = here(zero_ref)
        read, invert, residual, power = strip_rows(
            here(disp_ref), here(geo_ref), here(inv_ref), zero, here(one_ref), in_ref, rhs_ref
        )
        read(near_nodes, cube_ref)
        invert(near_zero)
        weight = residual(near_zero[0] - 1, near_zero[-1] + 1)
        curve = power(zero, here(one_ref), near_one[0] - 1, near_one[-1] + 1)
        down = lambda value: jnp.sum(value, 0, keepdims=True)
        sums = [down(curve), down(weight), down(mask)]
        for target in range(slabs):
            base = sums_place(target) * sum_rows
            for index, value in enumerate(sums):
                sum_ref[base + index : base + index + 1] = value
            sum_ref[base + 3 : base + 3 + half] = share[target]
            sum_ref[base + 3 + half : base + sum_rows] = filtered[
                target * half : (target + 1) * half
            ]

    disp, cube, geometry, inverses, zeroth, first, sums = call(
        residual_body,
        (
            block(comps),
            block(1),
            block(2),
            block(1),
            block(comps),
            block(comps),
            flat(slabs * sum_rows),
        ),
        received,
        right_side,
        name="residual",
        flops=1 << 26,
    )
    all_sums = exchange(sums, "slab", sums_ring)

    def powers_body(
        in_ref, rhs_ref, disp_ref, geo_ref, inv_ref, zero_ref, one_ref, two_ref, three_ref,
        far_disp, far_geo, far_inv, far_zero, far_one,
    ):
        choose = lambda near, far, rows: lambda row: near if row in rows else far
        zero = choose(zero_ref, far_zero, near_zero)
        one = choose(one_ref, far_one, near_one)
        read, invert, residual, power = strip_rows(
            choose(disp_ref, far_disp, near_nodes),
            choose(geo_ref, far_geo, near_nodes),
            choose(inv_ref, far_inv, near_zero),
            zero,
            one,
            in_ref,
            rhs_ref,
        )
        read([row for row in range(span) if row not in near_nodes])
        invert([row for row in range(1, span - 1) if row not in near_zero])
        residual(0, near_zero[0])
        residual(near_zero[-1], span - 1)
        power(zero, one, 1, near_one[0])
        power(zero, one, near_one[-1], span - 2)
        power(one, lambda row: two_ref, 2, span - 3)
        power(lambda row: two_ref, lambda row: three_ref, 3, span - 4)

    second, third = call(
        powers_body,
        (block(comps), block(comps)),
        received,
        right_side,
        disp,
        geometry,
        inverses,
        zeroth,
        first,
        scratch=[
            pltpu.VMEM((count, span) + plane, F32) for count in (comps, 2, 1, comps, comps)
        ],
        name="powers",
        flops=1 << 26,
    )

    def energy_body(
        sums_ref, disp_ref, cube_ref, geo_ref, zero_ref, one_ref, two_ref, three_ref,
        disp_out_ref, numer_ref, count_ref, weak_ref,
    ):
        above, below = shifts(plane, rows_x, ring_start)
        gather = lambda index: sum(
            sums_ref[layer * sum_rows + index : layer * sum_rows + index + 1]
            for layer in range(slabs)
        )
        curve, weight, count = gather(0), gather(1), gather(2)
        across = lambda value: jnp.sum(value, 1, keepdims=True)
        count_ref[...] = jnp.broadcast_to(across(count), (8, width))
        owner = iota((1, width), 1) // rows_x
        inverse = jnp.zeros((1, width), F32)
        for load in range(loads):
            mine = owner == load
            upper = UPPER_FACTOR * (
                across(jnp.where(mine, curve, 0.0)) / across(jnp.where(mine, weight, 0.0))
            )
            inverse = jnp.where(mine, 1.0 / (0.5 * (upper + LOWER_RATIO * upper)), inverse)
        inverse = jnp.broadcast_to(inverse, plane)
        lower = None
        for row in range(HALO_LOW, HALO_LOW + strip + 1):
            free = geo_ref[1, row]
            values = []
            for comp in range(comps):
                value = smoother[3] * three_ref[comp, row]
                value = smoother[2] * two_ref[comp, row] + inverse * value
                value = smoother[1] * one_ref[comp, row] + inverse * value
                value = smoother[0] * zero_ref[comp, row] + inverse * value
                value = disp_ref[comp, row] + inverse * value
                if row < HALO_LOW + strip:
                    start = comp * strip + row - HALO_LOW
                    disp_out_ref[pl.ds(start, depth, stride=out_rows), :] = value
                values.append(free * value)
            modes = row_modes(values, above)
            if lower is not None:
                weak_ref[pl.ds(row - 1 - HALO_LOW, depth, stride=strip), :] = (
                    (3.0 * (1.0 - STIFF_VOID))
                    * cube_ref[0, row - 1]
                    * element_energy(element_modes(lower, modes))
                )
            lower = modes
        disp_out_ref[pl.ds(out_rows - 1, depth, stride=out_rows), :] = jnp.zeros(plane, F32)
        shape = (rows_x, width)
        table_x = gauss(iota(shape, 0) - iota(shape, 1) % rows_x)
        weak = weak_ref[...]
        across_x = dot(table_x, weak, turned=True)
        shape = (width, width)
        table_x = gauss(iota(shape, 0) % rows_x - iota(shape, 1) % rows_x)
        smooth = dot(weak, table_x)
        weighted = jnp.zeros((1, width), F32)
        for source in range(slabs):
            base = sums_place(source) * sum_rows + 3
            weighted = weighted + jnp.sum(
                across_x[source * half : (source + 1) * half] * sums_ref[base : base + half],
                0,
                keepdims=True,
            )
        block_of = iota((half, width), 1) // rows_x
        pieces = []
        for layer in range(depth):
            rows = place(layer) * strip
            piece = smooth[rows : rows + half]
            for block_at in range(1, strip // half):
                rows = rows + half
                piece = jnp.where(block_of == block_at, smooth[rows : rows + half], piece)
            pieces.append(piece)
        for layer, piece in enumerate(filter_depth(pieces)):
            for part in range(parts):
                base = (part * slabs + layer) * numer_rows
                numer_ref[base : base + half] = piece
                numer_ref[base + half : base + numer_rows] = weighted

    disp_message, numer_message, count = call(
        energy_body,
        (flat(slabs * out_rows), flat(parts * slabs * numer_rows), flat(8)),
        all_sums,
        disp,
        cube,
        geometry,
        zeroth,
        first,
        second,
        third,
        scratch=[pltpu.VMEM((strip * depth, width), F32)],
        name="energy",
        flops=1 << 24,
    )
    numer_pieces = exchange(numer_message, ("load", "slab"))

    def trial_body(
        numer_ref, dens_ref, sums_ref, design_ref, count_ref, disp_ref, trial_ref, out_ref,
        plane_ref, filtered_ref,
    ):
        weighted = jnp.zeros((1, width), F32)
        for source in range(slabs):
            total = jnp.zeros((half, width), F32)
            for part in range(parts):
                base = (part * slabs + source) * numer_rows
                total = total + numer_ref[base : base + half]
                weighted = weighted + numer_ref[base + half : base + numer_rows]
            base = sums_place(source) * sum_rows + 3 + half
            filtered_ref[source * half : (source + 1) * half] = sums_ref[base : base + half]
            plane_ref[source * half : (source + 1) * half] = total
        mean = jnp.sum(weighted, 1, keepdims=True) / count_ref[0:1] + EPSILON
        packed = plane_ref[...].T
        numer = 0.0
        for block_at in range(strip // half):
            shape = (slabs * half, cols_y)
            row = iota(shape, 0)
            table = gauss(row // half * strip + block_at * half + row % half - iota(shape, 1))
            numer = numer + dot(packed[block_at * rows_x : (block_at + 1) * rows_x], table)
        mask = design_ref[0].astype(F32)
        dens = dens_ref[0]
        ratio = mask * (numer / filtered_ref[...]) / mean
        trial = jnp.clip(dens * jnp.sqrt(ratio), dens - MOVE_LIMIT, dens + MOVE_LIMIT)
        trial_ref[...] = trial
        volume = jnp.sum(mask * trial, 0, keepdims=True)
        for target in range(slabs):
            base = (target + 1) * out_rows - 1
            out_ref[base : base + 1] = volume

    trial, out_message = call(
        trial_body,
        (flat(rows_x), flat(slabs * out_rows)),
        numer_pieces,
        density,
        all_sums,
        design,
        count,
        disp_message,
        scratch=[pltpu.VMEM((rows_x, cols_y), F32)] * 2,
        name="trial",
        aliases={5: 1},
    )
    out_pieces = exchange(out_message, "slab", ring)

    def final_body(pieces_ref, trial_ref, design_ref, count_ref, disp_ref, dens_ref, whole_ref):
        volume = jnp.zeros((1, width), F32)
        for source in range(slabs):
            base = (place(source) + 1) * out_rows
            volume = volume + pieces_ref[base - 1 : base]
            for comp in range(comps):
                base = place(source) * out_rows + comp * strip
                whole_ref[comp, source * strip : (source + 1) * strip] = pieces_ref[
                    base : base + strip
                ]
        volume = jnp.sum(volume, 1, keepdims=True)
        scale = VOLUME_TARGET / (volume / count_ref[0:1] + EPSILON)
        mask = design_ref[0].astype(F32)
        dens_ref[0] = mask * jnp.minimum(scale * trial_ref[...], 1.0)
        for comp in range(comps):
            turned = whole_ref[comp].T
            for load in range(loads):
                disp_ref[load, comp, 0] = turned[load * rows_x : (load + 1) * rows_x]

    return call(
        final_body,
        (
            jax.ShapeDtypeStruct(start_disp.shape, F32),
            jax.ShapeDtypeStruct(density.shape, F32),
        ),
        out_pieces,
        trial,
        design,
        count,
        scratch=[pltpu.VMEM((comps, cols_y, width), F32)],
        name="final",
    )


def solution(mesh):
    return jax.shard_map(
        shards,
        mesh=mesh,
        in_specs=(
            P("load", None, "slab", None, None),
            P("slab", None, None),
            P("slab", None, None),
            P("slab", None, None),
            P("load", None),
            P("load", None, None),
        ),
        out_specs=(P("load", None, "slab", None, None), P("slab", None, None)),
        check_vma=False,
    )
```

```python
import functools

import jax
import jax.numpy as jnp
import numpy as np
from jax import lax
from jax.experimental import pallas as pl
from jax.experimental.pallas import tpu as pltpu
from jax.sharding import PartitionSpec as P

RADIUS = 2
POISSON = 0.3
STIFF_VOID = 0.001
UPPER_FACTOR = 1.2
LOWER_RATIO = 0.1
MOVE_LIMIT = 0.2
VOLUME_TARGET = 0.5
EPSILON = 1e-06
F32 = jnp.float32

HALO_LOW = 4
HALO_HIGH = 5
HALO = HALO_LOW + HALO_HIGH
VMEM_LIMIT = 24 * 1024 * 1024


def hex_stiffness():
    lame_first = POISSON / ((1 + POISSON) * (1 - 2 * POISSON))
    lame_shear = 1 / (2 * (1 + POISSON))
    elastic = np.zeros((6, 6))
    elastic[:3, :3] = lame_first
    for axis_a in range(3):
        elastic[axis_a, axis_a] += 2 * lame_shear
        elastic[3 + axis_a, 3 + axis_a] = lame_shear
    shear_pairs = ((0, 1), (1, 2), (0, 2))
    gauss_point = 1 / np.sqrt(3)
    matrix = np.zeros((24, 24))
    for quad_index in range(8):
        quad_coords = [
            gauss_point * (2 * (quad_index >> 2 - axis_a & 1) - 1) for axis_a in range(3)
        ]
        shape_grads = np.zeros((8, 3))
        for corner in range(8):
            corner_signs = [2 * (corner >> 2 - axis_a & 1) - 1 for axis_a in range(3)]
            for axis_a in range(3):
                deriv_value = float(corner_signs[axis_a])
                for axis_b in range(3):
                    if axis_b != axis_a:
                        deriv_value *= (1 + corner_signs[axis_b] * quad_coords[axis_b]) / 2
                shape_grads[corner, axis_a] = deriv_value
        strain = np.zeros((6, 24))
        for corner in range(8):
            for axis_a in range(3):
                strain[axis_a, 3 * corner + axis_a] = shape_grads[corner, axis_a]
            for pair_index, shear_pair in enumerate(shear_pairs):
                strain[3 + pair_index, 3 * corner + shear_pair[0]] = shape_grads[
                    corner, shear_pair[1]
                ]
                strain[3 + pair_index, 3 * corner + shear_pair[1]] = shape_grads[
                    corner, shear_pair[0]
                ]
        matrix += strain.T @ elastic @ strain / 8
    return matrix.astype(np.float32)


def mode_stiffness():
    signs = np.zeros((8, 8))
    for mode in range(8):
        for corner in range(8):
            flips = bin(mode & ~corner & 7).count("1")
            signs[mode, corner] = -1.0 if flips & 1 else 1.0
    spread = np.kron(signs, np.eye(3))
    return spread @ hex_stiffness().astype(np.float64) @ spread.T / 64


MODES = mode_stiffness()
DIAG_ENTRY = float(hex_stiffness()[0, 0])


def entry(mode_a, comp_a, mode_b, comp_b):
    return float(MODES[3 * mode_a + comp_a, 3 * mode_b + comp_b])


NORMAL = ((4, 0), (2, 1), (1, 2))
SHEAR = (((2, 0), (4, 1)), ((1, 0), (4, 2)), ((1, 1), (2, 2)))
TWIST = ((3, 0), (5, 1), (6, 2))
BEND = (((3, 1), (5, 0)), ((3, 2), (6, 0)), ((5, 2), (6, 1)))
WARP = ((7, 0), (7, 1), (7, 2))
NORMAL_ON = entry(4, 0, 4, 0)
NORMAL_OFF = entry(4, 0, 2, 1)
SHEAR_ON = entry(2, 0, 4, 1)
TWIST_ON = entry(3, 0, 3, 0)
TWIST_OFF = entry(3, 0, 5, 1)
BEND_ON = entry(3, 1, 3, 1)
BEND_OFF = entry(3, 1, 5, 0)
WARP_ON = entry(7, 0, 7, 0)


def smoother_factors():
    sigma = (1 + LOWER_RATIO) / (1 - LOWER_RATIO)
    factor = 1 / sigma
    residual = np.array([1.0, 0.0, 0.0, 0.0])
    update = np.array([1.0, 0.0, 0.0, 0.0])
    total = np.zeros(4)
    for sweep in range(4):
        total = total + update
        if sweep < 3:
            residual = residual - np.concatenate([[0.0], update[:3]])
            factor_next = 1 / (2 * sigma - factor)
            update = factor_next * factor * update + 2 * factor_next * sigma * residual
            factor = factor_next
    return [float(value) for value in total]


def iota(shape, axis):
    return lax.broadcasted_iota(jnp.int32, shape, axis)


def gauss(offsets):
    return jnp.exp(-((offsets.astype(F32) / RADIUS) ** 2))


def gauss_table(count):
    return gauss(iota((count, count), 0) - iota((count, count), 1))


def shifts(shape, rows_x, first):
    inner = {}
    for axis, start, count in ((0, first, shape[0]), (1, 0, rows_x)):
        index = (iota(shape, axis) + start) % count
        inner[axis] = (index < count - 1, index > 0)

    def above(value, axis):
        moved = pltpu.roll(value, shape[axis] - 1, axis)
        return jnp.where(inner[axis][0], moved, 0.0)

    def below(value, axis):
        moved = pltpu.roll(value, 1, axis)
        return jnp.where(inner[axis][1], moved, 0.0)

    return above, below


def row_modes(values, above):
    modes = {}
    for comp, value in enumerate(values):
        beside = above(value, 1)
        for bit, part in ((0, value + beside), (2, beside - value)):
            ahead = above(part, 0)
            modes[bit, comp] = part + ahead
            modes[bit + 4, comp] = ahead - part
    return modes


def element_modes(low, high):
    modes = {}
    for (bits, comp), value in low.items():
        other = high[bits, comp]
        if bits:
            modes[bits, comp] = value + other
        modes[bits + 1, comp] = other - value
    return modes


def element_forces(modes, scale):
    forces = {}
    total = modes[NORMAL[0]] + modes[NORMAL[1]] + modes[NORMAL[2]]
    shared = (scale * NORMAL_OFF) * total
    own = scale * (NORMAL_ON - NORMAL_OFF)
    for key in NORMAL:
        forces[key] = shared + own * modes[key]
    shear = scale * SHEAR_ON
    for key_a, key_b in SHEAR:
        forces[key_a] = forces[key_b] = shear * (modes[key_a] + modes[key_b])
    total = modes[TWIST[0]] + modes[TWIST[1]] + modes[TWIST[2]]
    shared = (scale * TWIST_OFF) * total
    own = scale * (TWIST_ON - TWIST_OFF)
    for key in TWIST:
        forces[key] = shared + own * modes[key]
    bend_on = scale * BEND_ON
    bend_off = scale * BEND_OFF
    for key_a, key_b in BEND:
        forces[key_a] = bend_on * modes[key_a] + bend_off * modes[key_b]
        forces[key_b] = bend_on * modes[key_b] + bend_off * modes[key_a]
    warp = scale * WARP_ON
    for key in WARP:
        forces[key] = warp * modes[key]
    return forces


def element_energy(modes):
    total = modes[NORMAL[0]] + modes[NORMAL[1]] + modes[NORMAL[2]]
    squares = sum(modes[key] * modes[key] for key in NORMAL)
    energy = NORMAL_OFF * (total * total) + (NORMAL_ON - NORMAL_OFF) * squares
    shear = 0.0
    for key_a, key_b in SHEAR:
        both = modes[key_a] + modes[key_b]
        shear = shear + both * both
    energy = energy + SHEAR_ON * shear
    total = modes[TWIST[0]] + modes[TWIST[1]] + modes[TWIST[2]]
    squares = sum(modes[key] * modes[key] for key in TWIST)
    energy = energy + TWIST_OFF * (total * total) + (TWIST_ON - TWIST_OFF) * squares
    squares = sum(modes[key] * modes[key] for pair in BEND for key in pair)
    crossed = sum(modes[key_a] * modes[key_b] for key_a, key_b in BEND)
    energy = energy + BEND_ON * squares + (2 * BEND_OFF) * crossed
    squares = sum(modes[key] * modes[key] for key in WARP)
    return energy + WARP_ON * squares


ROW_KEYS = [(bits, comp) for comp in range(3) for bits in (0, 2, 4, 6)]


def split_forces(forces):
    here, there = {}, {}
    for bits, comp in ROW_KEYS:
        change = forces[bits + 1, comp]
        if bits:
            common = forces[bits, comp]
            here[bits, comp] = common - change
            there[bits, comp] = common + change
        else:
            here[bits, comp] = -change
            there[bits, comp] = change
    return here, there


def node_forces(modes, below):
    values = []
    for comp in range(3):
        parts = []
        for bit in (0, 2):
            common, change = modes[bit, comp], modes[bit + 4, comp]
            parts.append((common - change) + below(common + change, 0))
        values.append((parts[0] - parts[1]) + below(parts[0] + parts[1], 1))
    return values


def apply_rows(first, last, load_row, scale_row, emit, above, below, carry=None):
    def advance(index, low, pending):
        high = row_modes(load_row(index + 1), above)
        forces = element_forces(element_modes(low, high), scale_row(index))
        here, there = split_forces(forces)
        return high, {key: pending[key] + here[key] for key in ROW_KEYS}, there

    low = row_modes(load_row(first), above)
    zero = {key: jnp.zeros_like(low[key]) for key in ROW_KEYS}
    low, _, pending = advance(first, low, zero)

    for index in range(first + 1, last):
        low, modes, pending = advance(index, low, pending)
        carry = emit(index, node_forces(modes, below), carry)
    return carry


def dot(left, right, turned=False):
    dims = (((1,), (1 if turned else 0,)), ((), ()))

    def halves(value):
        high = value.astype(jnp.bfloat16)
        return high, (value - high.astype(F32)).astype(jnp.bfloat16)

    def product(a, b):
        return lax.dot_general(a, b, dims, preferred_element_type=F32)

    left_high, left_low = halves(left)
    right_high, right_low = halves(right)
    return product(left_high, right_high) + (
        product(left_high, right_low) + product(left_low, right_high)
    )


def swap_blocks(values, block):
    values = list(values)
    lanes = values[0].shape[1]
    place = iota(values[0].shape, 1) // block
    bit = 1
    while bit < len(values):
        lower = (place & bit) == 0
        for index in range(len(values)):
            if not index & bit:
                low, high = values[index], values[index + bit]
                values[index] = jnp.where(lower, low, pltpu.roll(high, bit * block, 1))
                values[index + bit] = jnp.where(
                    lower, pltpu.roll(low, lanes - bit * block, 1), high
                )
        bit *= 2
    return values


def filter_depth(layers):
    depth = len(layers)
    if depth <= 16:
        weights = [float(np.exp(-((step / RADIUS) ** 2))) for step in range(depth)]
        return [
            sum(weights[abs(to - source)] * layers[source] for source in range(depth))
            for to in range(depth)
        ]
    rows = layers[0].shape[0]
    shape = (depth * rows, depth * rows)
    to, source = iota(shape, 0), iota(shape, 1)
    table = jnp.where(to % rows == source % rows, gauss(to // rows - source // rows), 0.0)
    mixed = dot(table, jnp.concatenate(layers, 0))
    return [mixed[layer * rows : (layer + 1) * rows] for layer in range(depth)]


def call(body, outs, *args, scratch=(), name=None, flops=0, space=pltpu.VMEM, aliases=None):
    return pl.pallas_call(
        body,
        out_shape=outs,
        in_specs=[pl.BlockSpec(memory_space=space)] * len(args),
        out_specs=jax.tree.map(lambda _: pl.BlockSpec(memory_space=pltpu.VMEM), outs),
        scratch_shapes=list(scratch),
        compiler_params=pltpu.CompilerParams(vmem_limit_bytes=VMEM_LIMIT),
        cost_estimate=pl.CostEstimate(flops=flops, bytes_accessed=1 << 20, transcendentals=0),
        input_output_aliases=aliases or {},
        name=name,
    )(*args)


def exchange(message, axes, order=None):
    rows = message.shape[0]
    return lax.all_to_all(
        message.reshape(rows, 1, message.shape[1]),
        axes,
        split_axis=0,
        concat_axis=0,
        tiled=True,
        axis_index_groups=order and [order],
    ).reshape(message.shape)


def shards(start_disp, density, design, support, load_nodes, load_forces):
    slabs = lax.axis_size("slab")
    parts = lax.axis_size("load")
    loads, comps, layers, rows_x, cols_y = start_disp.shape
    points = load_nodes.shape[1]
    depth = slabs * layers
    strip = cols_y // slabs
    span = strip + HALO
    width = loads * rows_x
    half = rows_x // slabs
    plane = (depth, width)
    in_rows = (comps + 1) * span + 2 * half
    sum_rows = 3 + 2 * half
    numer_rows = half + 1
    out_rows = comps * strip + 1
    block = lambda count: jax.ShapeDtypeStruct((count, span) + plane, F32)
    flat = lambda rows: jax.ShapeDtypeStruct((rows, width), F32)
    smoother = smoother_factors()
    ring_start = slabs // 2 - 1
    ring = [(at + ring_start) % slabs for at in range(slabs)]
    place = lambda index: (index - ring_start) % slabs
    sums_start = slabs // 2 - 2
    sums_ring = [(at + sums_start) % slabs for at in range(slabs)]
    sums_place = lambda index: (index - sums_start) % slabs

    def pack_body(
        disp_ref, dens_ref, design_ref, support_ref, out_ref,
        stage_ref, dens_in, design_in, support_in, pad_ref, sems,
    ):
        copies = [
            pltpu.make_async_copy(dens_ref.at[0], dens_in, sems.at[0]),
            pltpu.make_async_copy(design_ref.at[0], design_in, sems.at[1]),
            pltpu.make_async_copy(support_ref.at[0], support_in, sems.at[2]),
        ]
        for load in range(loads):
            copies.append(
                pltpu.make_async_copy(
                    disp_ref.at[load, :, 0],
                    stage_ref.at[:, load * rows_x : (load + 1) * rows_x],
                    sems.at[3 + load],
                )
            )
        for copy in copies:
            copy.start()
        cube_side = iota((1, width), 1) < rows_x
        for field in range(comps + 1):
            fill = jnp.zeros((1, width), F32) if field < comps else jnp.where(cube_side, -1.0, 1.0)
            pad_ref[field, 0:HALO_LOW] = jnp.broadcast_to(fill, (HALO_LOW, width))
            pad_ref[field, HALO_LOW + cols_y : HALO + cols_y] = jnp.broadcast_to(
                fill, (HALO_HIGH, width)
            )
        for copy in copies[:3]:
            copy.wait()
        spread = dot(dot(gauss_table(rows_x), dens_in[...]), gauss_table(cols_y))
        solid = design_in[...].astype(F32) * dens_in[...]
        both = jnp.concatenate([solid * solid * solid, support_in[...].astype(F32)], 0)
        pad_ref[comps, HALO_LOW : HALO_LOW + cols_y] = both.T
        for copy in copies[3:]:
            copy.wait()
        for comp in range(comps):
            pad_ref[comp, HALO_LOW : HALO_LOW + cols_y] = stage_ref[comp].T
        for target in range(slabs):
            base = place(target) * in_rows
            for field in range(comps + 1):
                out_ref[base + field * span : base + (field + 1) * span] = pad_ref[
                    field, target * strip : target * strip + span
                ]
            rows = slice(target * half, (target + 1) * half)
            base = base + (comps + 1) * span
            out_ref[base : base + half] = spread[rows]
            out_ref[base + half : base + 2 * half] = design_in[rows].astype(F32)

    message = call(
        pack_body,
        flat(slabs * in_rows),
        *(
            pltpu.with_memory_space_constraint(value, pltpu.HBM)
            for value in (start_disp, density, design, support)
        ),
        scratch=[
            pltpu.VMEM((comps, width, cols_y), F32),
            pltpu.VMEM((rows_x, cols_y), F32),
            pltpu.VMEM((rows_x, cols_y), jnp.int32),
            pltpu.VMEM((rows_x, cols_y), jnp.int32),
            pltpu.VMEM((comps + 1, cols_y + 2 * 8, width), F32),
            pltpu.SemaphoreType.DMA((3 + loads,)),
        ],
        name="pack",
        space=pltpu.HBM,
    )
    received = exchange(message, "slab", ring)

    cells = -(-span * depth // 16) * 16
    chunk = min(256, points)

    def loads_body(nodes_ref, forces_ref, out_ref):
        first = lax.axis_index("slab") * strip - HALO_LOW
        out_ref[...] = jnp.zeros_like(out_ref)
        for load in range(loads):
            for start in range(0, points, chunk):
                part = slice(start, start + chunk)
                node = nodes_ref[load : load + 1, part]
                row = node % cols_y - first
                lane = load * rows_x + (node // cols_y) % rows_x
                layer = (node // (cols_y * rows_x) + depth - ring_start) % depth
                cell = jnp.where((row >= 0) & (row < span), row * depth + layer, -1)
                hit = iota((cells, chunk), 0) == cell
                spot = (iota((width, chunk), 0) == lane).astype(F32).astype(jnp.bfloat16)
                for comp in range(comps):
                    rest = forces_ref[load, comp : comp + 1, part]
                    for piece in range(3):
                        rounded = rest.astype(jnp.bfloat16).astype(F32)
                        rest = rest - rounded
                        picked = jnp.where(hit, rounded, 0.0).astype(jnp.bfloat16)
                        out_ref[comp] += lax.dot_general(
                            picked, spot, (((1,), (1,)), ((), ())), preferred_element_type=F32
                        )

    right_side = call(
        loads_body,
        jax.ShapeDtypeStruct((comps, cells, width), F32),
        load_nodes,
        load_forces,
        name="point_loads",
        flops=1 << 28,
    )

    def own_row(row):
        return HALO_LOW <= row < HALO_LOW + strip

    last_row = HALO_LOW + strip
    near_nodes = range(HALO_LOW - 1, last_row + 2)
    near_zero = range(HALO_LOW, last_row + 1)

    def strip_rows(disp, geo, inverse, zero, in_ref, rhs_ref):
        above, below = shifts(plane, rows_x, ring_start)
        cube_side = iota(plane, 1) < rows_x
        scale_row = lambda row: geo(row)[0, row]

        def read(rows, cube_ref=None):
            for row in rows:
                pick = lambda field: in_ref[pl.ds(field * span + row, depth, stride=in_rows), :]
                for comp in range(comps):
                    disp(row)[comp, row] = pick(comp)
                both = pick(comps)
                other = pltpu.roll(both, rows_x, 1)
                cube = jnp.where(cube_side, both, other)
                if cube_ref is not None:
                    cube_ref[0, row] = cube
                geo(row)[0, row] = jnp.where(
                    cube < 0.0, 0.0, STIFF_VOID + (1.0 - STIFF_VOID) * cube
                )
                geo(row)[1, row] = 1.0 - jnp.where(cube_side, other, both)

        def invert(rows):
            for row in rows:
                beside = geo(row)[0, row] + geo(row - 1)[0, row - 1]
                beside = beside + below(beside, 0)
                beside = beside + below(beside, 1)
                free = geo(row)[1, row]
                inverse(row)[0, row] = 1.0 / (free * DIAG_ENTRY * beside + (1.0 - free))

        def masked(source):
            def load_row(row):
                free = geo(row)[1, row]
                return [free * source(row)[comp, row] for comp in range(comps)]

            return load_row

        def residual(first, last):
            def emit(row, forces, carried):
                free, inverted = geo(row)[1, row], inverse(row)[0, row]
                total = jnp.zeros(plane, F32)
                for comp, force in enumerate(forces):
                    load_row = rhs_ref[comp, row * depth : (row + 1) * depth, :]
                    rest = free * (load_row - force) - (1.0 - free) * disp(row)[comp, row]
                    value = rest * inverted
                    zero(row)[comp, row] = value
                    total = total + value * rest
                return carried + total if own_row(row) else carried

            return apply_rows(
                first, last, masked(disp), scale_row, emit, above, below, jnp.zeros(plane, F32)
            )

        def curvature():
            total, lower = jnp.zeros(plane, F32), None
            for row in near_zero:
                modes = row_modes(masked(zero)(row), above)
                if lower is not None:
                    total = total + scale_row(row - 1) * element_energy(
                        element_modes(lower, modes)
                    )
                if own_row(row):
                    fixed = 1.0 - geo(row)[1, row]
                    values = [zero(row)[comp, row] for comp in range(comps)]
                    total = total + fixed * sum(value * value for value in values)
                lower = modes
            return total

        def power(source, target, first, last):
            def emit(row, forces, carried):
                free, inverted = geo(row)[1, row], inverse(row)[0, row]
                for comp, force in enumerate(forces):
                    applied = free * force + (1.0 - free) * source(row)[comp, row]
                    target(row)[comp, row] = applied * inverted

            apply_rows(first, last, masked(source), scale_row, emit, above, below)

        return read, invert, residual, curvature, power

    def residual_body(in_ref, rhs_ref, disp_ref, cube_ref, geo_ref, inv_ref, zero_ref, sum_ref):
        def gather(offset):
            offset = offset + (comps + 1) * span
            return [
                in_ref[place(layer) * in_rows + offset : place(layer) * in_rows + offset + half]
                for layer in range(depth)
            ]

        mask = jnp.concatenate(gather(half), 0)
        filtered = jnp.concatenate(filter_depth(gather(0)), 0)
        share = dot(mask / filtered, gauss_table(cols_y))
        share = filter_depth([share[layer * half : (layer + 1) * half] for layer in range(depth)])
        share = swap_blocks([share[layer] for layer in ring], strip)
        here = lambda ref: lambda row: ref
        read, invert, residual, curvature, _ = strip_rows(
            here(disp_ref), here(geo_ref), here(inv_ref), here(zero_ref), in_ref, rhs_ref
        )
        read(near_nodes, cube_ref)
        invert(near_zero)
        weight = residual(near_zero[0] - 1, near_zero[-1] + 1)
        curve = curvature()
        down = lambda value: jnp.sum(value, 0, keepdims=True)
        sums = [down(curve), down(weight), down(mask)]
        for target in range(slabs):
            base = sums_place(target) * sum_rows
            for index, value in enumerate(sums):
                sum_ref[base + index : base + index + 1] = value
            sum_ref[base + 3 : base + 3 + half] = share[target]
            sum_ref[base + 3 + half : base + sum_rows] = filtered[
                target * half : (target + 1) * half
            ]

    disp, cube, geometry, inverses, zeroth, sums = call(
        residual_body,
        (
            block(comps),
            block(1),
            block(2),
            block(1),
            block(comps),
            flat(slabs * sum_rows),
        ),
        received,
        right_side,
        name="residual",
        flops=1 << 26,
    )
    all_sums = exchange(sums, "slab", sums_ring)

    def powers_body(
        in_ref, rhs_ref, disp_ref, geo_ref, inv_ref, zero_ref, one_ref, two_ref, three_ref,
        far_disp, far_geo, far_inv, far_zero,
    ):
        choose = lambda near, far, rows: lambda row: near if row in rows else far
        zero = choose(zero_ref, far_zero, near_zero)
        read, invert, residual, _, power = strip_rows(
            choose(disp_ref, far_disp, near_nodes),
            choose(geo_ref, far_geo, near_nodes),
            choose(inv_ref, far_inv, near_zero),
            zero,
            in_ref,
            rhs_ref,
        )
        read([row for row in range(span) if row not in near_nodes])
        invert([row for row in range(1, span - 1) if row not in near_zero])
        residual(0, near_zero[0])
        residual(near_zero[-1], span - 1)
        power(zero, lambda row: one_ref, 1, span - 2)
        power(lambda row: one_ref, lambda row: two_ref, 2, span - 3)
        power(lambda row: two_ref, lambda row: three_ref, 3, span - 4)

    first, second, third = call(
        powers_body,
        (block(comps), block(comps), block(comps)),
        received,
        right_side,
        disp,
        geometry,
        inverses,
        zeroth,
        scratch=[pltpu.VMEM((count, span) + plane, F32) for count in (comps, 2, 1, comps)],
        name="powers",
        flops=1 << 26,
    )

    def energy_body(
        sums_ref, disp_ref, cube_ref, geo_ref, zero_ref, one_ref, two_ref, three_ref,
        disp_out_ref, numer_ref, count_ref, weak_ref,
    ):
        above, below = shifts(plane, rows_x, ring_start)
        gather = lambda index: sum(
            sums_ref[layer * sum_rows + index : layer * sum_rows + index + 1]
            for layer in range(slabs)
        )
        curve, weight, count = gather(0), gather(1), gather(2)
        across = lambda value: jnp.sum(value, 1, keepdims=True)
        count_ref[...] = jnp.broadcast_to(across(count), (8, width))
        owner = iota((1, width), 1) // rows_x
        inverse = jnp.zeros((1, width), F32)
        for load in range(loads):
            mine = owner == load
            upper = UPPER_FACTOR * (
                across(jnp.where(mine, curve, 0.0)) / across(jnp.where(mine, weight, 0.0))
            )
            inverse = jnp.where(mine, 1.0 / (0.5 * (upper + LOWER_RATIO * upper)), inverse)
        inverse = jnp.broadcast_to(inverse, plane)
        lower = None
        for row in range(HALO_LOW, HALO_LOW + strip + 1):
            free = geo_ref[1, row]
            values = []
            for comp in range(comps):
                value = smoother[3] * three_ref[comp, row]
                value = smoother[2] * two_ref[comp, row] + inverse * value
                value = smoother[1] * one_ref[comp, row] + inverse * value
                value = smoother[0] * zero_ref[comp, row] + inverse * value
                value = disp_ref[comp, row] + inverse * value
                if row < HALO_LOW + strip:
                    start = comp * strip + row - HALO_LOW
                    disp_out_ref[pl.ds(start, depth, stride=out_rows), :] = value
                values.append(free * value)
            modes = row_modes(values, above)
            if lower is not None:
                weak_ref[pl.ds(row - 1 - HALO_LOW, depth, stride=strip), :] = (
                    (3.0 * (1.0 - STIFF_VOID))
                    * cube_ref[0, row - 1]
                    * element_energy(element_modes(lower, modes))
                )
            lower = modes
        disp_out_ref[pl.ds(out_rows - 1, depth, stride=out_rows), :] = jnp.zeros(plane, F32)
        shape = (rows_x, width)
        table_x = gauss(iota(shape, 0) - iota(shape, 1) % rows_x)
        weak = weak_ref[...]
        across_x = dot(table_x, weak, turned=True)
        shape = (width, width)
        table_x = gauss(iota(shape, 0) % rows_x - iota(shape, 1) % rows_x)
        smooth = dot(weak, table_x)
        weighted = jnp.zeros((1, width), F32)
        for source in range(slabs):
            base = sums_place(source) * sum_rows + 3
            weighted = weighted + jnp.sum(
                across_x[source * half : (source + 1) * half] * sums_ref[base : base + half],
                0,
                keepdims=True,
            )
        block_of = iota((half, width), 1) // rows_x
        pieces = []
        for layer in range(depth):
            rows = place(layer) * strip
            piece = smooth[rows : rows + half]
            for block_at in range(1, strip // half):
                rows = rows + half
                piece = jnp.where(block_of == block_at, smooth[rows : rows + half], piece)
            pieces.append(piece)
        for layer, piece in enumerate(filter_depth(pieces)):
            for part in range(parts):
                base = (part * slabs + layer) * numer_rows
                numer_ref[base : base + half] = piece
                numer_ref[base + half : base + numer_rows] = weighted

    disp_message, numer_message, count = call(
        energy_body,
        (flat(slabs * out_rows), flat(parts * slabs * numer_rows), flat(8)),
        all_sums,
        disp,
        cube,
        geometry,
        zeroth,
        first,
        second,
        third,
        scratch=[pltpu.VMEM((strip * depth, width), F32)],
        name="energy",
        flops=1 << 24,
    )
    numer_pieces = exchange(numer_message, ("load", "slab"))

    def trial_body(
        numer_ref, dens_ref, sums_ref, design_ref, count_ref, disp_ref, trial_ref, out_ref,
        plane_ref, filtered_ref,
    ):
        weighted = jnp.zeros((1, width), F32)
        for source in range(slabs):
            total = jnp.zeros((half, width), F32)
            for part in range(parts):
                base = (part * slabs + source) * numer_rows
                total = total + numer_ref[base : base + half]
                weighted = weighted + numer_ref[base + half : base + numer_rows]
            base = sums_place(source) * sum_rows + 3 + half
            filtered_ref[source * half : (source + 1) * half] = sums_ref[base : base + half]
            plane_ref[source * half : (source + 1) * half] = total
        mean = jnp.sum(weighted, 1, keepdims=True) / count_ref[0:1] + EPSILON
        packed = plane_ref[...].T
        numer = 0.0
        for block_at in range(strip // half):
            shape = (slabs * half, cols_y)
            row = iota(shape, 0)
            table = gauss(row // half * strip + block_at * half + row % half - iota(shape, 1))
            numer = numer + dot(packed[block_at * rows_x : (block_at + 1) * rows_x], table)
        mask = design_ref[0].astype(F32)
        dens = dens_ref[0]
        ratio = mask * (numer / filtered_ref[...]) / mean
        trial = jnp.clip(dens * jnp.sqrt(ratio), dens - MOVE_LIMIT, dens + MOVE_LIMIT)
        trial_ref[...] = trial
        volume = jnp.sum(mask * trial, 0, keepdims=True)
        for target in range(slabs):
            base = (target + 1) * out_rows - 1
            out_ref[base : base + 1] = volume

    trial, out_message = call(
        trial_body,
        (flat(rows_x), flat(slabs * out_rows)),
        numer_pieces,
        density,
        all_sums,
        design,
        count,
        disp_message,
        scratch=[pltpu.VMEM((rows_x, cols_y), F32)] * 2,
        name="trial",
        aliases={5: 1},
    )
    out_pieces = exchange(out_message, "slab", ring)

    def final_body(pieces_ref, trial_ref, design_ref, count_ref, disp_ref, dens_ref, whole_ref):
        volume = jnp.zeros((1, width), F32)
        for source in range(slabs):
            base = (place(source) + 1) * out_rows
            volume = volume + pieces_ref[base - 1 : base]
            for comp in range(comps):
                base = place(source) * out_rows + comp * strip
                whole_ref[comp, source * strip : (source + 1) * strip] = pieces_ref[
                    base : base + strip
                ]
        volume = jnp.sum(volume, 1, keepdims=True)
        scale = VOLUME_TARGET / (volume / count_ref[0:1] + EPSILON)
        mask = design_ref[0].astype(F32)
        dens_ref[0] = mask * jnp.minimum(scale * trial_ref[...], 1.0)
        for comp in range(comps):
            turned = whole_ref[comp].T
            for load in range(loads):
                disp_ref[load, comp, 0] = turned[load * rows_x : (load + 1) * rows_x]

    return call(
        final_body,
        (
            jax.ShapeDtypeStruct(start_disp.shape, F32),
            jax.ShapeDtypeStruct(density.shape, F32),
        ),
        out_pieces,
        trial,
        design,
        count,
        scratch=[pltpu.VMEM((comps, cols_y, width), F32)],
        name="final",
    )


def solution(mesh):
    return jax.shard_map(
        shards,
        mesh=mesh,
        in_specs=(
            P("load", None, "slab", None, None),
            P("slab", None, None),
            P("slab", None, None),
            P("slab", None, None),
            P("load", None),
            P("load", None, None),
        ),
        out_specs=(P("load", None, "slab", None, None), P("slab", None, None)),
        check_vma=False,
    )
```

```python
import functools

import jax
import jax.numpy as jnp
import numpy as np
from jax import lax
from jax.experimental import pallas as pl
from jax.experimental.pallas import tpu as pltpu
from jax.sharding import PartitionSpec as P

RADIUS = 2
POISSON = 0.3
STIFF_VOID = 0.001
UPPER_FACTOR = 1.2
LOWER_RATIO = 0.1
MOVE_LIMIT = 0.2
VOLUME_TARGET = 0.5
EPSILON = 1e-06
F32 = jnp.float32

HALO_LOW = 4
HALO_HIGH = 5
HALO = HALO_LOW + HALO_HIGH
VMEM_LIMIT = 24 * 1024 * 1024


def hex_stiffness():
    lame_first = POISSON / ((1 + POISSON) * (1 - 2 * POISSON))
    lame_shear = 1 / (2 * (1 + POISSON))
    elastic = np.zeros((6, 6))
    elastic[:3, :3] = lame_first
    for axis_a in range(3):
        elastic[axis_a, axis_a] += 2 * lame_shear
        elastic[3 + axis_a, 3 + axis_a] = lame_shear
    shear_pairs = ((0, 1), (1, 2), (0, 2))
    gauss_point = 1 / np.sqrt(3)
    matrix = np.zeros((24, 24))
    for quad_index in range(8):
        quad_coords = [
            gauss_point * (2 * (quad_index >> 2 - axis_a & 1) - 1) for axis_a in range(3)
        ]
        shape_grads = np.zeros((8, 3))
        for corner in range(8):
            corner_signs = [2 * (corner >> 2 - axis_a & 1) - 1 for axis_a in range(3)]
            for axis_a in range(3):
                deriv_value = float(corner_signs[axis_a])
                for axis_b in range(3):
                    if axis_b != axis_a:
                        deriv_value *= (1 + corner_signs[axis_b] * quad_coords[axis_b]) / 2
                shape_grads[corner, axis_a] = deriv_value
        strain = np.zeros((6, 24))
        for corner in range(8):
            for axis_a in range(3):
                strain[axis_a, 3 * corner + axis_a] = shape_grads[corner, axis_a]
            for pair_index, shear_pair in enumerate(shear_pairs):
                strain[3 + pair_index, 3 * corner + shear_pair[0]] = shape_grads[
                    corner, shear_pair[1]
                ]
                strain[3 + pair_index, 3 * corner + shear_pair[1]] = shape_grads[
                    corner, shear_pair[0]
                ]
        matrix += strain.T @ elastic @ strain / 8
    return matrix.astype(np.float32)


def mode_stiffness():
    signs = np.zeros((8, 8))
    for mode in range(8):
        for corner in range(8):
            flips = bin(mode & ~corner & 7).count("1")
            signs[mode, corner] = -1.0 if flips & 1 else 1.0
    spread = np.kron(signs, np.eye(3))
    return spread @ hex_stiffness().astype(np.float64) @ spread.T / 64


MODES = mode_stiffness()
DIAG_ENTRY = float(hex_stiffness()[0, 0])


def entry(mode_a, comp_a, mode_b, comp_b):
    return float(MODES[3 * mode_a + comp_a, 3 * mode_b + comp_b])


NORMAL = ((4, 0), (2, 1), (1, 2))
SHEAR = (((2, 0), (4, 1)), ((1, 0), (4, 2)), ((1, 1), (2, 2)))
TWIST = ((3, 0), (5, 1), (6, 2))
BEND = (((3, 1), (5, 0)), ((3, 2), (6, 0)), ((5, 2), (6, 1)))
WARP = ((7, 0), (7, 1), (7, 2))
NORMAL_ON = entry(4, 0, 4, 0)
NORMAL_OFF = entry(4, 0, 2, 1)
SHEAR_ON = entry(2, 0, 4, 1)
TWIST_ON = entry(3, 0, 3, 0)
TWIST_OFF = entry(3, 0, 5, 1)
BEND_ON = entry(3, 1, 3, 1)
BEND_OFF = entry(3, 1, 5, 0)
WARP_ON = entry(7, 0, 7, 0)


def smoother_factors():
    sigma = (1 + LOWER_RATIO) / (1 - LOWER_RATIO)
    factor = 1 / sigma
    residual = np.array([1.0, 0.0, 0.0, 0.0])
    update = np.array([1.0, 0.0, 0.0, 0.0])
    total = np.zeros(4)
    for sweep in range(4):
        total = total + update
        if sweep < 3:
            residual = residual - np.concatenate([[0.0], update[:3]])
            factor_next = 1 / (2 * sigma - factor)
            update = factor_next * factor * update + 2 * factor_next * sigma * residual
            factor = factor_next
    return [float(value) for value in total]


def iota(shape, axis):
    return lax.broadcasted_iota(jnp.int32, shape, axis)


def gauss(offsets):
    return jnp.exp(-((offsets.astype(F32) / RADIUS) ** 2))


def gauss_table(count):
    return gauss(iota((count, count), 0) - iota((count, count), 1))


def shifts(shape, rows_x, first):
    inner = {}
    for axis, start, count in ((0, first, shape[0]), (1, 0, rows_x)):
        index = (iota(shape, axis) + start) % count
        inner[axis] = (index < count - 1, index > 0)

    def above(value, axis):
        moved = pltpu.roll(value, shape[axis] - 1, axis)
        return jnp.where(inner[axis][0], moved, 0.0)

    def below(value, axis):
        moved = pltpu.roll(value, 1, axis)
        return jnp.where(inner[axis][1], moved, 0.0)

    return above, below


def row_modes(values, above):
    modes = {}
    for comp, value in enumerate(values):
        beside = above(value, 1)
        for bit, part in ((0, value + beside), (2, beside - value)):
            ahead = above(part, 0)
            modes[bit, comp] = part + ahead
            modes[bit + 4, comp] = ahead - part
    return modes


def element_modes(low, high):
    modes = {}
    for (bits, comp), value in low.items():
        other = high[bits, comp]
        if bits:
            modes[bits, comp] = value + other
        modes[bits + 1, comp] = other - value
    return modes


def element_forces(modes, scale):
    forces = {}
    total = modes[NORMAL[0]] + modes[NORMAL[1]] + modes[NORMAL[2]]
    shared = (scale * NORMAL_OFF) * total
    own = scale * (NORMAL_ON - NORMAL_OFF)
    for key in NORMAL:
        forces[key] = shared + own * modes[key]
    shear = scale * SHEAR_ON
    for key_a, key_b in SHEAR:
        forces[key_a] = forces[key_b] = shear * (modes[key_a] + modes[key_b])
    total = modes[TWIST[0]] + modes[TWIST[1]] + modes[TWIST[2]]
    shared = (scale * TWIST_OFF) * total
    own = scale * (TWIST_ON - TWIST_OFF)
    for key in TWIST:
        forces[key] = shared + own * modes[key]
    bend_on = scale * BEND_ON
    bend_off = scale * BEND_OFF
    for key_a, key_b in BEND:
        forces[key_a] = bend_on * modes[key_a] + bend_off * modes[key_b]
        forces[key_b] = bend_on * modes[key_b] + bend_off * modes[key_a]
    warp = scale * WARP_ON
    for key in WARP:
        forces[key] = warp * modes[key]
    return forces


def element_energy(modes):
    total = modes[NORMAL[0]] + modes[NORMAL[1]] + modes[NORMAL[2]]
    squares = sum(modes[key] * modes[key] for key in NORMAL)
    energy = NORMAL_OFF * (total * total) + (NORMAL_ON - NORMAL_OFF) * squares
    shear = 0.0
    for key_a, key_b in SHEAR:
        both = modes[key_a] + modes[key_b]
        shear = shear + both * both
    energy = energy + SHEAR_ON * shear
    total = modes[TWIST[0]] + modes[TWIST[1]] + modes[TWIST[2]]
    squares = sum(modes[key] * modes[key] for key in TWIST)
    energy = energy + TWIST_OFF * (total * total) + (TWIST_ON - TWIST_OFF) * squares
    squares = sum(modes[key] * modes[key] for pair in BEND for key in pair)
    crossed = sum(modes[key_a] * modes[key_b] for key_a, key_b in BEND)
    energy = energy + BEND_ON * squares + (2 * BEND_OFF) * crossed
    squares = sum(modes[key] * modes[key] for key in WARP)
    return energy + WARP_ON * squares


ROW_KEYS = [(bits, comp) for comp in range(3) for bits in (0, 2, 4, 6)]


def split_forces(forces):
    here, there = {}, {}
    for bits, comp in ROW_KEYS:
        change = forces[bits + 1, comp]
        if bits:
            common = forces[bits, comp]
            here[bits, comp] = common - change
            there[bits, comp] = common + change
        else:
            here[bits, comp] = -change
            there[bits, comp] = change
    return here, there


def node_forces(modes, below):
    values = []
    for comp in range(3):
        parts = []
        for bit in (0, 2):
            common, change = modes[bit, comp], modes[bit + 4, comp]
            parts.append((common - change) + below(common + change, 0))
        values.append((parts[0] - parts[1]) + below(parts[0] + parts[1], 1))
    return values


def apply_rows(first, last, load_row, scale_row, emit, above, below, carry=None):
    def advance(index, low, pending):
        high = row_modes(load_row(index + 1), above)
        forces = element_forces(element_modes(low, high), scale_row(index))
        here, there = split_forces(forces)
        return high, {key: pending[key] + here[key] for key in ROW_KEYS}, there

    low = row_modes(load_row(first), above)
    zero = {key: jnp.zeros_like(low[key]) for key in ROW_KEYS}
    low, _, pending = advance(first, low, zero)

    for index in range(first + 1, last):
        low, modes, pending = advance(index, low, pending)
        carry = emit(index, node_forces(modes, below), carry)
    return carry


def dot(left, right, turned=False):
    dims = (((1,), (1 if turned else 0,)), ((), ()))

    def halves(value):
        high = value.astype(jnp.bfloat16)
        return high, (value - high.astype(F32)).astype(jnp.bfloat16)

    def product(a, b):
        return lax.dot_general(a, b, dims, preferred_element_type=F32)

    left_high, left_low = halves(left)
    right_high, right_low = halves(right)
    return product(left_high, right_high) + (
        product(left_high, right_low) + product(left_low, right_high)
    )


def swap_blocks(values, block):
    values = list(values)
    lanes = values[0].shape[1]
    place = iota(values[0].shape, 1) // block
    bit = 1
    while bit < len(values):
        lower = (place & bit) == 0
        for index in range(len(values)):
            if not index & bit:
                low, high = values[index], values[index + bit]
                values[index] = jnp.where(lower, low, pltpu.roll(high, bit * block, 1))
                values[index + bit] = jnp.where(
                    lower, pltpu.roll(low, lanes - bit * block, 1), high
                )
        bit *= 2
    return values


def filter_depth(layers):
    depth = len(layers)
    if depth <= 16:
        weights = [float(np.exp(-((step / RADIUS) ** 2))) for step in range(depth)]
        return [
            sum(weights[abs(to - source)] * layers[source] for source in range(depth))
            for to in range(depth)
        ]
    rows = layers[0].shape[0]
    shape = (depth * rows, depth * rows)
    to, source = iota(shape, 0), iota(shape, 1)
    table = jnp.where(to % rows == source % rows, gauss(to // rows - source // rows), 0.0)
    mixed = dot(table, jnp.concatenate(layers, 0))
    return [mixed[layer * rows : (layer + 1) * rows] for layer in range(depth)]


def call(body, outs, *args, scratch=(), name=None, flops=0, space=pltpu.VMEM):
    return pl.pallas_call(
        body,
        out_shape=outs,
        in_specs=[pl.BlockSpec(memory_space=space)] * len(args),
        out_specs=jax.tree.map(lambda _: pl.BlockSpec(memory_space=pltpu.VMEM), outs),
        scratch_shapes=list(scratch),
        compiler_params=pltpu.CompilerParams(vmem_limit_bytes=VMEM_LIMIT),
        cost_estimate=pl.CostEstimate(flops=flops, bytes_accessed=1 << 20, transcendentals=0),
        name=name,
    )(*args)


def exchange(message, axes, order=None):
    rows = message.shape[0]
    return lax.all_to_all(
        message.reshape(rows, 1, message.shape[1]),
        axes,
        split_axis=0,
        concat_axis=0,
        tiled=True,
        axis_index_groups=order and [order],
    ).reshape(message.shape)


def shards(start_disp, density, design, support, load_nodes, load_forces):
    slabs = lax.axis_size("slab")
    parts = lax.axis_size("load")
    loads, comps, layers, rows_x, cols_y = start_disp.shape
    points = load_nodes.shape[1]
    depth = slabs * layers
    strip = cols_y // slabs
    span = strip + HALO
    width = loads * rows_x
    half = rows_x // slabs
    plane = (depth, width)
    in_rows = (comps + 1) * span + 2 * half
    sum_rows = 3 + 2 * half
    numer_rows = half + 1
    out_rows = comps * strip + 1
    block = lambda count: jax.ShapeDtypeStruct((count, span) + plane, F32)
    flat = lambda rows: jax.ShapeDtypeStruct((rows, width), F32)
    smoother = smoother_factors()
    ring_start = slabs // 2 - 1
    ring = [(at + ring_start) % slabs for at in range(slabs)]
    place = lambda index: (index - ring_start) % slabs
    sums_start = slabs // 2 - 2
    sums_ring = [(at + sums_start) % slabs for at in range(slabs)]
    sums_place = lambda index: (index - sums_start) % slabs

    def pack_body(
        disp_ref, dens_ref, design_ref, support_ref, out_ref,
        stage_ref, dens_in, design_in, support_in, pad_ref, sems,
    ):
        copies = [
            pltpu.make_async_copy(dens_ref.at[0], dens_in, sems.at[0]),
            pltpu.make_async_copy(design_ref.at[0], design_in, sems.at[1]),
            pltpu.make_async_copy(support_ref.at[0], support_in, sems.at[2]),
        ]
        for load in range(loads):
            copies.append(
                pltpu.make_async_copy(
                    disp_ref.at[load, :, 0],
                    stage_ref.at[:, load * rows_x : (load + 1) * rows_x],
                    sems.at[3 + load],
                )
            )
        for copy in copies:
            copy.start()
        cube_side = iota((1, width), 1) < rows_x
        for field in range(comps + 1):
            fill = jnp.zeros((1, width), F32) if field < comps else jnp.where(cube_side, -1.0, 1.0)
            pad_ref[field, 0:HALO_LOW] = jnp.broadcast_to(fill, (HALO_LOW, width))
            pad_ref[field, HALO_LOW + cols_y : HALO + cols_y] = jnp.broadcast_to(
                fill, (HALO_HIGH, width)
            )
        for copy in copies[:3]:
            copy.wait()
        spread = dot(dot(gauss_table(rows_x), dens_in[...]), gauss_table(cols_y))
        solid = design_in[...].astype(F32) * dens_in[...]
        both = jnp.concatenate([solid * solid * solid, support_in[...].astype(F32)], 0)
        pad_ref[comps, HALO_LOW : HALO_LOW + cols_y] = both.T
        for copy in copies[3:]:
            copy.wait()
        for comp in range(comps):
            pad_ref[comp, HALO_LOW : HALO_LOW + cols_y] = stage_ref[comp].T
        for target in range(slabs):
            base = place(target) * in_rows
            for field in range(comps + 1):
                out_ref[base + field * span : base + (field + 1) * span] = pad_ref[
                    field, target * strip : target * strip + span
                ]
            rows = slice(target * half, (target + 1) * half)
            base = base + (comps + 1) * span
            out_ref[base : base + half] = spread[rows]
            out_ref[base + half : base + 2 * half] = design_in[rows].astype(F32)

    message = call(
        pack_body,
        flat(slabs * in_rows),
        *(
            pltpu.with_memory_space_constraint(value, pltpu.HBM)
            for value in (start_disp, density, design, support)
        ),
        scratch=[
            pltpu.VMEM((comps, width, cols_y), F32),
            pltpu.VMEM((rows_x, cols_y), F32),
            pltpu.VMEM((rows_x, cols_y), jnp.int32),
            pltpu.VMEM((rows_x, cols_y), jnp.int32),
            pltpu.VMEM((comps + 1, cols_y + 2 * 8, width), F32),
            pltpu.SemaphoreType.DMA((3 + loads,)),
        ],
        name="pack",
        space=pltpu.HBM,
    )
    received = exchange(message, "slab", ring)

    cells = -(-span * depth // 16) * 16
    chunk = min(256, points)

    def loads_body(nodes_ref, forces_ref, out_ref):
        first = lax.axis_index("slab") * strip - HALO_LOW
        out_ref[...] = jnp.zeros_like(out_ref)
        for load in range(loads):
            for start in range(0, points, chunk):
                part = slice(start, start + chunk)
                node = nodes_ref[load : load + 1, part]
                row = node % cols_y - first
                lane = load * rows_x + (node // cols_y) % rows_x
                layer = (node // (cols_y * rows_x) + depth - ring_start) % depth
                cell = jnp.where((row >= 0) & (row < span), row * depth + layer, -1)
                hit = iota((cells, chunk), 0) == cell
                spot = (iota((width, chunk), 0) == lane).astype(F32).astype(jnp.bfloat16)
                for comp in range(comps):
                    rest = forces_ref[load, comp : comp + 1, part]
                    for piece in range(3):
                        rounded = rest.astype(jnp.bfloat16).astype(F32)
                        rest = rest - rounded
                        picked = jnp.where(hit, rounded, 0.0).astype(jnp.bfloat16)
                        out_ref[comp] += lax.dot_general(
                            picked, spot, (((1,), (1,)), ((), ())), preferred_element_type=F32
                        )

    right_side = call(
        loads_body,
        jax.ShapeDtypeStruct((comps, cells, width), F32),
        load_nodes,
        load_forces,
        name="point_loads",
        flops=1 << 28,
    )

    def own_row(row):
        return HALO_LOW <= row < HALO_LOW + strip

    last_row = HALO_LOW + strip
    near_nodes = range(HALO_LOW - 1, last_row + 2)
    near_zero = range(HALO_LOW, last_row + 1)

    def strip_rows(disp, geo, inverse, zero, in_ref, rhs_ref):
        above, below = shifts(plane, rows_x, ring_start)
        cube_side = iota(plane, 1) < rows_x
        scale_row = lambda row: geo(row)[0, row]

        def read(rows, cube_ref=None):
            for row in rows:
                pick = lambda field: in_ref[pl.ds(field * span + row, depth, stride=in_rows), :]
                for comp in range(comps):
                    disp(row)[comp, row] = pick(comp)
                both = pick(comps)
                other = pltpu.roll(both, rows_x, 1)
                cube = jnp.where(cube_side, both, other)
                if cube_ref is not None:
                    cube_ref[0, row] = cube
                geo(row)[0, row] = jnp.where(
                    cube < 0.0, 0.0, STIFF_VOID + (1.0 - STIFF_VOID) * cube
                )
                geo(row)[1, row] = 1.0 - jnp.where(cube_side, other, both)

        def invert(rows):
            for row in rows:
                beside = geo(row)[0, row] + geo(row - 1)[0, row - 1]
                beside = beside + below(beside, 0)
                beside = beside + below(beside, 1)
                free = geo(row)[1, row]
                inverse(row)[0, row] = 1.0 / (free * DIAG_ENTRY * beside + (1.0 - free))

        def masked(source):
            def load_row(row):
                free = geo(row)[1, row]
                return [free * source(row)[comp, row] for comp in range(comps)]

            return load_row

        def residual(first, last):
            def emit(row, forces, carried):
                free, inverted = geo(row)[1, row], inverse(row)[0, row]
                total = jnp.zeros(plane, F32)
                for comp, force in enumerate(forces):
                    load_row = rhs_ref[comp, row * depth : (row + 1) * depth, :]
                    rest = free * (load_row - force) - (1.0 - free) * disp(row)[comp, row]
                    value = rest * inverted
                    zero(row)[comp, row] = value
                    total = total + value * rest
                return carried + total if own_row(row) else carried

            return apply_rows(
                first, last, masked(disp), scale_row, emit, above, below, jnp.zeros(plane, F32)
            )

        def curvature():
            total, lower = jnp.zeros(plane, F32), None
            for row in near_zero:
                modes = row_modes(masked(zero)(row), above)
                if lower is not None:
                    total = total + scale_row(row - 1) * element_energy(
                        element_modes(lower, modes)
                    )
                if own_row(row):
                    fixed = 1.0 - geo(row)[1, row]
                    values = [zero(row)[comp, row] for comp in range(comps)]
                    total = total + fixed * sum(value * value for value in values)
                lower = modes
            return total

        def power(source, target, first, last):
            def emit(row, forces, carried):
                free, inverted = geo(row)[1, row], inverse(row)[0, row]
                for comp, force in enumerate(forces):
                    applied = free * force + (1.0 - free) * source(row)[comp, row]
                    target(row)[comp, row] = applied * inverted

            apply_rows(first, last, masked(source), scale_row, emit, above, below)

        return read, invert, residual, curvature, power

    def residual_body(in_ref, rhs_ref, disp_ref, cube_ref, geo_ref, inv_ref, zero_ref, sum_ref):
        def gather(offset):
            offset = offset + (comps + 1) * span
            return [
                in_ref[place(layer) * in_rows + offset : place(layer) * in_rows + offset + half]
                for layer in range(depth)
            ]

        mask = jnp.concatenate(gather(half), 0)
        filtered = jnp.concatenate(filter_depth(gather(0)), 0)
        share = dot(mask / filtered, gauss_table(cols_y))
        share = filter_depth([share[layer * half : (layer + 1) * half] for layer in range(depth)])
        share = swap_blocks([share[layer] for layer in ring], strip)
        here = lambda ref: lambda row: ref
        read, invert, residual, curvature, _ = strip_rows(
            here(disp_ref), here(geo_ref), here(inv_ref), here(zero_ref), in_ref, rhs_ref
        )
        read(near_nodes, cube_ref)
        invert(near_zero)
        weight = residual(near_zero[0] - 1, near_zero[-1] + 1)
        curve = curvature()
        down = lambda value: jnp.sum(value, 0, keepdims=True)
        sums = [down(curve), down(weight), down(mask)]
        for target in range(slabs):
            base = sums_place(target) * sum_rows
            for index, value in enumerate(sums):
                sum_ref[base + index : base + index + 1] = value
            sum_ref[base + 3 : base + 3 + half] = share[target]
            sum_ref[base + 3 + half : base + sum_rows] = filtered[
                target * half : (target + 1) * half
            ]

    disp, cube, geometry, inverses, zeroth, sums = call(
        residual_body,
        (
            block(comps),
            block(1),
            block(2),
            block(1),
            block(comps),
            flat(slabs * sum_rows),
        ),
        received,
        right_side,
        name="residual",
        flops=1 << 26,
    )
    all_sums = exchange(sums, "slab", sums_ring)

    def powers_body(
        in_ref, rhs_ref, disp_ref, geo_ref, inv_ref, zero_ref, one_ref, two_ref, three_ref,
        far_disp, far_geo, far_inv, far_zero,
    ):
        choose = lambda near, far, rows: lambda row: near if row in rows else far
        zero = choose(zero_ref, far_zero, near_zero)
        read, invert, residual, _, power = strip_rows(
            choose(disp_ref, far_disp, near_nodes),
            choose(geo_ref, far_geo, near_nodes),
            choose(inv_ref, far_inv, near_zero),
            zero,
            in_ref,
            rhs_ref,
        )
        read([row for row in range(span) if row not in near_nodes])
        invert([row for row in range(1, span - 1) if row not in near_zero])
        residual(0, near_zero[0])
        residual(near_zero[-1], span - 1)
        power(zero, lambda row: one_ref, 1, span - 2)
        power(lambda row: one_ref, lambda row: two_ref, 2, span - 3)
        power(lambda row: two_ref, lambda row: three_ref, 3, span - 4)

    first, second, third = call(
        powers_body,
        (block(comps), block(comps), block(comps)),
        received,
        right_side,
        disp,
        geometry,
        inverses,
        zeroth,
        scratch=[pltpu.VMEM((count, span) + plane, F32) for count in (comps, 2, 1, comps)],
        name="powers",
        flops=1 << 26,
    )

    def energy_body(
        sums_ref, disp_ref, cube_ref, geo_ref, zero_ref, one_ref, two_ref, three_ref,
        disp_out_ref, numer_ref, count_ref, weak_ref,
    ):
        above, below = shifts(plane, rows_x, ring_start)
        gather = lambda index: sum(
            sums_ref[layer * sum_rows + index : layer * sum_rows + index + 1]
            for layer in range(slabs)
        )
        curve, weight, count = gather(0), gather(1), gather(2)
        across = lambda value: jnp.sum(value, 1, keepdims=True)
        count_ref[...] = jnp.broadcast_to(across(count), (8, width))
        owner = iota((1, width), 1) // rows_x
        inverse = jnp.zeros((1, width), F32)
        for load in range(loads):
            mine = owner == load
            upper = UPPER_FACTOR * (
                across(jnp.where(mine, curve, 0.0)) / across(jnp.where(mine, weight, 0.0))
            )
            inverse = jnp.where(mine, 1.0 / (0.5 * (upper + LOWER_RATIO * upper)), inverse)
        inverse = jnp.broadcast_to(inverse, plane)
        lower = None
        for row in range(HALO_LOW, HALO_LOW + strip + 1):
            free = geo_ref[1, row]
            values = []
            for comp in range(comps):
                value = smoother[3] * three_ref[comp, row]
                value = smoother[2] * two_ref[comp, row] + inverse * value
                value = smoother[1] * one_ref[comp, row] + inverse * value
                value = smoother[0] * zero_ref[comp, row] + inverse * value
                value = disp_ref[comp, row] + inverse * value
                if row < HALO_LOW + strip:
                    start = comp * strip + row - HALO_LOW
                    disp_out_ref[pl.ds(start, depth, stride=out_rows), :] = value
                values.append(free * value)
            modes = row_modes(values, above)
            if lower is not None:
                weak_ref[pl.ds(row - 1 - HALO_LOW, depth, stride=strip), :] = (
                    (3.0 * (1.0 - STIFF_VOID))
                    * cube_ref[0, row - 1]
                    * element_energy(element_modes(lower, modes))
                )
            lower = modes
        disp_out_ref[pl.ds(out_rows - 1, depth, stride=out_rows), :] = jnp.zeros(plane, F32)
        shape = (rows_x, width)
        table_x = gauss(iota(shape, 0) - iota(shape, 1) % rows_x)
        weak = weak_ref[...]
        across_x = dot(table_x, weak, turned=True)
        shape = (width, width)
        table_x = gauss(iota(shape, 0) % rows_x - iota(shape, 1) % rows_x)
        smooth = dot(weak, table_x)
        weighted = jnp.zeros((1, width), F32)
        for source in range(slabs):
            base = sums_place(source) * sum_rows + 3
            weighted = weighted + jnp.sum(
                across_x[source * half : (source + 1) * half] * sums_ref[base : base + half],
                0,
                keepdims=True,
            )
        block_of = iota((half, width), 1) // rows_x
        pieces = []
        for layer in range(depth):
            rows = place(layer) * strip
            piece = smooth[rows : rows + half]
            for block_at in range(1, strip // half):
                rows = rows + half
                piece = jnp.where(block_of == block_at, smooth[rows : rows + half], piece)
            pieces.append(piece)
        for layer, piece in enumerate(filter_depth(pieces)):
            for part in range(parts):
                base = (part * slabs + layer) * numer_rows
                numer_ref[base : base + half] = piece
                numer_ref[base + half : base + numer_rows] = weighted

    disp_message, numer_message, count = call(
        energy_body,
        (flat(slabs * out_rows), flat(parts * slabs * numer_rows), flat(8)),
        all_sums,
        disp,
        cube,
        geometry,
        zeroth,
        first,
        second,
        third,
        scratch=[pltpu.VMEM((strip * depth, width), F32)],
        name="energy",
        flops=1 << 24,
    )
    numer_pieces = exchange(numer_message, ("load", "slab"))

    def trial_body(
        numer_ref, dens_ref, sums_ref, design_ref, count_ref, disp_ref, trial_ref, out_ref,
        plane_ref, filtered_ref,
    ):
        weighted = jnp.zeros((1, width), F32)
        for source in range(slabs):
            total = jnp.zeros((half, width), F32)
            for part in range(parts):
                base = (part * slabs + source) * numer_rows
                total = total + numer_ref[base : base + half]
                weighted = weighted + numer_ref[base + half : base + numer_rows]
            base = sums_place(source) * sum_rows + 3 + half
            filtered_ref[source * half : (source + 1) * half] = sums_ref[base : base + half]
            plane_ref[source * half : (source + 1) * half] = total
        mean = jnp.sum(weighted, 1, keepdims=True) / count_ref[0:1] + EPSILON
        packed = plane_ref[...].T
        numer = 0.0
        for block_at in range(strip // half):
            shape = (slabs * half, cols_y)
            row = iota(shape, 0)
            table = gauss(row // half * strip + block_at * half + row % half - iota(shape, 1))
            numer = numer + dot(packed[block_at * rows_x : (block_at + 1) * rows_x], table)
        mask = design_ref[0].astype(F32)
        dens = dens_ref[0]
        ratio = mask * (numer / filtered_ref[...]) / mean
        trial = jnp.clip(dens * jnp.sqrt(ratio), dens - MOVE_LIMIT, dens + MOVE_LIMIT)
        trial_ref[...] = trial
        out_ref[...] = disp_ref[...]
        volume = jnp.sum(mask * trial, 0, keepdims=True)
        for target in range(slabs):
            base = (target + 1) * out_rows - 1
            out_ref[base : base + 1] = volume

    trial, out_message = call(
        trial_body,
        (flat(rows_x), flat(slabs * out_rows)),
        numer_pieces,
        density,
        all_sums,
        design,
        count,
        disp_message,
        scratch=[pltpu.VMEM((rows_x, cols_y), F32)] * 2,
        name="trial",
    )
    out_pieces = exchange(out_message, "slab", ring)

    def final_body(pieces_ref, trial_ref, design_ref, count_ref, disp_ref, dens_ref, whole_ref):
        volume = jnp.zeros((1, width), F32)
        for source in range(slabs):
            base = (place(source) + 1) * out_rows
            volume = volume + pieces_ref[base - 1 : base]
            for comp in range(comps):
                base = place(source) * out_rows + comp * strip
                whole_ref[comp, source * strip : (source + 1) * strip] = pieces_ref[
                    base : base + strip
                ]
        volume = jnp.sum(volume, 1, keepdims=True)
        scale = VOLUME_TARGET / (volume / count_ref[0:1] + EPSILON)
        mask = design_ref[0].astype(F32)
        dens_ref[0] = mask * jnp.minimum(scale * trial_ref[...], 1.0)
        for comp in range(comps):
            turned = whole_ref[comp].T
            for load in range(loads):
                disp_ref[load, comp, 0] = turned[load * rows_x : (load + 1) * rows_x]

    return call(
        final_body,
        (
            jax.ShapeDtypeStruct(start_disp.shape, F32),
            jax.ShapeDtypeStruct(density.shape, F32),
        ),
        out_pieces,
        trial,
        design,
        count,
        scratch=[pltpu.VMEM((comps, cols_y, width), F32)],
        name="final",
    )


def solution(mesh):
    return jax.shard_map(
        shards,
        mesh=mesh,
        in_specs=(
            P("load", None, "slab", None, None),
            P("slab", None, None),
            P("slab", None, None),
            P("slab", None, None),
            P("load", None),
            P("load", None, None),
        ),
        out_specs=(P("load", None, "slab", None, None), P("slab", None, None)),
        check_vma=False,
    )
```

```python
import functools

import jax
import jax.numpy as jnp
import numpy as np
from jax import lax
from jax.experimental import pallas as pl
from jax.experimental.pallas import tpu as pltpu
from jax.sharding import PartitionSpec as P

RADIUS = 2
POISSON = 0.3
STIFF_VOID = 0.001
UPPER_FACTOR = 1.2
LOWER_RATIO = 0.1
MOVE_LIMIT = 0.2
VOLUME_TARGET = 0.5
EPSILON = 1e-06
F32 = jnp.float32

HALO_LOW = 4
HALO_HIGH = 5
HALO = HALO_LOW + HALO_HIGH
VMEM_LIMIT = 24 * 1024 * 1024


def hex_stiffness():
    lame_first = POISSON / ((1 + POISSON) * (1 - 2 * POISSON))
    lame_shear = 1 / (2 * (1 + POISSON))
    elastic = np.zeros((6, 6))
    elastic[:3, :3] = lame_first
    for axis_a in range(3):
        elastic[axis_a, axis_a] += 2 * lame_shear
        elastic[3 + axis_a, 3 + axis_a] = lame_shear
    shear_pairs = ((0, 1), (1, 2), (0, 2))
    gauss_point = 1 / np.sqrt(3)
    matrix = np.zeros((24, 24))
    for quad_index in range(8):
        quad_coords = [
            gauss_point * (2 * (quad_index >> 2 - axis_a & 1) - 1) for axis_a in range(3)
        ]
        shape_grads = np.zeros((8, 3))
        for corner in range(8):
            corner_signs = [2 * (corner >> 2 - axis_a & 1) - 1 for axis_a in range(3)]
            for axis_a in range(3):
                deriv_value = float(corner_signs[axis_a])
                for axis_b in range(3):
                    if axis_b != axis_a:
                        deriv_value *= (1 + corner_signs[axis_b] * quad_coords[axis_b]) / 2
                shape_grads[corner, axis_a] = deriv_value
        strain = np.zeros((6, 24))
        for corner in range(8):
            for axis_a in range(3):
                strain[axis_a, 3 * corner + axis_a] = shape_grads[corner, axis_a]
            for pair_index, shear_pair in enumerate(shear_pairs):
                strain[3 + pair_index, 3 * corner + shear_pair[0]] = shape_grads[
                    corner, shear_pair[1]
                ]
                strain[3 + pair_index, 3 * corner + shear_pair[1]] = shape_grads[
                    corner, shear_pair[0]
                ]
        matrix += strain.T @ elastic @ strain / 8
    return matrix.astype(np.float32)


def mode_stiffness():
    signs = np.zeros((8, 8))
    for mode in range(8):
        for corner in range(8):
            flips = bin(mode & ~corner & 7).count("1")
            signs[mode, corner] = -1.0 if flips & 1 else 1.0
    spread = np.kron(signs, np.eye(3))
    return spread @ hex_stiffness().astype(np.float64) @ spread.T / 64


MODES = mode_stiffness()
DIAG_ENTRY = float(hex_stiffness()[0, 0])


def entry(mode_a, comp_a, mode_b, comp_b):
    return float(MODES[3 * mode_a + comp_a, 3 * mode_b + comp_b])


NORMAL = ((4, 0), (2, 1), (1, 2))
SHEAR = (((2, 0), (4, 1)), ((1, 0), (4, 2)), ((1, 1), (2, 2)))
TWIST = ((3, 0), (5, 1), (6, 2))
BEND = (((3, 1), (5, 0)), ((3, 2), (6, 0)), ((5, 2), (6, 1)))
WARP = ((7, 0), (7, 1), (7, 2))
NORMAL_ON = entry(4, 0, 4, 0)
NORMAL_OFF = entry(4, 0, 2, 1)
SHEAR_ON = entry(2, 0, 4, 1)
TWIST_ON = entry(3, 0, 3, 0)
TWIST_OFF = entry(3, 0, 5, 1)
BEND_ON = entry(3, 1, 3, 1)
BEND_OFF = entry(3, 1, 5, 0)
WARP_ON = entry(7, 0, 7, 0)


def smoother_factors():
    sigma = (1 + LOWER_RATIO) / (1 - LOWER_RATIO)
    factor = 1 / sigma
    residual = np.array([1.0, 0.0, 0.0, 0.0])
    update = np.array([1.0, 0.0, 0.0, 0.0])
    total = np.zeros(4)
    for sweep in range(4):
        total = total + update
        if sweep < 3:
            residual = residual - np.concatenate([[0.0], update[:3]])
            factor_next = 1 / (2 * sigma - factor)
            update = factor_next * factor * update + 2 * factor_next * sigma * residual
            factor = factor_next
    return [float(value) for value in total]


def iota(shape, axis):
    return lax.broadcasted_iota(jnp.int32, shape, axis)


def gauss(offsets):
    return jnp.exp(-((offsets.astype(F32) / RADIUS) ** 2))


def gauss_table(count):
    return gauss(iota((count, count), 0) - iota((count, count), 1))


def shifts(shape, rows_x, first):
    inner = {}
    for axis, start, count in ((0, first, shape[0]), (1, 0, rows_x)):
        index = (iota(shape, axis) + start) % count
        inner[axis] = (index < count - 1, index > 0)

    def above(value, axis):
        moved = pltpu.roll(value, shape[axis] - 1, axis)
        return jnp.where(inner[axis][0], moved, 0.0)

    def below(value, axis):
        moved = pltpu.roll(value, 1, axis)
        return jnp.where(inner[axis][1], moved, 0.0)

    return above, below


def row_modes(values, above):
    modes = {}
    for comp, value in enumerate(values):
        beside = above(value, 1)
        for bit, part in ((0, value + beside), (2, beside - value)):
            ahead = above(part, 0)
            modes[bit, comp] = part + ahead
            modes[bit + 4, comp] = ahead - part
    return modes


def element_modes(low, high):
    modes = {}
    for (bits, comp), value in low.items():
        other = high[bits, comp]
        if bits:
            modes[bits, comp] = value + other
        modes[bits + 1, comp] = other - value
    return modes


def element_forces(modes, scale):
    forces = {}
    total = modes[NORMAL[0]] + modes[NORMAL[1]] + modes[NORMAL[2]]
    shared = (scale * NORMAL_OFF) * total
    own = scale * (NORMAL_ON - NORMAL_OFF)
    for key in NORMAL:
        forces[key] = shared + own * modes[key]
    shear = scale * SHEAR_ON
    for key_a, key_b in SHEAR:
        forces[key_a] = forces[key_b] = shear * (modes[key_a] + modes[key_b])
    total = modes[TWIST[0]] + modes[TWIST[1]] + modes[TWIST[2]]
    shared = (scale * TWIST_OFF) * total
    own = scale * (TWIST_ON - TWIST_OFF)
    for key in TWIST:
        forces[key] = shared + own * modes[key]
    bend_on = scale * BEND_ON
    bend_off = scale * BEND_OFF
    for key_a, key_b in BEND:
        forces[key_a] = bend_on * modes[key_a] + bend_off * modes[key_b]
        forces[key_b] = bend_on * modes[key_b] + bend_off * modes[key_a]
    warp = scale * WARP_ON
    for key in WARP:
        forces[key] = warp * modes[key]
    return forces


def element_energy(modes):
    total = modes[NORMAL[0]] + modes[NORMAL[1]] + modes[NORMAL[2]]
    squares = sum(modes[key] * modes[key] for key in NORMAL)
    energy = NORMAL_OFF * (total * total) + (NORMAL_ON - NORMAL_OFF) * squares
    shear = 0.0
    for key_a, key_b in SHEAR:
        both = modes[key_a] + modes[key_b]
        shear = shear + both * both
    energy = energy + SHEAR_ON * shear
    total = modes[TWIST[0]] + modes[TWIST[1]] + modes[TWIST[2]]
    squares = sum(modes[key] * modes[key] for key in TWIST)
    energy = energy + TWIST_OFF * (total * total) + (TWIST_ON - TWIST_OFF) * squares
    squares = sum(modes[key] * modes[key] for pair in BEND for key in pair)
    crossed = sum(modes[key_a] * modes[key_b] for key_a, key_b in BEND)
    energy = energy + BEND_ON * squares + (2 * BEND_OFF) * crossed
    squares = sum(modes[key] * modes[key] for key in WARP)
    return energy + WARP_ON * squares


ROW_KEYS = [(bits, comp) for comp in range(3) for bits in (0, 2, 4, 6)]


def split_forces(forces):
    here, there = {}, {}
    for bits, comp in ROW_KEYS:
        change = forces[bits + 1, comp]
        if bits:
            common = forces[bits, comp]
            here[bits, comp] = common - change
            there[bits, comp] = common + change
        else:
            here[bits, comp] = -change
            there[bits, comp] = change
    return here, there


def node_forces(modes, below):
    values = []
    for comp in range(3):
        parts = []
        for bit in (0, 2):
            common, change = modes[bit, comp], modes[bit + 4, comp]
            parts.append((common - change) + below(common + change, 0))
        values.append((parts[0] - parts[1]) + below(parts[0] + parts[1], 1))
    return values


def apply_rows(first, last, load_row, scale_row, emit, above, below, carry=None):
    def advance(index, low, pending):
        high = row_modes(load_row(index + 1), above)
        forces = element_forces(element_modes(low, high), scale_row(index))
        here, there = split_forces(forces)
        return high, {key: pending[key] + here[key] for key in ROW_KEYS}, there

    low = row_modes(load_row(first), above)
    zero = {key: jnp.zeros_like(low[key]) for key in ROW_KEYS}
    low, _, pending = advance(first, low, zero)

    for index in range(first + 1, last):
        low, modes, pending = advance(index, low, pending)
        carry = emit(index, node_forces(modes, below), carry)
    return carry


def dot(left, right, turned=False):
    dims = (((1,), (1 if turned else 0,)), ((), ()))

    def halves(value):
        high = value.astype(jnp.bfloat16)
        return high, (value - high.astype(F32)).astype(jnp.bfloat16)

    def product(a, b):
        return lax.dot_general(a, b, dims, preferred_element_type=F32)

    left_high, left_low = halves(left)
    right_high, right_low = halves(right)
    return product(left_high, right_high) + (
        product(left_high, right_low) + product(left_low, right_high)
    )


def swap_blocks(values, block):
    values = list(values)
    lanes = values[0].shape[1]
    place = iota(values[0].shape, 1) // block
    bit = 1
    while bit < len(values):
        lower = (place & bit) == 0
        for index in range(len(values)):
            if not index & bit:
                low, high = values[index], values[index + bit]
                values[index] = jnp.where(lower, low, pltpu.roll(high, bit * block, 1))
                values[index + bit] = jnp.where(
                    lower, pltpu.roll(low, lanes - bit * block, 1), high
                )
        bit *= 2
    return values


def filter_depth(layers):
    depth = len(layers)
    if depth <= 16:
        weights = [float(np.exp(-((step / RADIUS) ** 2))) for step in range(depth)]
        return [
            sum(weights[abs(to - source)] * layers[source] for source in range(depth))
            for to in range(depth)
        ]
    rows = layers[0].shape[0]
    shape = (depth * rows, depth * rows)
    to, source = iota(shape, 0), iota(shape, 1)
    table = jnp.where(to % rows == source % rows, gauss(to // rows - source // rows), 0.0)
    mixed = dot(table, jnp.concatenate(layers, 0))
    return [mixed[layer * rows : (layer + 1) * rows] for layer in range(depth)]


def call(body, outs, *args, scratch=(), name=None, flops=0, space=pltpu.VMEM, out_space=pltpu.VMEM):
    return pl.pallas_call(
        body,
        out_shape=outs,
        in_specs=[pl.BlockSpec(memory_space=space)] * len(args),
        out_specs=jax.tree.map(lambda _: pl.BlockSpec(memory_space=out_space), outs),
        scratch_shapes=list(scratch),
        compiler_params=pltpu.CompilerParams(vmem_limit_bytes=VMEM_LIMIT),
        cost_estimate=pl.CostEstimate(flops=flops, bytes_accessed=1 << 20, transcendentals=0),
        name=name,
    )(*args)


def exchange(message, axes, order=None):
    rows = message.shape[0]
    return lax.all_to_all(
        message.reshape(rows, 1, message.shape[1]),
        axes,
        split_axis=0,
        concat_axis=0,
        tiled=True,
        axis_index_groups=order and [order],
    ).reshape(message.shape)


def shards(start_disp, density, design, support, load_nodes, load_forces):
    slabs = lax.axis_size("slab")
    parts = lax.axis_size("load")
    loads, comps, layers, rows_x, cols_y = start_disp.shape
    points = load_nodes.shape[1]
    depth = slabs * layers
    strip = cols_y // slabs
    span = strip + HALO
    width = loads * rows_x
    half = rows_x // slabs
    plane = (depth, width)
    in_rows = (comps + 1) * span + 2 * half
    sum_rows = 3 + 2 * half
    numer_rows = half + 1
    out_rows = comps * strip + 1
    block = lambda count: jax.ShapeDtypeStruct((count, span) + plane, F32)
    flat = lambda rows: jax.ShapeDtypeStruct((rows, width), F32)
    smoother = smoother_factors()
    ring_start = slabs // 2 - 1
    ring = [(at + ring_start) % slabs for at in range(slabs)]
    place = lambda index: (index - ring_start) % slabs
    sums_start = slabs // 2 - 2
    sums_ring = [(at + sums_start) % slabs for at in range(slabs)]
    sums_place = lambda index: (index - sums_start) % slabs

    def pack_body(
        disp_ref, dens_ref, design_ref, support_ref, message_ref,
        stage_ref, dens_in, design_in, support_in, pad_ref, sems, out_ref, out_sems,
    ):
        sent = []
        copies = [
            pltpu.make_async_copy(dens_ref.at[0], dens_in, sems.at[0]),
            pltpu.make_async_copy(design_ref.at[0], design_in, sems.at[1]),
            pltpu.make_async_copy(support_ref.at[0], support_in, sems.at[2]),
        ]
        for load in range(loads):
            copies.append(
                pltpu.make_async_copy(
                    disp_ref.at[load, :, 0],
                    stage_ref.at[:, load * rows_x : (load + 1) * rows_x],
                    sems.at[3 + load],
                )
            )
        for copy in copies:
            copy.start()
        cube_side = iota((1, width), 1) < rows_x
        for field in range(comps + 1):
            fill = jnp.zeros((1, width), F32) if field < comps else jnp.where(cube_side, -1.0, 1.0)
            pad_ref[field, 0:HALO_LOW] = jnp.broadcast_to(fill, (HALO_LOW, width))
            pad_ref[field, HALO_LOW + cols_y : HALO + cols_y] = jnp.broadcast_to(
                fill, (HALO_HIGH, width)
            )
        for copy in copies[:3]:
            copy.wait()
        spread = dot(dot(gauss_table(rows_x), dens_in[...]), gauss_table(cols_y))
        solid = design_in[...].astype(F32) * dens_in[...]
        both = jnp.concatenate([solid * solid * solid, support_in[...].astype(F32)], 0)
        pad_ref[comps, HALO_LOW : HALO_LOW + cols_y] = both.T
        for copy in copies[3:]:
            copy.wait()
        for comp in range(comps):
            pad_ref[comp, HALO_LOW : HALO_LOW + cols_y] = stage_ref[comp].T
        for target in range(slabs):
            base = place(target) * in_rows
            for field in range(comps + 1):
                out_ref[base + field * span : base + (field + 1) * span] = pad_ref[
                    field, target * strip : target * strip + span
                ]
            rows = slice(target * half, (target + 1) * half)
            base = base + (comps + 1) * span
            out_ref[base : base + half] = spread[rows]
            out_ref[base + half : base + 2 * half] = design_in[rows].astype(F32)
            part = pl.ds(place(target) * in_rows, in_rows)
            sent.append(
                pltpu.make_async_copy(
                    out_ref.at[part], message_ref.at[part], out_sems.at[target]
                )
            )
            sent[-1].start()
        for copy in sent:
            copy.wait()

    message = call(
        pack_body,
        flat(slabs * in_rows),
        *(
            pltpu.with_memory_space_constraint(value, pltpu.HBM)
            for value in (start_disp, density, design, support)
        ),
        scratch=[
            pltpu.VMEM((comps, width, cols_y), F32),
            pltpu.VMEM((rows_x, cols_y), F32),
            pltpu.VMEM((rows_x, cols_y), jnp.int32),
            pltpu.VMEM((rows_x, cols_y), jnp.int32),
            pltpu.VMEM((comps + 1, cols_y + 2 * 8, width), F32),
            pltpu.SemaphoreType.DMA((3 + loads,)),
            pltpu.VMEM((slabs * in_rows, width), F32),
            pltpu.SemaphoreType.DMA((slabs,)),
        ],
        name="pack",
        space=pltpu.HBM,
        out_space=pltpu.HBM,
    )
    received = exchange(message, "slab", ring)

    cells = -(-span * depth // 16) * 16
    chunk = min(256, points)

    def loads_body(nodes_ref, forces_ref, out_ref):
        first = lax.axis_index("slab") * strip - HALO_LOW
        out_ref[...] = jnp.zeros_like(out_ref)
        for load in range(loads):
            for start in range(0, points, chunk):
                part = slice(start, start + chunk)
                node = nodes_ref[load : load + 1, part]
                row = node % cols_y - first
                lane = load * rows_x + (node // cols_y) % rows_x
                layer = (node // (cols_y * rows_x) + depth - ring_start) % depth
                cell = jnp.where((row >= 0) & (row < span), row * depth + layer, -1)
                hit = iota((cells, chunk), 0) == cell
                spot = (iota((width, chunk), 0) == lane).astype(F32).astype(jnp.bfloat16)
                for comp in range(comps):
                    rest = forces_ref[load, comp : comp + 1, part]
                    for piece in range(3):
                        rounded = rest.astype(jnp.bfloat16).astype(F32)
                        rest = rest - rounded
                        picked = jnp.where(hit, rounded, 0.0).astype(jnp.bfloat16)
                        out_ref[comp] += lax.dot_general(
                            picked, spot, (((1,), (1,)), ((), ())), preferred_element_type=F32
                        )

    right_side = call(
        loads_body,
        jax.ShapeDtypeStruct((comps, cells, width), F32),
        load_nodes,
        load_forces,
        name="point_loads",
        flops=1 << 28,
    )

    def own_row(row):
        return HALO_LOW <= row < HALO_LOW + strip

    last_row = HALO_LOW + strip
    near_nodes = range(HALO_LOW - 1, last_row + 2)
    near_zero = range(HALO_LOW, last_row + 1)

    def strip_rows(disp, geo, inverse, zero, in_ref, rhs_ref):
        above, below = shifts(plane, rows_x, ring_start)
        cube_side = iota(plane, 1) < rows_x
        scale_row = lambda row: geo(row)[0, row]

        def read(rows, cube_ref=None):
            for row in rows:
                pick = lambda field: in_ref[pl.ds(field * span + row, depth, stride=in_rows), :]
                for comp in range(comps):
                    disp(row)[comp, row] = pick(comp)
                both = pick(comps)
                other = pltpu.roll(both, rows_x, 1)
                cube = jnp.where(cube_side, both, other)
                if cube_ref is not None:
                    cube_ref[0, row] = cube
                geo(row)[0, row] = jnp.where(
                    cube < 0.0, 0.0, STIFF_VOID + (1.0 - STIFF_VOID) * cube
                )
                geo(row)[1, row] = 1.0 - jnp.where(cube_side, other, both)

        def invert(rows):
            for row in rows:
                beside = geo(row)[0, row] + geo(row - 1)[0, row - 1]
                beside = beside + below(beside, 0)
                beside = beside + below(beside, 1)
                free = geo(row)[1, row]
                inverse(row)[0, row] = 1.0 / (free * DIAG_ENTRY * beside + (1.0 - free))

        def masked(source):
            def load_row(row):
                free = geo(row)[1, row]
                return [free * source(row)[comp, row] for comp in range(comps)]

            return load_row

        def residual(first, last):
            def emit(row, forces, carried):
                free, inverted = geo(row)[1, row], inverse(row)[0, row]
                total = jnp.zeros(plane, F32)
                for comp, force in enumerate(forces):
                    load_row = rhs_ref[comp, row * depth : (row + 1) * depth, :]
                    rest = free * (load_row - force) - (1.0 - free) * disp(row)[comp, row]
                    value = rest * inverted
                    zero(row)[comp, row] = value
                    total = total + value * rest
                return carried + total if own_row(row) else carried

            return apply_rows(
                first, last, masked(disp), scale_row, emit, above, below, jnp.zeros(plane, F32)
            )

        def curvature():
            total, lower = jnp.zeros(plane, F32), None
            for row in near_zero:
                modes = row_modes(masked(zero)(row), above)
                if lower is not None:
                    total = total + scale_row(row - 1) * element_energy(
                        element_modes(lower, modes)
                    )
                if own_row(row):
                    fixed = 1.0 - geo(row)[1, row]
                    values = [zero(row)[comp, row] for comp in range(comps)]
                    total = total + fixed * sum(value * value for value in values)
                lower = modes
            return total

        def power(source, target, first, last):
            def emit(row, forces, carried):
                free, inverted = geo(row)[1, row], inverse(row)[0, row]
                for comp, force in enumerate(forces):
                    applied = free * force + (1.0 - free) * source(row)[comp, row]
                    target(row)[comp, row] = applied * inverted

            apply_rows(first, last, masked(source), scale_row, emit, above, below)

        return read, invert, residual, curvature, power

    def residual_body(in_ref, rhs_ref, disp_ref, cube_ref, geo_ref, inv_ref, zero_ref, sum_ref):
        def gather(offset):
            offset = offset + (comps + 1) * span
            return [
                in_ref[place(layer) * in_rows + offset : place(layer) * in_rows + offset + half]
                for layer in range(depth)
            ]

        mask = jnp.concatenate(gather(half), 0)
        filtered = jnp.concatenate(filter_depth(gather(0)), 0)
        share = dot(mask / filtered, gauss_table(cols_y))
        share = filter_depth([share[layer * half : (layer + 1) * half] for layer in range(depth)])
        share = swap_blocks([share[layer] for layer in ring], strip)
        here = lambda ref: lambda row: ref
        read, invert, residual, curvature, _ = strip_rows(
            here(disp_ref), here(geo_ref), here(inv_ref), here(zero_ref), in_ref, rhs_ref
        )
        read(near_nodes, cube_ref)
        invert(near_zero)
        weight = residual(near_zero[0] - 1, near_zero[-1] + 1)
        curve = curvature()
        down = lambda value: jnp.sum(value, 0, keepdims=True)
        sums = [down(curve), down(weight), down(mask)]
        for target in range(slabs):
            base = sums_place(target) * sum_rows
            for index, value in enumerate(sums):
                sum_ref[base + index : base + index + 1] = value
            sum_ref[base + 3 : base + 3 + half] = share[target]
            sum_ref[base + 3 + half : base + sum_rows] = filtered[
                target * half : (target + 1) * half
            ]

    disp, cube, geometry, inverses, zeroth, sums = call(
        residual_body,
        (
            block(comps),
            block(1),
            block(2),
            block(1),
            block(comps),
            flat(slabs * sum_rows),
        ),
        received,
        right_side,
        name="residual",
        flops=1 << 26,
    )
    all_sums = exchange(sums, "slab", sums_ring)

    def powers_body(
        in_ref, rhs_ref, disp_ref, geo_ref, inv_ref, zero_ref, one_ref, two_ref, three_ref,
        far_disp, far_geo, far_inv, far_zero,
    ):
        choose = lambda near, far, rows: lambda row: near if row in rows else far
        zero = choose(zero_ref, far_zero, near_zero)
        read, invert, residual, _, power = strip_rows(
            choose(disp_ref, far_disp, near_nodes),
            choose(geo_ref, far_geo, near_nodes),
            choose(inv_ref, far_inv, near_zero),
            zero,
            in_ref,
            rhs_ref,
        )
        read([row for row in range(span) if row not in near_nodes])
        invert([row for row in range(1, span - 1) if row not in near_zero])
        residual(0, near_zero[0])
        residual(near_zero[-1], span - 1)
        power(zero, lambda row: one_ref, 1, span - 2)
        power(lambda row: one_ref, lambda row: two_ref, 2, span - 3)
        power(lambda row: two_ref, lambda row: three_ref, 3, span - 4)

    first, second, third = call(
        powers_body,
        (block(comps), block(comps), block(comps)),
        received,
        right_side,
        disp,
        geometry,
        inverses,
        zeroth,
        scratch=[pltpu.VMEM((count, span) + plane, F32) for count in (comps, 2, 1, comps)],
        name="powers",
        flops=1 << 26,
    )

    def energy_body(
        sums_ref, disp_ref, cube_ref, geo_ref, zero_ref, one_ref, two_ref, three_ref,
        disp_out_ref, numer_ref, count_ref, weak_ref,
    ):
        above, below = shifts(plane, rows_x, ring_start)
        gather = lambda index: sum(
            sums_ref[layer * sum_rows + index : layer * sum_rows + index + 1]
            for layer in range(slabs)
        )
        curve, weight, count = gather(0), gather(1), gather(2)
        across = lambda value: jnp.sum(value, 1, keepdims=True)
        count_ref[...] = jnp.broadcast_to(across(count), (8, width))
        owner = iota((1, width), 1) // rows_x
        inverse = jnp.zeros((1, width), F32)
        for load in range(loads):
            mine = owner == load
            upper = UPPER_FACTOR * (
                across(jnp.where(mine, curve, 0.0)) / across(jnp.where(mine, weight, 0.0))
            )
            inverse = jnp.where(mine, 1.0 / (0.5 * (upper + LOWER_RATIO * upper)), inverse)
        inverse = jnp.broadcast_to(inverse, plane)
        lower = None
        for row in range(HALO_LOW, HALO_LOW + strip + 1):
            free = geo_ref[1, row]
            values = []
            for comp in range(comps):
                value = smoother[3] * three_ref[comp, row]
                value = smoother[2] * two_ref[comp, row] + inverse * value
                value = smoother[1] * one_ref[comp, row] + inverse * value
                value = smoother[0] * zero_ref[comp, row] + inverse * value
                value = disp_ref[comp, row] + inverse * value
                if row < HALO_LOW + strip:
                    start = comp * strip + row - HALO_LOW
                    disp_out_ref[pl.ds(start, depth, stride=out_rows), :] = value
                values.append(free * value)
            modes = row_modes(values, above)
            if lower is not None:
                weak_ref[pl.ds(row - 1 - HALO_LOW, depth, stride=strip), :] = (
                    (3.0 * (1.0 - STIFF_VOID))
                    * cube_ref[0, row - 1]
                    * element_energy(element_modes(lower, modes))
                )
            lower = modes
        disp_out_ref[pl.ds(out_rows - 1, depth, stride=out_rows), :] = jnp.zeros(plane, F32)
        shape = (rows_x, width)
        table_x = gauss(iota(shape, 0) - iota(shape, 1) % rows_x)
        weak = weak_ref[...]
        across_x = dot(table_x, weak, turned=True)
        shape = (width, width)
        table_x = gauss(iota(shape, 0) % rows_x - iota(shape, 1) % rows_x)
        smooth = dot(weak, table_x)
        weighted = jnp.zeros((1, width), F32)
        for source in range(slabs):
            base = sums_place(source) * sum_rows + 3
            weighted = weighted + jnp.sum(
                across_x[source * half : (source + 1) * half] * sums_ref[base : base + half],
                0,
                keepdims=True,
            )
        block_of = iota((half, width), 1) // rows_x
        pieces = []
        for layer in range(depth):
            rows = place(layer) * strip
            piece = smooth[rows : rows + half]
            for block_at in range(1, strip // half):
                rows = rows + half
                piece = jnp.where(block_of == block_at, smooth[rows : rows + half], piece)
            pieces.append(piece)
        for layer, piece in enumerate(filter_depth(pieces)):
            for part in range(parts):
                base = (part * slabs + layer) * numer_rows
                numer_ref[base : base + half] = piece
                numer_ref[base + half : base + numer_rows] = weighted

    disp_message, numer_message, count = call(
        energy_body,
        (flat(slabs * out_rows), flat(parts * slabs * numer_rows), flat(8)),
        all_sums,
        disp,
        cube,
        geometry,
        zeroth,
        first,
        second,
        third,
        scratch=[pltpu.VMEM((strip * depth, width), F32)],
        name="energy",
        flops=1 << 24,
    )
    numer_pieces = exchange(numer_message, ("load", "slab"))

    def trial_body(
        numer_ref, dens_ref, sums_ref, design_ref, count_ref, disp_ref, trial_ref, out_ref,
        plane_ref, filtered_ref,
    ):
        weighted = jnp.zeros((1, width), F32)
        for source in range(slabs):
            total = jnp.zeros((half, width), F32)
            for part in range(parts):
                base = (part * slabs + source) * numer_rows
                total = total + numer_ref[base : base + half]
                weighted = weighted + numer_ref[base + half : base + numer_rows]
            base = sums_place(source) * sum_rows + 3 + half
            filtered_ref[source * half : (source + 1) * half] = sums_ref[base : base + half]
            plane_ref[source * half : (source + 1) * half] = total
        mean = jnp.sum(weighted, 1, keepdims=True) / count_ref[0:1] + EPSILON
        packed = plane_ref[...].T
        numer = 0.0
        for block_at in range(strip // half):
            shape = (slabs * half, cols_y)
            row = iota(shape, 0)
            table = gauss(row // half * strip + block_at * half + row % half - iota(shape, 1))
            numer = numer + dot(packed[block_at * rows_x : (block_at + 1) * rows_x], table)
        mask = design_ref[0].astype(F32)
        dens = dens_ref[0]
        ratio = mask * (numer / filtered_ref[...]) / mean
        trial = jnp.clip(dens * jnp.sqrt(ratio), dens - MOVE_LIMIT, dens + MOVE_LIMIT)
        trial_ref[...] = trial
        out_ref[...] = disp_ref[...]
        volume = jnp.sum(mask * trial, 0, keepdims=True)
        for target in range(slabs):
            base = (target + 1) * out_rows - 1
            out_ref[base : base + 1] = volume

    trial, out_message = call(
        trial_body,
        (flat(rows_x), flat(slabs * out_rows)),
        numer_pieces,
        density,
        all_sums,
        design,
        count,
        disp_message,
        scratch=[pltpu.VMEM((rows_x, cols_y), F32)] * 2,
        name="trial",
    )
    out_pieces = exchange(out_message, "slab", ring)

    def final_body(pieces_ref, trial_ref, design_ref, count_ref, disp_ref, dens_ref, whole_ref):
        volume = jnp.zeros((1, width), F32)
        for source in range(slabs):
            base = (place(source) + 1) * out_rows
            volume = volume + pieces_ref[base - 1 : base]
            for comp in range(comps):
                base = place(source) * out_rows + comp * strip
                whole_ref[comp, source * strip : (source + 1) * strip] = pieces_ref[
                    base : base + strip
                ]
        volume = jnp.sum(volume, 1, keepdims=True)
        scale = VOLUME_TARGET / (volume / count_ref[0:1] + EPSILON)
        mask = design_ref[0].astype(F32)
        dens_ref[0] = mask * jnp.minimum(scale * trial_ref[...], 1.0)
        for comp in range(comps):
            turned = whole_ref[comp].T
            for load in range(loads):
                disp_ref[load, comp, 0] = turned[load * rows_x : (load + 1) * rows_x]

    return call(
        final_body,
        (
            jax.ShapeDtypeStruct(start_disp.shape, F32),
            jax.ShapeDtypeStruct(density.shape, F32),
        ),
        out_pieces,
        trial,
        design,
        count,
        scratch=[pltpu.VMEM((comps, cols_y, width), F32)],
        name="final",
    )


def solution(mesh):
    return jax.shard_map(
        shards,
        mesh=mesh,
        in_specs=(
            P("load", None, "slab", None, None),
            P("slab", None, None),
            P("slab", None, None),
            P("slab", None, None),
            P("load", None),
            P("load", None, None),
        ),
        out_specs=(P("load", None, "slab", None, None), P("slab", None, None)),
        check_vma=False,
    )
```
